32 devices in a mesh: dp: 4 (over y, x), expert: 8 (over z, core).
Axes of the slice: x: 2, y: 2, z: 4, core: 2. Of those that a mesh axis runs over, the one named last changes fastest.
Arguments:
- tokens: bfloat16 [4096, 1280], P(('dp', 'expert')), may hold values from -6 to 6
- cotangent: bfloat16 [4096, 1280], P(('dp', 'expert')), may hold values from -6 to 6
- routes: int32 [4096, 6], P(('dp', 'expert')), may hold values from 0 to 14, all different within a row; in each aligned block of 128 rows (0 to 127, 128 to 255, ...) at most 64 rows name the same one
- expert_at: int32 [16], replicated, may hold values from 0 to 15, each once
- norm1_gain: float32 [1280], replicated, may hold values from 0.5 to 1.5
- w_query: bfloat16 [1280, 1280], replicated, may hold values from -0.15625 to 0.15625
- w_key: bfloat16 [1280, 1280], replicated, may hold values from -0.15625 to 0.15625
- w_value: bfloat16 [1280, 1280], replicated, may hold values from -0.15625 to 0.15625
- w_out: bfloat16 [1280, 1280], replicated, may hold values from -1 to 1
- norm2_gain: float32 [1280], replicated, may hold values from 0.5 to 1.5
- w_router: bfloat16 [1280, 15], replicated, may hold values from -0.078125 to 0.078125
- shared_gate: bfloat16 [1280, 896], replicated, may hold values from -0.15625 to 0.15625
- shared_up: bfloat16 [1280, 896], replicated, may hold values from -0.15625 to 0.15625
- shared_down: bfloat16 [896, 1280], replicated, may hold values from -0.1875 to 0.1875
- routed_gate: bfloat16 [16, 1280, 896], P('expert'), may hold values from -0.15625 to 0.15625
- routed_up: bfloat16 [16, 1280, 896], P('expert'), may hold values from -0.15625 to 0.15625
- routed_down: bfloat16 [16, 896, 1280], P('expert'), may hold values from -0.875 to 0.875
Outputs:
- output: bfloat16 [4096, 1280], P(('dp', 'expert'))
- grad_tokens: float32 [4096, 1280], P(('dp', 'expert'))
- grad_norm1: float32 [1280], P(('dp', 'expert'))
- grad_query: float32 [1280, 1280], P(('dp', 'expert'))
- grad_key: float32 [1280, 1280], P(('dp', 'expert'))
- grad_value: float32 [1280, 1280], P(('dp', 'expert'))
- grad_out: float32 [1280, 1280], P(('dp', 'expert'))
- grad_norm2: float32 [1280], P(('dp', 'expert'))
- grad_router: float32 [1280, 15], P(('dp', 'expert'))
- grad_shared_gate: float32 [1280, 896], P(('dp', 'expert'))
- grad_shared_up: float32 [1280, 896], P(('dp', 'expert'))
- grad_shared_down: float32 [896, 1280], P(('dp', 'expert'))
- grad_routed_gate: float32 [16, 1280, 896], P('expert', 'dp')
- grad_routed_up: float32 [16, 1280, 896], P('expert', 'dp')
- grad_routed_down: float32 [16, 896, 1280], P('expert', 'dp')
The draws below stay inside these ranges and needn't reach their ends.
Inputs may be any that keep to these rules, and one draw needn't show every extreme that they name: `routes`: each token names 6 different experts. Among the 128 tokens of one device no expert is named more than 64 times, a bound that some block reaches. `expert_at`: each slot holds one expert; every value appears once, and the slot holding the value 15 is empty.
All inputs are finite; a program needn't handle non-finite values.
Results may differ from the reference program's by a relative error of at most 0.015.
Values may be sent and summed in bfloat16 or wider, within the bound.
No kernel may reach another device: no remote copies, remote signals or barrier semaphores. Data moves between devices by JAX's collectives and lax.ppermute only.
A program may use at most 320 MiB of HBM per device.

```python
import math
import jax
import jax.numpy as jnp
import numpy as np
from jax import lax

D = 1280
HEADS = 10
HEAD_DIM = 128
FF = 896
TOP = 6
TOK_DEV = 128
SLOTS = 16
EXPERTS = 15
CAP = 64
TOKENS = 4096


def levels(rng, shape, cuts, smallest, largest):
    level = 1.0
    for dim, parts in cuts:
        steps = jax.random.uniform(jax.random.fold_in(jax.random.fold_in(rng, 6), dim), (parts,), jnp.float32, smallest / len(cuts), largest / len(cuts))
        level = level * jnp.repeat(jnp.exp(steps), shape[dim] // parts).reshape((-1,) + (1,) * (len(shape) - 1 - dim))
    return level


def shared_out(own_key, own, number, rows, amount, top, reach, slope):
    ranking = jax.random.permutation(own_key, amount)
    crowded, ordinary = portions_of(amount, rows * top, reach, slope, True), portions_of(amount, rows * top, reach, slope, False)
    places = jnp.arange(amount)

    def named(lengths, offset_by):
        used = int((lengths > 0).sum())
        fixed = max(1, used // 4)
        shifted = fixed + (places - fixed + offset_by * (used - fixed)) % max(1, amount - fixed)
        return jnp.zeros((amount,), jnp.int32).at[ranking[jnp.where(places < fixed, places, shifted)]].set(jnp.asarray(lengths, jnp.int32))

    lengths = jnp.where(number % 4 == 0, named(crowded, number // 4), named(ordinary, number - number // 4 - 1))
    mixed = jax.random.permutation(jax.random.fold_in(own, 3), amount)
    donor, sink = mixed[0:amount // 2 * 2:2], mixed[1:amount // 2 * 2:2]
    room = jnp.minimum(lengths[donor] - 1, reach - lengths[sink]) // 2
    room = jnp.where((donor == ranking[0]) | (sink == ranking[0]) | (lengths[sink] == 0), 0, jnp.maximum(room, 0))
    shifted = jax.random.randint(jax.random.fold_in(own, 4), (amount // 2,), 0, 1 << 20) % (room + 1)
    lengths = lengths.at[donor].add(-shifted).at[sink].add(shifted)
    members = jnp.searchsorted(jnp.cumsum(lengths), jnp.arange(rows * top), side="right").astype(jnp.int32)
    listing = members.reshape(top, rows).T
    listing = listing[jax.random.permutation(jax.random.fold_in(own, 1), rows)]
    offset_by = jax.random.randint(jax.random.fold_in(own, 2), (rows, 1), 0, top)
    return jnp.take_along_axis(listing, (jnp.arange(top)[None, :] + offset_by) % top, axis=1)


def portions_of(amount, total, bound, skew, full):
    weights = [(1 << 20) // math.isqrt(rank ** skew) + 1 for rank in range(1, amount + 1)]
    largest = bound if full else min(bound, max(-(-total // amount), total * weights[0] // sum(weights)))
    least = 1 if total - largest >= amount - 1 else 0
    holding, spare = [largest] + [least] * (amount - 1), total - largest - least * (amount - 1)
    while spare > 0:
        movable = [i for i in range(1, amount) if holding[i] < largest] or [i for i in range(1, amount) if holding[i] < bound]
        pool, remaining = sum([weights[i] for i in movable]), spare
        for i in movable:
            addition = min(bound - holding[i], max(1, remaining * weights[i] // pool), spare)
            holding[i] = holding[i] + addition
            spare = spare - addition
    return np.array(holding)


def noise(stream_key, extent, deviation, limit, cuts=(), held_as=jnp.bfloat16):
    loudness = levels(stream_key, extent, cuts, -0.22, 0.18) if cuts else 1.0
    drawn = jax.random.normal(stream_key, extent, jnp.float32) * deviation * loudness
    return jnp.minimum(jnp.maximum(drawn, -limit), limit).astype(held_as)


def setup_inputs(seed: int = 0) -> dict:
    splits = jax.random.split(jax.random.key(seed), 18)
    tokens = noise(splits[0], (TOKENS, D), 1.0, 6.0, ((0, 32),))
    cotangent = noise(splits[1], (TOKENS, D), 1.0, 6.0, ((0, 32),))
    routes_keys = jax.random.split(jax.random.fold_in(splits[2], 1), TOKENS // TOK_DEV)
    routes_turns = jax.random.permutation(jax.random.fold_in(splits[2], 3), TOKENS // TOK_DEV)
    routes = jax.vmap(lambda own, number: shared_out(jax.random.fold_in(splits[2], 2), own, number, TOK_DEV, EXPERTS, TOP, CAP, 1))(routes_keys, routes_turns).reshape((TOKENS, TOP))
    expert_at = jax.random.permutation(splits[3], SLOTS).astype(jnp.int32)
    norm1_gain = jnp.clip(1.0 + 0.1 * jax.random.normal(splits[4], (D,), jnp.float32), 0.5, 1.5)
    w_query = noise(splits[5], (D, D), D ** -0.5, 0.15625)
    w_key = noise(splits[6], (D, D), D ** -0.5, 0.15625)
    w_value = noise(splits[7], (D, D), D ** -0.5, 0.15625)
    w_out = noise(splits[8], (D, D), (D // 32) ** -0.5, 1.0)
    norm2_gain = jnp.clip(1.0 + 0.1 * jax.random.normal(splits[9], (D,), jnp.float32), 0.5, 1.5)
    w_router = noise(splits[10], (D, EXPERTS), (4 * D) ** -0.5, 0.078125)
    shared_gate = noise(splits[11], (D, FF), D ** -0.5, 0.15625)
    shared_up = noise(splits[12], (D, FF), D ** -0.5, 0.15625)
    shared_down = noise(splits[13], (FF, D), FF ** -0.5, 0.1875)
    routed_gate = noise(splits[14], (SLOTS, D, FF), D ** -0.5, 0.15625, ((0, 8),))
    routed_up = noise(splits[15], (SLOTS, D, FF), D ** -0.5, 0.15625, ((0, 8),))
    routed_down = noise(splits[16], (SLOTS, FF, D), (max(1, 13 * FF // (EXPERTS * EXPERTS))) ** -0.5, 0.875, ((0, 8),))
    return {"tokens": tokens, "cotangent": cotangent, "routes": routes, "expert_at": expert_at, "norm1_gain": norm1_gain, "w_query": w_query, "w_key": w_key, "w_value": w_value, "w_out": w_out, "norm2_gain": norm2_gain, "w_router": w_router, "shared_gate": shared_gate, "shared_up": shared_up, "shared_down": shared_down, "routed_gate": routed_gate, "routed_up": routed_up, "routed_down": routed_down}


@jax.custom_vjp
def low(v):
    return lax.optimization_barrier(v.astype(jnp.bfloat16)).astype(jnp.float32)

@jax.custom_vjp
def low_back(v):
    return v

def low_keep(v):
    return (low(v), None)

def low_pass(kept, grad):
    return (grad,)

def back_keep(v):
    return (v, None)

def back_low(kept, grad):
    return (low(grad),)
low.defvjp(low_keep, low_pass)
low_back.defvjp(back_keep, back_low)
epsilon = 1e-06
highest = lax.Precision.HIGHEST

def swish_of(operand):
    return operand * jax.nn.sigmoid(operand)

def rotary_tables(length, half_width):
    position = jnp.arange(length, dtype=jnp.float32)[:, None]
    frequencies = jnp.exp(jnp.arange(half_width, dtype=jnp.float32) * (-math.log(10000.0) / half_width))
    angles = position * frequencies[None, :]
    return (jnp.cos(angles)[:, None, :], jnp.sin(angles)[:, None, :])

def rotate(operand, cosine, sine_table, direction):
    half_width = operand.shape[-1] // 2
    first_half = operand[..., :half_width]
    second = operand[..., half_width:]
    return jnp.concatenate([first_half * cosine - direction * second * sine_table, second * cosine + direction * first_half * sine_table], -1)

def softmax_rows(logits):
    row_max = lax.optimization_barrier(jnp.max(logits, -1, keepdims=True))
    expo_terms = jnp.exp(logits - row_max)
    return expo_terms / lax.optimization_barrier(jnp.sum(expo_terms, -1, keepdims=True))

def layer_rows(params, tokens_in, route_ids, slot_of):
    gain_first, w_query, w_key, w_value, w_out, gain_second, w_router, shared_gate, shared_up, shared_down, routed_gate, routed_up, routed_down = params
    length = tokens_in.shape[0]
    scale_first = lax.rsqrt(lax.optimization_barrier(jnp.mean(tokens_in * tokens_in, -1, keepdims=True)) + epsilon)
    normed_first = low(tokens_in * scale_first * gain_first)
    cosine, sine_table = rotary_tables(length, HEAD_DIM // 2)

    def heads_of(weight):
        return low_back(jnp.dot(normed_first, weight, precision=highest)).reshape(length, HEADS, HEAD_DIM)
    queries = low(rotate(heads_of(w_query), cosine, sine_table, 1.0))
    key_heads = low(rotate(heads_of(w_key), cosine, sine_table, 1.0))
    value_heads = low(heads_of(w_value))
    raw_scores = low_back(jnp.einsum('qhd,khd->hqk', queries, key_heads, precision=highest) * (1.0 / math.sqrt(HEAD_DIM)))
    causal = jnp.arange(length)[:, None] >= jnp.arange(length)[None, :]
    att_probs = low(softmax_rows(jnp.where(causal[None], raw_scores, -1e+30)))
    attended = low(low_back(jnp.einsum('hqk,khd->qhd', att_probs, value_heads, precision=highest))).reshape(length, D)
    residual = tokens_in + low_back(jnp.dot(attended, w_out, precision=highest))
    scale_second = lax.rsqrt(lax.optimization_barrier(jnp.mean(residual * residual, -1, keepdims=True)) + epsilon)
    normed_second = low(residual * scale_second * gain_second)
    shared_g = low_back(jnp.dot(normed_second, shared_gate, precision=highest))
    shared_u = low_back(jnp.dot(normed_second, shared_up, precision=highest))
    shared_hidden = low(swish_of(shared_g) * shared_u)
    shared_result = low_back(jnp.dot(shared_hidden, shared_down, precision=highest))
    router_probs = softmax_rows(low_back(jnp.dot(normed_second, w_router, precision=highest)))
    expert_ids = jnp.arange(EXPERTS, dtype=jnp.int32)
    chosen = (route_ids[:, :, None] == expert_ids[None, None, :]).astype(jnp.float32)
    gate_values = lax.optimization_barrier(jnp.sum(chosen * router_probs[:, None, :], -1))
    flat_ids = route_ids.reshape(-1)
    onehot = (flat_ids[:, None] == expert_ids[None, :]).astype(jnp.int32)
    position = lax.optimization_barrier(jnp.sum(jnp.cumsum(onehot, 0) * onehot, 1)) - 1
    target_row = (lax.optimization_barrier(jnp.sum(onehot * slot_of[None, :], 1)) * CAP + position).astype(jnp.int32)
    token_rows = low_back(jnp.broadcast_to(normed_second[:, None, :], (length, TOP, D)).reshape(length * TOP, D))
    buffer = jnp.zeros((SLOTS * CAP, D), jnp.float32).at[target_row].set(token_rows).reshape(SLOTS, CAP, D)
    expert_g = low_back(jnp.einsum('scd,sdf->scf', buffer, routed_gate, precision=highest))
    expert_u = low_back(jnp.einsum('scd,sdf->scf', buffer, routed_up, precision=highest))
    expert_hidden = low(swish_of(expert_g) * expert_u)
    expert_result = low(low_back(jnp.einsum('scf,sfd->scd', expert_hidden, routed_down, precision=highest)))
    returned = expert_result.reshape(SLOTS * CAP, D)[target_row].reshape(length, TOP, D)
    return residual + shared_result + lax.optimization_barrier(jnp.sum(gate_values[:, :, None] * returned, 1))

def reference(tokens, cotangent, routes, expert_at, norm1_gain, w_query, w_key, w_value, w_out, norm2_gain, w_router, shared_gate, shared_up, shared_down, routed_gate, routed_up, routed_down):
    groups = TOKENS // TOK_DEV
    params = tuple((weight.astype(jnp.float32) for weight in (norm1_gain, w_query, w_key, w_value, w_out, norm2_gain, w_router, shared_gate, shared_up, shared_down, routed_gate, routed_up, routed_down)))
    expert_ids = jnp.arange(EXPERTS, dtype=jnp.int32)
    slot_of = lax.optimization_barrier(jnp.sum(jnp.where(expert_at[None, :] == expert_ids[:, None], jnp.arange(SLOTS, dtype=jnp.int32)[None, :], 0), 1)).astype(jnp.int32)
    token_groups = tokens.astype(jnp.float32).reshape(groups, TOK_DEV, D)
    route_groups = routes.reshape(groups, TOK_DEV, TOP)

    def forward(weights, inputs):

        def one_group(group_item):
            return layer_rows(weights, group_item[0], group_item[1], slot_of)
        return lax.map(jax.checkpoint(one_group), (inputs, route_groups))
    result, pullback = jax.vjp(forward, params, token_groups)
    grad_params, grad_inputs = pullback(cotangent.astype(jnp.float32).reshape(groups, TOK_DEV, D))
    return (result.reshape(TOKENS, D).astype(jnp.bfloat16), grad_inputs.reshape(TOKENS, D), grad_params[0], grad_params[1], grad_params[2], grad_params[3], grad_params[4], grad_params[5], grad_params[6], grad_params[7], grad_params[8], grad_params[9], grad_params[10], grad_params[11], grad_params[12])
```

```python
import math

import jax
import jax.numpy as jnp
from jax import lax
from jax.sharding import PartitionSpec as P

HEADS = 10
HEAD_DIM = 128
TOP = 6
LANES = 128
epsilon = 1e-06
BF = jnp.bfloat16
F32 = jnp.float32


def rotary_tables(length, half_width):
    position = jnp.arange(length, dtype=jnp.float32)[:, None]
    frequencies = jnp.exp(
        jnp.arange(half_width, dtype=jnp.float32) * (-math.log(10000.0) / half_width)
    )
    angles = position * frequencies[None, :]
    return (jnp.cos(angles)[:, None, :], jnp.sin(angles)[:, None, :])


def rotate(operand, cosine, sine_table, direction):
    half_width = operand.shape[-1] // 2
    first_half = operand[..., :half_width]
    second = operand[..., half_width:]
    return jnp.concatenate(
        [
            first_half * cosine - direction * second * sine_table,
            second * cosine + direction * first_half * sine_table,
        ],
        -1,
    )


def product(left, right):
    return jnp.dot(left, right, preferred_element_type=jnp.float32)


def product_right(left, right):
    return lax.dot_general(
        left, right, (((1,), (1,)), ((), ())), preferred_element_type=jnp.float32
    )


def norm_backward(grad_normed, unit_rows, row_scale, gain):
    scaled_grad = grad_normed * gain
    grad_gain = jnp.sum(grad_normed * unit_rows, 0)
    grad_rows = row_scale * (
        scaled_grad - unit_rows * jnp.mean(scaled_grad * unit_rows, -1, keepdims=True)
    )
    return (grad_rows, grad_gain)


def partner(v, axis, mask):
    n = lax.axis_size(axis)
    return lax.ppermute(v, axis, [(i, i ^ mask) for i in range(n)])


def plus(a, b):
    return (a.astype(F32) + b.astype(F32)).astype(BF)


def gather_expert(v):
    pairs = lax.axis_size("expert") // 2
    mine = jnp.stack([v] + [partner(v, "expert", 2 * k) for k in range(1, pairs)])
    return jnp.stack([mine, partner(mine, "expert", 1)])


def reduce_z(s):
    total = s[0].astype(F32)
    for k in range(1, s.shape[0]):
        total = total + partner(s[k], "expert", 2 * k).astype(F32)
    return total


def reduce_expert(y):
    return reduce_z(plus(y[0], partner(y[1], "expert", 1)))


def reduce_dp(g, masks):
    n = g.shape[0]
    left = list(range(n))
    parts = {r: g[r] for r in left}
    for mask in masks:
        keep = [r for r in left if not r & mask]
        sent = jnp.stack([parts[r ^ mask] for r in keep])
        got = partner(sent, "dp", mask)
        parts = {r: plus(parts[r], got[i]) for i, r in enumerate(keep)}
        left = keep
    return parts[0]


def dp_masks():
    n = lax.axis_size("dp")
    return [1 << b for b in range(n.bit_length() - 1)]


def reduce_rest(g):
    cols = g.shape[-1]
    half = cols // 2 // LANES * LANES
    up = dp_masks()
    a = reduce_dp(g[..., :half], up)
    b = reduce_dp(g[..., half:], up[::-1])
    return jnp.concatenate([reduce_z(a), reduce_z(b)], -1)


def relative_rows(d):
    n_dp, n_ex = lax.axis_size("dp"), lax.axis_size("expert")
    n = n_dp * n_ex
    rows = d // n
    me = lax.axis_index("dp") * n_ex + lax.axis_index("expert")
    i = jnp.arange(d, dtype=jnp.int32)
    half = i // (d // 2)
    block = (i % (d // 2)) // rows * 2 + half
    source = (me ^ block) * rows + i % rows
    return (source[:, None] == jnp.arange(d, dtype=jnp.int32)[None, :]).astype(BF)


def split_rows(x, order):
    return product_right(order, x).astype(BF).reshape(2, x.shape[1] // 2, x.shape[0])


def pair_rows(x, order):
    xt = split_rows(x, order)
    return jnp.concatenate([xt[0], partner(xt[1], "expert", 1)], -1)


def pair_tokens(v):
    return jnp.concatenate([v, partner(v, "expert", 1)], 0)


def weight_grad(xt, dy):
    n_dp, n_z = lax.axis_size("dp"), lax.axis_size("expert") // 2
    g = product(xt, dy).astype(BF)
    return g.reshape(n_dp, n_z, -1, dy.shape[1])


def shards(
    tokens,
    cotangent,
    routes,
    expert_at,
    norm1_gain,
    w_query,
    w_key,
    w_value,
    w_out,
    norm2_gain,
    w_router,
    shared_gate,
    shared_up,
    shared_down,
    routed_gate,
    routed_up,
    routed_down,
):
    length, model_width = tokens.shape
    expert_count = w_router.shape[1]
    slot_count = expert_at.shape[0]
    slot_dev = routed_gate.shape[0]
    n_ex = lax.axis_size("expert")
    n_dp = lax.axis_size("dp")
    capacity = (length * TOP * 5 // (4 * expert_count) + 7) // 8 * 8
    score_scale = 1.0 / math.sqrt(HEAD_DIM)
    expert_ids = jnp.arange(expert_count, dtype=jnp.int32)
    order_d = relative_rows(model_width)

    routes_low = jnp.pad(routes.astype(BF), ((0, 0), (0, LANES - TOP)))
    early = gather_expert(jnp.concatenate([cotangent, routes_low], 1))
    early = early.reshape(n_ex, length, model_width + LANES)
    all_dy = early[:, :, :model_width]
    all_routes = early[:, :, model_width : model_width + TOP].astype(jnp.int32)

    inputs_f = tokens.astype(jnp.float32)
    scale_first = lax.rsqrt(jnp.mean(inputs_f * inputs_f, -1, keepdims=True) + epsilon)
    unit_first = inputs_f * scale_first
    normed_first = (unit_first * norm1_gain).astype(jnp.bfloat16)
    cosine, sine_table = rotary_tables(length, HEAD_DIM // 2)

    def heads_of(weight):
        return product(normed_first, weight).reshape(length, HEADS, HEAD_DIM)

    queries = rotate(heads_of(w_query), cosine, sine_table, 1.0).astype(jnp.bfloat16)
    key_heads = rotate(heads_of(w_key), cosine, sine_table, 1.0).astype(jnp.bfloat16)
    value_heads = heads_of(w_value).astype(jnp.bfloat16)
    causal = jnp.arange(length)[:, None] >= jnp.arange(length)[None, :]

    def masked_scores():
        raw_scores = (
            jnp.einsum("qhd,khd->hqk", queries, key_heads, preferred_element_type=jnp.float32)
            * score_scale
        )
        return jnp.where(causal[None], raw_scores, -1e30)

    scores_fwd = masked_scores()
    row_max = jnp.max(scores_fwd, -1, keepdims=True)
    expo_terms = jnp.exp(scores_fwd - row_max)
    row_total = jnp.sum(expo_terms, -1, keepdims=True)
    log_total = row_max + jnp.log(row_total)
    probs_low = (expo_terms / row_total).astype(jnp.bfloat16)
    attended = (
        jnp.einsum("hqk,khd->qhd", probs_low, value_heads, preferred_element_type=jnp.float32)
        .reshape(length, model_width)
        .astype(jnp.bfloat16)
    )
    residual = inputs_f + product(attended, w_out)
    scale_second = lax.rsqrt(jnp.mean(residual * residual, -1, keepdims=True) + epsilon)
    unit_second = residual * scale_second
    normed_second = (unit_second * norm2_gain).astype(jnp.bfloat16)

    all_normed = gather_expert(normed_second).reshape(n_ex, length, model_width)

    shared_g = product(normed_second, shared_gate)
    shared_u = product(normed_second, shared_up)
    shared_sigmoid = jax.nn.sigmoid(shared_g)
    shared_act = shared_g * shared_sigmoid
    shared_hidden = (shared_act * shared_u).astype(jnp.bfloat16)
    shared_result = product(shared_hidden, shared_down)
    grad_output = cotangent.astype(jnp.float32)
    d_shared = cotangent
    d_shared_hidden = product_right(d_shared, shared_down)
    d_shared_g = (
        d_shared_hidden * shared_u * shared_sigmoid * (1.0 + shared_g * (1.0 - shared_sigmoid))
    ).astype(jnp.bfloat16)
    d_shared_u = (d_shared_hidden * shared_act).astype(jnp.bfloat16)
    normed_second_t = pair_rows(normed_second, order_d)
    shared_part = weight_grad(
        normed_second_t, pair_tokens(jnp.concatenate([d_shared_g, d_shared_u], 1))
    )
    down_part = weight_grad(pair_rows(shared_hidden, relative_rows(shared_hidden.shape[1])), pair_tokens(d_shared))
    grad_sgu = reduce_rest(shared_part)
    grad_sdown = reduce_rest(down_part)
    ff = shared_gate.shape[1]
    grad_sgate, grad_sup = grad_sgu[:, :ff], grad_sgu[:, ff:]

    def router_of(rows):
        logits = product(rows, w_router)
        logit_terms = jnp.exp(logits - jnp.max(logits, -1, keepdims=True))
        return logit_terms / jnp.sum(logit_terms, -1, keepdims=True)

    router_probs = router_of(normed_second)

    my_expert = lax.dynamic_slice_in_dim(
        expert_at, lax.axis_index("expert") * slot_dev, slot_dev
    )
    member = jnp.sum(
        (all_routes[None] == my_expert[:, None, None, None]).astype(F32), -1
    )
    place = jnp.arange(length)
    earlier = (place[:, None] < place[None, :]).astype(BF)
    position = jnp.einsum("snt,tv->snv", member.astype(BF), earlier, preferred_element_type=F32)
    row_ids = jnp.arange(capacity, dtype=jnp.int32)
    pick = (
        (position.astype(jnp.int32)[:, :, None, :] == row_ids[None, None, :, None])
        & (member[:, :, None, :] > 0.5)
    )
    pick_low = pick.astype(BF)
    all_probs = router_of(all_normed)
    slot_probs = jnp.einsum(
        "nte,se->snt", all_probs, (my_expert[:, None] == expert_ids[None, :]).astype(F32),
        precision=lax.Precision.HIGHEST,
    )
    row_gate = jnp.sum(jnp.where(pick, slot_probs[:, :, None, :], 0.0), -1)
    row_gate = row_gate.reshape(slot_dev, n_ex * capacity)

    def rows_of(table):
        return (
            jnp.einsum("snrt,ntd->snrd", pick_low, table, preferred_element_type=F32)
            .astype(BF)
            .reshape(slot_dev, n_ex * capacity, model_width)
        )

    x_rows = rows_of(all_normed)
    dy_rows = rows_of(all_dy)
    d_result = (row_gate[:, :, None] * dy_rows.astype(F32)).astype(BF)
    expert_g = jnp.einsum("srd,sdf->srf", x_rows, routed_gate, preferred_element_type=F32)
    expert_u = jnp.einsum("srd,sdf->srf", x_rows, routed_up, preferred_element_type=F32)
    sigmoid_gate = jax.nn.sigmoid(expert_g)
    activated = expert_g * sigmoid_gate
    expert_hidden = (activated * expert_u).astype(BF)
    expert_result = jnp.einsum(
        "srf,sfd->srd", expert_hidden, routed_down, preferred_element_type=F32
    ).astype(BF)
    d_hidden = jnp.einsum("srd,sfd->srf", d_result, routed_down, preferred_element_type=F32)
    d_expert_g = (
        d_hidden * expert_u * sigmoid_gate * (1.0 + expert_g * (1.0 - sigmoid_gate))
    ).astype(BF)
    d_expert_u = (d_hidden * activated).astype(BF)
    d_rows = (
        jnp.einsum("srf,sdf->srd", d_expert_g, routed_gate, preferred_element_type=F32)
        + jnp.einsum("srf,sdf->srd", d_expert_u, routed_up, preferred_element_type=F32)
    ).astype(BF)
    row_d_gate = jnp.sum(dy_rows.astype(F32) * expert_result.astype(F32), -1)
    scaled = (row_gate[:, :, None] * expert_result.astype(F32)).astype(BF)

    def tokens_of(rows):
        return jnp.einsum(
            "snrt,snrd->ntd",
            pick_low,
            rows.reshape(slot_dev, n_ex, capacity, model_width),
            preferred_element_type=F32,
        ).astype(BF)

    d_gate_tokens = jnp.sum(
        jnp.where(pick, row_d_gate.reshape(slot_dev, n_ex, capacity)[..., None], 0.0), 2
    )
    wide_ids = jnp.arange(LANES, dtype=jnp.int32)
    d_gate_cols = jnp.sum(
        jnp.where(
            my_expert[:, None, None, None] == wide_ids[None, None, None, :],
            d_gate_tokens[..., None],
            0.0,
        ),
        0,
    ).astype(BF)
    back = jnp.concatenate([tokens_of(d_rows), d_gate_cols], -1)
    back = reduce_expert(back.reshape(2, n_ex // 2, length, -1))
    routed_grad, d_probs = back[:, :model_width], back[:, model_width : model_width + expert_count]
    combined = reduce_expert(tokens_of(scaled).reshape(2, n_ex // 2, length, -1))
    output = (residual + shared_result + combined).astype(BF)

    my_dp = lax.axis_index("dp")

    def routed_grad_of(left, right):
        width = left.shape[-1]
        left_t = jnp.swapaxes(left, 1, 2).reshape(slot_dev, n_dp, width // n_dp, -1)
        left_t = jnp.concatenate(
            [lax.dynamic_slice_in_dim(left_t, my_dp ^ q, 1, 1) for q in range(n_dp)], 1
        )
        return jnp.einsum("sqdr,srf->sqdf", left_t, right, preferred_element_type=F32).astype(BF)

    rg_part = routed_grad_of(x_rows, d_expert_g)
    ru_part = routed_grad_of(x_rows, d_expert_u)
    rd_part = routed_grad_of(expert_hidden, d_result)
    up_masks = dp_masks()

    def reduce_slots(part):
        return jnp.stack(
            [
                reduce_dp(part[s], up_masks if s % 2 == 0 else up_masks[::-1]).astype(F32)
                for s in range(slot_dev)
            ]
        )

    grad_rgate, grad_rup, grad_rdown = reduce_slots(rg_part), reduce_slots(ru_part), reduce_slots(rd_part)

    d_logits = (
        router_probs * (d_probs - jnp.sum(router_probs * d_probs, -1, keepdims=True))
    ).astype(jnp.bfloat16)
    d_normed_second = (
        product_right(d_shared_g, shared_gate)
        + product_right(d_shared_u, shared_up)
        + product_right(d_logits, w_router)
        + routed_grad
    )
    d_second, grad_gain_second = norm_backward(
        d_normed_second, unit_second, scale_second, norm2_gain
    )
    d_residual = grad_output + d_second
    d_branch = d_residual.astype(jnp.bfloat16)
    out_part = weight_grad(pair_rows(attended, order_d), pair_tokens(d_branch))
    grad_wout = reduce_rest(out_part)
    d_attended = (
        product_right(d_branch, w_out).astype(jnp.bfloat16).reshape(length, HEADS, HEAD_DIM)
    )
    att_probs = jnp.exp(masked_scores() - log_total)
    d_att = jnp.einsum("qhd,khd->hqk", d_attended, value_heads, preferred_element_type=jnp.float32)
    d_scores = (att_probs * (d_att - jnp.sum(att_probs * d_att, -1, keepdims=True))).astype(
        jnp.bfloat16
    )
    d_values = (
        jnp.einsum(
            "hqk,qhd->khd",
            att_probs.astype(jnp.bfloat16),
            d_attended,
            preferred_element_type=jnp.float32,
        )
        .astype(jnp.bfloat16)
        .reshape(length, model_width)
    )
    d_query_rot = (
        jnp.einsum("hqk,khd->qhd", d_scores, key_heads, preferred_element_type=jnp.float32)
        * score_scale
    )
    d_key_rot = (
        jnp.einsum("hqk,qhd->khd", d_scores, queries, preferred_element_type=jnp.float32)
        * score_scale
    )
    d_queries = (
        rotate(d_query_rot, cosine, sine_table, -1.0)
        .astype(jnp.bfloat16)
        .reshape(length, model_width)
    )
    d_keys = (
        rotate(d_key_rot, cosine, sine_table, -1.0)
        .astype(jnp.bfloat16)
        .reshape(length, model_width)
    )
    normed_first_t = pair_rows(normed_first, order_d)
    qkv_part = weight_grad(
        normed_first_t, pair_tokens(jnp.concatenate([d_queries, d_keys, d_values], 1))
    )
    d_normed_first = (
        product_right(d_queries, w_query)
        + product_right(d_keys, w_key)
        + product_right(d_values, w_value)
    )
    d_first, grad_gain_first = norm_backward(d_normed_first, unit_first, scale_first, norm1_gain)
    grad_inputs = d_residual + d_first
    small_rows = weight_grad(
        normed_second_t,
        pair_tokens(jnp.pad(d_logits, ((0, 0), (0, LANES - expert_count)))),
    )
    gains = jnp.stack([grad_gain_first, grad_gain_second], 0).astype(BF)
    gains = split_rows(gains, order_d).reshape(2, n_dp, n_ex // 2, -1, 2)
    gains = plus(gains[0], partner(gains[1], "expert", 1))
    gains = jnp.pad(gains, ((0, 0),) * 3 + ((0, LANES - 2),))
    last = reduce_rest(jnp.concatenate([qkv_part, small_rows, gains], -1))
    w = model_width
    return (
        output,
        grad_inputs,
        last[:, 3 * w + LANES],
        last[:, :w],
        last[:, w : 2 * w],
        last[:, 2 * w : 3 * w],
        grad_wout,
        last[:, 3 * w + LANES + 1],
        last[:, 3 * w : 3 * w + expert_count],
        grad_sgate,
        grad_sup,
        grad_sdown,
        grad_rgate,
        grad_rup,
        grad_rdown,
    )


def solution(mesh):
    placed = (
        P(("dp", "expert"), None),
        P(("dp", "expert"), None),
        P(("dp", "expert"), None),
        P(),
        P(),
        P(),
        P(),
        P(),
        P(),
        P(),
        P(),
        P(),
        P(),
        P(),
        P("expert", None, None),
        P("expert", None, None),
        P("expert", None, None),
    )
    return jax.shard_map(
        shards,
        mesh=mesh,
        in_specs=placed,
        out_specs=(
            P(("dp", "expert"), None),
            P(("dp", "expert"), None),
            P(("dp", "expert")),
            P(("dp", "expert"), None),
            P(("dp", "expert"), None),
            P(("dp", "expert"), None),
            P(("dp", "expert"), None),
            P(("dp", "expert")),
            P(("dp", "expert"), None),
            P(("dp", "expert"), None),
            P(("dp", "expert"), None),
            P(("dp", "expert"), None),
            P("expert", "dp", None),
            P("expert", "dp", None),
            P("expert", "dp", None),
        ),
        check_vma=False,
    )
```

```python
import functools
import math

import jax
import jax.numpy as jnp
import numpy as np
from jax import lax
from jax.experimental import pallas as pl
from jax.experimental.pallas import tpu as pltpu
from jax.sharding import PartitionSpec as P

HEADS = 10
HEAD_DIM = 128
TOP = 6
LANES = 128
epsilon = 1e-06
BF = jnp.bfloat16
F32 = jnp.float32
VMEM_LIMIT = 60 * 2**20


def product(left, right):
    return jnp.dot(left, right, preferred_element_type=jnp.float32)


def product_right(left, right):
    return lax.dot_general(
        left, right, (((1,), (1,)), ((), ())), preferred_element_type=jnp.float32
    )


def partner(v, axis, mask):
    n = lax.axis_size(axis)
    return lax.ppermute(v, axis, [(i, i ^ mask) for i in range(n)])


def plus(a, b):
    return (a.astype(F32) + b.astype(F32)).astype(BF)


def gather_z(v):
    pairs = lax.axis_size("expert") // 2
    return jnp.stack([v] + [partner(v, "expert", 2 * k) for k in range(1, pairs)])


def swap_z(s):
    return [s[0]] + [partner(s[k], "expert", 2 * k) for k in range(1, s.shape[0])]


def total(blocks):
    out = blocks[0].astype(F32)
    for b in blocks[1:]:
        out = out + b.astype(F32)
    return out


def swap_expert(mine, other):
    return swap_z(plus(mine, partner(other, "expert", 1)))


def reduce_dp(g, masks):
    n = g.shape[0]
    left = list(range(n))
    parts = {r: g[r] for r in left}
    for mask in masks:
        keep = [r for r in left if not r & mask]
        sent = jnp.stack([parts[r ^ mask] for r in keep])
        got = partner(sent, "dp", mask)
        parts = {r: plus(parts[r], got[i]) for i, r in enumerate(keep)}
        left = keep
    return parts[0]


def dp_masks():
    n = lax.axis_size("dp")
    return [1 << b for b in range(n.bit_length() - 1)]


def reduce_rest(a, b):
    up = dp_masks()
    a = reduce_dp(a, up)
    b = reduce_dp(b, up[::-1])
    low = max(a.shape[1], b.shape[1])
    a, b = (jnp.pad(v, ((0, 0), (0, low - v.shape[1]), (0, 0))) for v in (a, b))
    return total(swap_z(jnp.concatenate([a, b], -1)))


def relative_rows(d):
    n_dp, n_ex = lax.axis_size("dp"), lax.axis_size("expert")
    n = n_dp * n_ex
    rows = d // n
    me = lax.axis_index("dp") * n_ex + lax.axis_index("expert")
    i = jnp.arange(d // 2, dtype=jnp.int32)
    source = (me ^ (i // rows * 2)) * rows + i % rows
    return (source[:, None] == jnp.arange(d, dtype=jnp.int32)[None, :]).astype(BF)


def pair_rows(order, x):
    return product_right(order, x).astype(BF)


def pair_tokens(v):
    return jnp.concatenate([v, partner(v, "expert", 1)], 0)


def weight_grad(xt, dy):
    n_dp, n_z = lax.axis_size("dp"), lax.axis_size("expert") // 2
    g = product(xt, dy).astype(BF)
    return g.reshape(n_dp, n_z, -1, dy.shape[1])


def dot_nn(a, b):
    return lax.dot_general(a, b, (((1,), (0,)), ((), ())), preferred_element_type=F32)


def dot_nt(a, b):
    return lax.dot_general(a, b, (((1,), (1,)), ((), ())), preferred_element_type=F32)


def dot_tn(a, b):
    return lax.dot_general(a, b, (((0,), (0,)), ((), ())), preferred_element_type=F32)


def picks(routes_t, expert, length, capacity):
    hit = jnp.where(routes_t.astype(F32) == expert.astype(F32), 1.0, 0.0)
    member = jnp.sum(hit, 0, keepdims=True)
    a = lax.broadcasted_iota(jnp.int32, (length, length), 0)
    b = lax.broadcasted_iota(jnp.int32, (length, length), 1)
    earlier = jnp.where(a < b, 1.0, 0.0).astype(BF)
    place = dot_nn(jnp.broadcast_to(member, (16, length)).astype(BF), earlier)[:1]
    row = lax.broadcasted_iota(jnp.int32, (capacity, length), 0).astype(F32)
    return jnp.where((place == row) & (member > 0.5), 1.0, 0.0).astype(BF)


def gates_of(x, router, expert, expert_count):
    logits = dot_nn(x, router)
    lane = lax.broadcasted_iota(jnp.int32, logits.shape, 1)
    logits = jnp.where(lane < expert_count, logits, -1e30)
    terms = jnp.exp(logits - jnp.max(logits, -1, keepdims=True))
    probs = terms / jnp.sum(terms, -1, keepdims=True)
    return jnp.sum(jnp.where(lane == expert, probs, 0.0), -1, keepdims=True)


def whole(shape):
    return pl.BlockSpec(shape, lambda *_: (0,) * len(shape))


def prepare_kernel(ids, early_ref, down_ref, pick_ref, dh_ref, rows_ref):
    s = pl.program_id(0)
    sources, _, width = early_ref.shape
    capacity, length = pick_ref.shape[2:]
    expert = ids[s]
    for n in range(sources):
        pick = picks(early_ref[n, length : length + 16, :length], expert, length, capacity)
        pick_ref[0, n] = pick
        rows_ref[n * capacity : (n + 1) * capacity] = dot_nn(pick, early_ref[n, :length]).astype(BF)
    dh_ref[0] = dot_nt(rows_ref[...], down_ref[0])


def prepare(ids, early, down, capacity):
    sources, tall, width = early.shape
    length = tall - 16
    slots, ff, _ = down.shape
    rows = sources * capacity
    return pl.pallas_call(
        prepare_kernel,
        grid_spec=pltpu.PrefetchScalarGridSpec(
            num_scalar_prefetch=1,
            grid=(slots,),
            in_specs=[
                whole(early.shape),
                pl.BlockSpec((1, ff, width), lambda s, _: (s, 0, 0)),
            ],
            out_specs=[
                pl.BlockSpec((1, sources, capacity, length), lambda s, _: (s, 0, 0, 0)),
                pl.BlockSpec((1, rows, ff), lambda s, _: (s, 0, 0)),
            ],
            scratch_shapes=[pltpu.VMEM((rows, width), BF)],
        ),
        out_shape=[
            jax.ShapeDtypeStruct((slots, sources, capacity, length), BF),
            jax.ShapeDtypeStruct((slots, rows, ff), F32),
        ],
        compiler_params=pltpu.CompilerParams(vmem_limit_bytes=VMEM_LIMIT),
        cost_estimate=pl.CostEstimate(
            flops=2 * slots * rows * width * (ff + length),
            bytes_accessed=slots * ff * (width * 2 + rows * 4),
            transcendentals=0,
        ),
        name="prepare",
    )(ids, early, down)


def experts_kernel(
    expert_count, ids, ns_ref, pick_ref, dh_ref, gate_ref, up_ref, router_ref,
    back_ref, hid_ref, row_gate_ref, x_ref, acc_ref, acc_p_ref,
):
    s = pl.program_id(0)
    slots = pl.num_programs(0)
    sources, length, width = ns_ref.shape
    capacity = pick_ref.shape[2]
    expert = ids[s]
    for n in range(sources):
        x_ref[n * capacity : (n + 1) * capacity] = dot_nn(pick_ref[0, n], ns_ref[n]).astype(BF)
    x = x_ref[...]
    row_gate = gates_of(x, router_ref[...], expert, expert_count)
    row_gate_ref[0] = jnp.broadcast_to(row_gate, row_gate_ref.shape[1:])
    g = dot_nn(x, gate_ref[0])
    u = dot_nn(x, up_ref[0])
    sig = jax.nn.sigmoid(g)
    act = g * sig
    hid = (act * u).astype(BF)
    hid_ref[0] = hid
    raw = dh_ref[0]
    d_gate = jnp.sum(hid.astype(F32) * raw, -1, keepdims=True)
    dh = raw * row_gate
    dg = (dh * u * sig * (1.0 + g * (1.0 - sig))).astype(BF)
    du = (dh * act).astype(BF)
    d_rows = (dot_nt(dg, gate_ref[0]) + dot_nt(du, up_ref[0])).astype(BF)

    @pl.when(s == 0)
    def _():
        acc_ref[...] = jnp.zeros_like(acc_ref)
        acc_p_ref[...] = jnp.zeros_like(acc_p_ref)

    parts = acc_p_ref.shape[2] // length
    row = lax.broadcasted_iota(jnp.int32, (16, length), 0)
    for n in range(sources):
        pick = pick_ref[0, n]
        acc_ref[n] += dot_tn(pick, d_rows[n * capacity : (n + 1) * capacity])
        column = d_gate[n * capacity : (n + 1) * capacity]
        token = jnp.sum(pick.astype(F32) * column, 0, keepdims=True)
        for b in range(parts):
            acc_p_ref[n, :, b * length : (b + 1) * length] += jnp.where(
                row == expert - 16 * b, token, 0.0
            )

    @pl.when(s == slots - 1)
    def _():
        wide = parts * length
        for n in range(sources):
            back_ref[n, :length] = acc_ref[n].astype(BF)
            back_ref[n, length:, :wide] = acc_p_ref[n].astype(BF)
            if wide < width:
                back_ref[n, length:, wide:] = jnp.zeros((16, width - wide), BF)


def experts(ids, ns, pick, dh, gate, up, router, expert_count):
    sources, length, width = ns.shape
    slots, _, capacity, _ = pick.shape
    ff = gate.shape[2]
    rows = sources * capacity
    wide = -(-expert_count // 16) * length
    per_slot = lambda *shape: pl.BlockSpec((1,) + shape, lambda s, _: (s,) + (0,) * len(shape))
    return pl.pallas_call(
        functools.partial(experts_kernel, expert_count),
        grid_spec=pltpu.PrefetchScalarGridSpec(
            num_scalar_prefetch=1,
            grid=(slots,),
            in_specs=[
                whole(ns.shape),
                per_slot(sources, capacity, length),
                per_slot(rows, ff),
                per_slot(width, ff),
                per_slot(width, ff),
                whole(router.shape),
            ],
            out_specs=[
                whole((sources, length + 16, width)),
                per_slot(rows, ff),
                per_slot(rows, LANES),
            ],
            scratch_shapes=[
                pltpu.VMEM((rows, width), BF),
                pltpu.VMEM((sources, length, width), F32),
                pltpu.VMEM((sources, 16, wide), F32),
            ],
        ),
        out_shape=[
            jax.ShapeDtypeStruct((sources, length + 16, width), BF),
            jax.ShapeDtypeStruct((slots, rows, ff), BF),
            jax.ShapeDtypeStruct((slots, rows, LANES), F32),
        ],
        compiler_params=pltpu.CompilerParams(vmem_limit_bytes=VMEM_LIMIT),
        cost_estimate=pl.CostEstimate(
            flops=8 * slots * rows * width * ff,
            bytes_accessed=slots * ff * (width * 4 + rows * 6),
            transcendentals=slots * rows * ff,
        ),
        name="experts",
    )(ids, ns, pick, dh, gate, up, router)


def combine_kernel(hid_ref, row_gate_ref, pick_ref, down_ref, out_ref, acc_ref):
    s = pl.program_id(0)
    sources, length, _ = out_ref.shape
    capacity = pick_ref.shape[2]
    result = dot_nn(hid_ref[0], down_ref[0]).astype(BF)
    scaled = (result.astype(F32) * row_gate_ref[0, :, :1]).astype(BF)

    @pl.when(s == 0)
    def _():
        acc_ref[...] = jnp.zeros_like(acc_ref)

    for n in range(sources):
        acc_ref[n] += dot_tn(pick_ref[0, n], scaled[n * capacity : (n + 1) * capacity])

    @pl.when(s == pl.num_programs(0) - 1)
    def _():
        out_ref[...] = acc_ref[...].astype(BF)


def combine(hid, row_gate, pick, down):
    slots, sources, capacity, length = pick.shape
    _, ff, width = down.shape
    rows = sources * capacity
    per_slot = lambda *shape: pl.BlockSpec((1,) + shape, lambda s: (s,) + (0,) * len(shape))
    return pl.pallas_call(
        combine_kernel,
        grid=(slots,),
        in_specs=[
            per_slot(rows, ff),
            per_slot(rows, LANES),
            per_slot(sources, capacity, length),
            per_slot(ff, width),
        ],
        out_specs=whole((sources, length, width)),
        scratch_shapes=[pltpu.VMEM((sources, length, width), F32)],
        out_shape=jax.ShapeDtypeStruct((sources, length, width), BF),
        compiler_params=pltpu.CompilerParams(vmem_limit_bytes=VMEM_LIMIT),
        cost_estimate=pl.CostEstimate(
            flops=2 * slots * rows * width * (ff + length),
            bytes_accessed=slots * ff * (width * 2 + rows * 2),
            transcendentals=0,
        ),
        name="combine",
    )(hid, row_gate, pick, down)


def routed_grads_kernel(
    groups, expert_count, capacity, ids, *refs
):
    ns_refs, early_refs = refs[:groups], refs[groups : 2 * groups]
    gate_ref, up_ref, down_ref, router_ref, sel_d_ref, sel_f_ref = refs[2 * groups : 2 * groups + 6]
    og_ref, ou_ref, od_ref = refs[2 * groups + 6 : 2 * groups + 9]
    ns_buf, early_buf, x_ref, dy_ref, sems = refs[2 * groups + 9 :]
    q, s = pl.program_id(0), pl.program_id(1)
    slots = pl.num_programs(1)
    sources, length, width = ns_buf.shape[1:]
    expert = ids[s]
    now = lax.rem(q, 2)

    def copies(i, slot):
        return (
            pltpu.make_async_copy(ns_refs[i], ns_buf.at[slot], sems.at[slot, 0]),
            pltpu.make_async_copy(early_refs[i], early_buf.at[slot], sems.at[slot, 1]),
        )

    @pl.when(s == 0)
    def _():
        for i in range(groups):
            @pl.when(q == i)
            def _():
                if i == 0:
                    for c in copies(0, 0):
                        c.start()
                if i + 1 < groups:
                    for c in copies(i + 1, (i + 1) % 2):
                        c.start()
                for c in copies(i, i % 2):
                    c.wait()

    for n in range(sources):
        pick = picks(early_buf[now, n, length:, :length], expert, length, capacity)
        x_ref[n * capacity : (n + 1) * capacity] = dot_nn(pick, ns_buf[now, n]).astype(BF)
        dy_ref[n * capacity : (n + 1) * capacity] = dot_nn(pick, early_buf[now, n, :length]).astype(BF)
    x = x_ref[...]
    row_gate = gates_of(x, router_ref[...], expert, expert_count)
    d_result = (dy_ref[...].astype(F32) * row_gate).astype(BF)
    g = dot_nn(x, gate_ref[s])
    u = dot_nn(x, up_ref[s])
    sig = jax.nn.sigmoid(g)
    act = g * sig
    hid = (act * u).astype(BF)
    dh = dot_nt(d_result, down_ref[s])
    dg = (dh * u * sig * (1.0 + g * (1.0 - sig))).astype(BF)
    du = (dh * act).astype(BF)
    x_t = dot_nt(sel_d_ref[...], x).astype(BF)
    hid_t = dot_nt(sel_f_ref[...], hid).astype(BF)

    @pl.when(q == 0)
    def _():
        og_ref[s] = dot_nn(x_t, dg)
        ou_ref[s] = dot_nn(x_t, du)
        od_ref[s] = dot_nn(hid_t, d_result)

    @pl.when(q > 0)
    def _():
        og_ref[s] += dot_nn(x_t, dg)
        ou_ref[s] += dot_nn(x_t, du)
        od_ref[s] += dot_nn(hid_t, d_result)


def routed_grads(ids, ns_groups, early_groups, gate, up, down, router, expert_count, capacity, n_dp):
    groups = len(ns_groups)
    sources, length, width = ns_groups[0].shape
    slots, _, ff = gate.shape
    rows = sources * capacity
    mine = lax.axis_index("dp")

    def selector(size):
        part = size // n_dp
        i = jnp.arange(part, dtype=jnp.int32)[:, None] + mine * part
        return (i == jnp.arange(size, dtype=jnp.int32)[None, :]).astype(BF)

    once = lambda shape: pl.BlockSpec(
        shape, lambda *_: (0,) * len(shape), pipeline_mode=pl.Buffered(1)
    )
    sel_d, sel_f = selector(width), selector(ff)
    shapes = [(slots, width // n_dp, ff)] * 2 + [(slots, ff // n_dp, width)]
    return pl.pallas_call(
        functools.partial(routed_grads_kernel, groups, expert_count, capacity),
        grid_spec=pltpu.PrefetchScalarGridSpec(
            num_scalar_prefetch=1,
            grid=(groups, slots),
            in_specs=[pl.BlockSpec(memory_space=pl.ANY)] * (2 * groups)
            + [once(a.shape) for a in (gate, up, down, router, sel_d, sel_f)],
            out_specs=[once(shape) for shape in shapes],
            scratch_shapes=[
                pltpu.VMEM((2, sources, length, width), BF),
                pltpu.VMEM((2, sources, length + 16, width), BF),
                pltpu.VMEM((rows, width), BF),
                pltpu.VMEM((rows, width), BF),
                pltpu.SemaphoreType.DMA((2, 2)),
            ],
        ),
        out_shape=[jax.ShapeDtypeStruct(shape, F32) for shape in shapes],
        compiler_params=pltpu.CompilerParams(vmem_limit_bytes=VMEM_LIMIT),
        cost_estimate=pl.CostEstimate(
            flops=10 * groups * slots * rows * width * ff,
            bytes_accessed=6 * slots * width * ff + 4 * groups * sources * length * width,
            transcendentals=groups * slots * rows * ff,
        ),
        name="routed_grads",
    )(ids, *ns_groups, *early_groups, gate, up, down, router, sel_d, sel_f)


def rotary(length):
    half = HEAD_DIM // 2
    frequencies = np.exp(np.arange(half, dtype=np.float32) * np.float32(-math.log(10000.0) / half))
    angles = np.arange(length, dtype=np.float32)[:, None] * frequencies.astype(np.float32)[None, :]
    cosine, sine = np.cos(angles), np.sin(angles)
    return (
        np.concatenate([cosine, cosine], 1).astype(np.float32),
        np.concatenate([-sine, sine], 1).astype(np.float32),
    )


def turn(x, cosine, sine):
    return x * cosine + pltpu.roll(x, HEAD_DIM // 2, 1) * sine


def causal_probs(q, k):
    scores = dot_nt(q, k) * (1.0 / math.sqrt(HEAD_DIM))
    row = lax.broadcasted_iota(jnp.int32, scores.shape, 0)
    lane = lax.broadcasted_iota(jnp.int32, scores.shape, 1)
    scores = jnp.where(row >= lane, scores, -1e30)
    terms = jnp.exp(scores - jnp.max(scores, -1, keepdims=True))
    return terms / jnp.sum(terms, -1, keepdims=True)


def unit_of(x):
    scale = lax.rsqrt(jnp.mean(x * x, -1, keepdims=True) + epsilon)
    return x * scale, scale


def attention_kernel(
    x_ref, gain1_ref, gain2_ref, cos_ref, sin_ref, wq_ref, wk_ref, wv_ref, wo_ref,
    q_ref, k_ref, v_ref, att_ref, nf_ref, residual_ref, ns_ref,
):
    i = pl.program_id(0)

    @pl.when(i == 0)
    def _():
        x = x_ref[...].astype(F32)
        nf_ref[...] = (unit_of(x)[0] * gain1_ref[...]).astype(BF)
        residual_ref[...] = x

    nf = nf_ref[...]
    q_all, k_all, v_all = dot_nn(nf, wq_ref[...]), dot_nn(nf, wk_ref[...]), dot_nn(nf, wv_ref[...])
    cosine, sine = cos_ref[...], sin_ref[...]
    v_ref[...] = v_all.astype(BF)
    for h in range(q_ref.shape[1] // HEAD_DIM):
        at = slice(h * HEAD_DIM, (h + 1) * HEAD_DIM)
        q = turn(q_all[:, at], cosine, sine).astype(BF)
        k = turn(k_all[:, at], cosine, sine).astype(BF)
        q_ref[:, at] = q
        k_ref[:, at] = k
        att_ref[:, at] = dot_nn(causal_probs(q, k).astype(BF), v_all[:, at].astype(BF)).astype(BF)
    residual_ref[...] += dot_nn(att_ref[...], wo_ref[...])

    @pl.when(i == pl.num_programs(0) - 1)
    def _():
        ns_ref[...] = (unit_of(residual_ref[...])[0] * gain2_ref[...]).astype(BF)


def attention(x, gain1, gain2, cosine, sine, wq, wk, wv, wo):
    length, width = x.shape
    step = 2 * HEAD_DIM
    columns = lambda rows: pl.BlockSpec((rows, step), lambda i: (0, i))
    low = jax.ShapeDtypeStruct((length, width), BF)
    return pl.pallas_call(
        attention_kernel,
        grid=(width // step,),
        in_specs=[
            whole((length, width)),
            whole((1, width)),
            whole((1, width)),
            whole(cosine.shape),
            whole(sine.shape),
            columns(width),
            columns(width),
            columns(width),
            pl.BlockSpec((step, width), lambda i: (i, 0)),
        ],
        out_specs=[columns(length)] * 4 + [whole((length, width))] * 3,
        out_shape=[low] * 5 + [jax.ShapeDtypeStruct((length, width), F32), low],
        compiler_params=pltpu.CompilerParams(vmem_limit_bytes=VMEM_LIMIT),
        cost_estimate=pl.CostEstimate(
            flops=8 * length * width * width, bytes_accessed=8 * width * width, transcendentals=0
        ),
        name="attention",
    )(x, gain1, gain2, cosine, sine, wq, wk, wv, wo)


def backward_kernel(
    expert_count, n_parts,
    x_ref, dy_ref, residual_ref, ns_ref, shared_ref, router_t_ref, gain1_ref, gain2_ref,
    cos_ref, sin_ref, q_ref, k_ref, v_ref, wq_ref, wk_ref, wv_ref, wo_ref, *refs,
):
    parts = refs[:n_parts]
    cat_ref, logits_ref, gains_ref, grad_ref, branch_ref, d_res_ref, acc_ref = refs[n_parts:]
    i = pl.program_id(0)
    length, width = x_ref.shape
    step = wq_ref.shape[1]

    @pl.when(i == 0)
    def _():
        back = parts[0][:length].astype(F32)
        tail = parts[0][length:].astype(F32)
        for p in parts[1:]:
            back += p[:length].astype(F32)
            tail += p[length:].astype(F32)
        blocks = router_t_ref.shape[0] // 16
        d_probs = jnp.concatenate([tail[:, b * length : (b + 1) * length] for b in range(blocks)], 0)
        logits = dot_nt(router_t_ref[...], ns_ref[...])
        row = lax.broadcasted_iota(jnp.int32, logits.shape, 0)
        logits = jnp.where(row < expert_count, logits, -1e30)
        terms = jnp.exp(logits - jnp.max(logits, 0, keepdims=True))
        probs = terms / jnp.sum(terms, 0, keepdims=True)
        d_logits = probs * (d_probs - jnp.sum(probs * d_probs, 0, keepdims=True))
        d_logits = jnp.where(row < expert_count, d_logits, 0.0).astype(BF)
        high = jnp.concatenate(
            [d_logits.astype(F32), jnp.zeros((LANES - d_logits.shape[0], length), F32)], 0
        )
        logits_ref[...] = high.T.astype(BF)
        d_normed = shared_ref[...] + back + dot_tn(d_logits, router_t_ref[...])
        unit, scale = unit_of(residual_ref[...])
        c = d_normed * gain2_ref[...]
        gains_ref[1:2] = jnp.sum(d_normed * unit, 0, keepdims=True)
        d_res = dy_ref[...].astype(F32) + scale * (c - unit * jnp.mean(c * unit, -1, keepdims=True))
        d_res_ref[...] = d_res
        branch_ref[...] = d_res.astype(BF)
        acc_ref[...] = jnp.zeros_like(acc_ref)

    cosine, sine = cos_ref[...], -sin_ref[...]
    att_scale = 1.0 / math.sqrt(HEAD_DIM)
    d_att_all = dot_nt(branch_ref[...], wo_ref[...]).astype(BF)
    for h in range(step // HEAD_DIM):
        at = slice(h * HEAD_DIM, (h + 1) * HEAD_DIM)
        q, k, v, d_attended = q_ref[:, at], k_ref[:, at], v_ref[:, at], d_att_all[:, at]
        probs = causal_probs(q, k)
        d_att = dot_nt(d_attended, v)
        d_scores = (probs * (d_att - jnp.sum(probs * d_att, -1, keepdims=True))).astype(BF)
        cat_ref[0, :, at] = turn(dot_nn(d_scores, k) * att_scale, cosine, sine).astype(BF)
        cat_ref[1, :, at] = turn(dot_tn(d_scores, q) * att_scale, cosine, sine).astype(BF)
        cat_ref[2, :, at] = dot_tn(probs.astype(BF), d_attended).astype(BF)
    cat_ref[3] = branch_ref[:, pl.ds(pl.multiple_of(i * step, step), step)]
    acc_ref[...] += (
        dot_nt(cat_ref[0], wq_ref[...])
        + dot_nt(cat_ref[1], wk_ref[...])
        + dot_nt(cat_ref[2], wv_ref[...])
    )

    @pl.when(i == pl.num_programs(0) - 1)
    def _():
        unit, scale = unit_of(x_ref[...].astype(F32))
        d_normed = acc_ref[...]
        c = d_normed * gain1_ref[...]
        gains_ref[0:1] = jnp.sum(d_normed * unit, 0, keepdims=True)
        grad_ref[...] = d_res_ref[...] + scale * (c - unit * jnp.mean(c * unit, -1, keepdims=True))


def backward(
    x, dy, residual, ns, shared, router_t, gain1, gain2, cosine, sine,
    q, k, v, wq, wk, wv, wo, parts, expert_count,
):
    length, width = x.shape
    step = 2 * HEAD_DIM
    columns = lambda rows: pl.BlockSpec((rows, step), lambda i: (0, i))
    tall = whole((length, width))
    return pl.pallas_call(
        functools.partial(backward_kernel, expert_count, len(parts)),
        grid=(width // step,),
        in_specs=[tall] * 5
        + [whole(router_t.shape), whole((1, width)), whole((1, width))]
        + [whole(cosine.shape)] * 2
        + [columns(length)] * 3
        + [columns(width)] * 3
        + [pl.BlockSpec((step, width), lambda i: (i, 0))]
        + [whole(parts[0].shape)] * len(parts),
        out_specs=[
            pl.BlockSpec((4, length, step), lambda i: (0, 0, i)),
            whole((length, LANES)),
            whole((2, width)),
            tall,
        ],
        scratch_shapes=[
            pltpu.VMEM((length, width), BF),
            pltpu.VMEM((length, width), F32),
            pltpu.VMEM((length, width), F32),
        ],
        out_shape=[
            jax.ShapeDtypeStruct((4, length, width), BF),
            jax.ShapeDtypeStruct((length, LANES), BF),
            jax.ShapeDtypeStruct((2, width), F32),
            jax.ShapeDtypeStruct((length, width), F32),
        ],
        compiler_params=pltpu.CompilerParams(vmem_limit_bytes=VMEM_LIMIT),
        cost_estimate=pl.CostEstimate(
            flops=8 * length * width * width, bytes_accessed=8 * width * width, transcendentals=0
        ),
        name="backward",
    )(
        x, dy, residual, ns, shared, router_t, gain1, gain2, cosine, sine,
        q, k, v, wq, wk, wv, wo, *parts,
    )


def tie(*values):
    return lax.optimization_barrier(values)


def shards(
    tokens,
    cotangent,
    routes,
    expert_at,
    norm1_gain,
    w_query,
    w_key,
    w_value,
    w_out,
    norm2_gain,
    w_router,
    shared_gate,
    shared_up,
    shared_down,
    routed_gate,
    routed_up,
    routed_down,
):
    length, model_width = tokens.shape
    expert_count = w_router.shape[1]
    slot_dev = routed_gate.shape[0]
    n_ex = lax.axis_size("expert")
    n_dp = lax.axis_size("dp")
    capacity = (length * TOP * 5 // (4 * expert_count) + 7) // 8 * 8
    order_d = relative_rows(model_width)

    routes_t = jnp.pad(routes.T.astype(BF), ((0, 16 - TOP), (0, 0)), constant_values=-1)
    routes_t = jnp.pad(routes_t, ((0, 0), (0, model_width - length)))
    early = gather_z(jnp.concatenate([cotangent, routes_t], 0))
    cosine, sine = (jnp.asarray(t) for t in rotary(length))
    gain1, gain2 = norm1_gain[None], norm2_gain[None]
    queries, key_rows, value_rows, attended, normed_first, residual, normed_second = attention(
        tokens, gain1, gain2, cosine, sine, w_query, w_key, w_value, w_out
    )
    early, normed_second = tie(early, normed_second)
    early_other = partner(early, "expert", 1)
    ns = gather_z(normed_second)
    ns_other = partner(ns, "expert", 1)

    shared_g = product(normed_second, shared_gate)
    shared_u = product(normed_second, shared_up)
    shared_sigmoid = jax.nn.sigmoid(shared_g)
    shared_act = shared_g * shared_sigmoid
    shared_hidden = (shared_act * shared_u).astype(jnp.bfloat16)
    shared_result = product(shared_hidden, shared_down)
    d_shared = cotangent
    d_shared_hidden = product_right(d_shared, shared_down)
    d_shared_g = (
        d_shared_hidden * shared_u * shared_sigmoid * (1.0 + shared_g * (1.0 - shared_sigmoid))
    ).astype(jnp.bfloat16)
    d_shared_u = (d_shared_hidden * shared_act).astype(jnp.bfloat16)
    both_second = jnp.concatenate([normed_second, ns_other[0]], 0)
    normed_second_t = pair_rows(order_d, both_second)
    ff = shared_gate.shape[1]
    from_shared = pair_tokens(jnp.concatenate([d_shared_g, d_shared_u, shared_hidden], 1))
    sgu_part = weight_grad(normed_second_t, from_shared[:, : 2 * ff])
    down_part = weight_grad(
        pair_rows(relative_rows(ff), from_shared[:, 2 * ff :]),
        jnp.concatenate([cotangent, early_other[0, :length]], 0),
    )
    grad_shared = reduce_rest(sgu_part, down_part)
    grad_sgate, grad_sup = grad_shared[:, :ff], grad_shared[:, ff : 2 * ff]
    grad_sdown = grad_shared[: ff // (n_dp * n_ex), 2 * ff :]

    my_expert = lax.dynamic_slice_in_dim(
        expert_at, lax.axis_index("expert") * slot_dev, slot_dev
    )
    router_wide = jnp.pad(w_router, ((0, 0), (0, LANES - expert_count)))
    sides = []
    for e_side, n_side in ((early, ns), (early_other, ns_other)):
        pick, dh_raw = prepare(my_expert, e_side, routed_down, capacity)
        back, hid, row_gate = experts(
            my_expert, n_side, pick, dh_raw, routed_gate, routed_up, router_wide, expert_count
        )
        sides.append((back, combine(hid, row_gate, pick, routed_down)))
    back = swap_expert(sides[0][0], sides[1][0])
    combined = total(swap_expert(sides[0][1], sides[1][1]))
    output = (residual + shared_result + combined).astype(BF)

    ns_groups, early_groups = [ns, ns_other], [early, early_other]
    for q in range(1, n_dp):
        for v, groups in ((ns, ns_groups), (early, early_groups)):
            mine = partner(v, "dp", q)
            groups += [mine, partner(mine, "expert", 1)]

    shared_back = product_right(d_shared_g, shared_gate) + product_right(d_shared_u, shared_up)
    high = -(-expert_count // 16) * 16
    router_t = jnp.pad(w_router.T, ((0, high - expert_count), (0, 0)))
    d_cat, wide_logits, gains, grad_inputs = backward(
        tokens, cotangent, residual, normed_second, shared_back, router_t, gain1, gain2, cosine, sine,
        queries, key_rows, value_rows, w_query, w_key, w_value, w_out, back, expert_count,
    )

    ns_groups[-1], d_cat = tie(ns_groups[-1], d_cat)
    grad_rgate, grad_rup, grad_rdown = routed_grads(
        my_expert, ns_groups, early_groups, routed_gate, routed_up, routed_down, router_wide,
        expert_count, capacity, n_dp,
    )

    w = model_width
    firsts = jnp.stack([normed_first, attended])
    firsts_other = partner(firsts, "expert", 1)
    lasts = jnp.concatenate([d_cat, partner(d_cat, "expert", 1)], 1)
    normed_first_t, attended_t = (
        pair_rows(order_d, jnp.concatenate([v, firsts_other[i]], 0))
        for i, v in enumerate((normed_first, attended))
    )
    gains = (gains + partner(gains, "expert", 1)).astype(BF)
    gains = pair_rows(order_d, gains).reshape(n_dp, n_ex // 2, -1, 2)
    gains = jnp.pad(gains, ((0, 0),) * 3 + ((0, LANES - 2),))
    q_part, k_part, v_part = (weight_grad(normed_first_t, lasts[i]) for i in range(3))
    out_part = weight_grad(attended_t, lasts[3])
    router_part = weight_grad(normed_second_t, pair_tokens(wide_logits))
    last = reduce_rest(
        jnp.concatenate([q_part, k_part], -1),
        jnp.concatenate([v_part, out_part, router_part, gains], -1),
    )
    return (
        output,
        grad_inputs,
        last[:, 4 * w + LANES],
        last[:, :w],
        last[:, w : 2 * w],
        last[:, 2 * w : 3 * w],
        last[:, 3 * w : 4 * w],
        last[:, 4 * w + LANES + 1],
        last[:, 4 * w : 4 * w + expert_count],
        grad_sgate,
        grad_sup,
        grad_sdown,
        grad_rgate,
        grad_rup,
        grad_rdown,
    )


def solution(mesh):
    placed = (
        P(("dp", "expert"), None),
        P(("dp", "expert"), None),
        P(("dp", "expert"), None),
        P(),
        P(),
        P(),
        P(),
        P(),
        P(),
        P(),
        P(),
        P(),
        P(),
        P(),
        P("expert", None, None),
        P("expert", None, None),
        P("expert", None, None),
    )
    return jax.shard_map(
        shards,
        mesh=mesh,
        in_specs=placed,
        out_specs=(
            P(("dp", "expert"), None),
            P(("dp", "expert"), None),
            P(("dp", "expert")),
            P(("dp", "expert"), None),
            P(("dp", "expert"), None),
            P(("dp", "expert"), None),
            P(("dp", "expert"), None),
            P(("dp", "expert")),
            P(("dp", "expert"), None),
            P(("dp", "expert"), None),
            P(("dp", "expert"), None),
            P(("dp", "expert"), None),
            P("expert", "dp", None),
            P("expert", "dp", None),
            P("expert", "dp", None),
        ),
        check_vma=False,
    )
```

```python
import functools
import math

import jax
import jax.numpy as jnp
import numpy as np
from jax import lax
from jax.experimental import pallas as pl
from jax.experimental.pallas import tpu as pltpu
from jax.sharding import PartitionSpec as P

HEADS = 10
HEAD_DIM = 128
TOP = 6
LANES = 128
epsilon = 1e-06
BF = jnp.bfloat16
F32 = jnp.float32
VMEM_LIMIT = 60 * 2**20
COST = 1


def partner(v, axis, mask):
    n = lax.axis_size(axis)
    return lax.ppermute(v, axis, [(i, i ^ mask) for i in range(n)])


def plus(a, b):
    return (a.astype(F32) + b.astype(F32)).astype(BF)


def along_z(v, pairs):
    return lax.ppermute(v, "expert", [(2 * a + c, 2 * b + c) for a, b in pairs for c in (0, 1)])


def gather_z(v):
    n_z = lax.axis_size("expert") // 2
    return [v] + [along_z(v, [((z - k) % n_z, z) for z in range(n_z)]) for k in range(1, n_z)]


def exchange_z(s):
    n_z = lax.axis_size("expert") // 2
    groups = [[2 * z + c for z in range(n_z)] for c in (0, 1)]
    return lax.all_to_all(s, "expert", 0, 0, tiled=True, axis_index_groups=groups)


def total(blocks):
    out = blocks[0].astype(F32)
    for b in blocks[1:]:
        out = out + b.astype(F32)
    return out


def reduce_here(s):
    return total(list(exchange_z(s)))


def rows_for(d, blocks):
    n_dp, n_ex = lax.axis_size("dp"), lax.axis_size("expert")
    rows = d // (n_dp * n_ex)
    n_z = n_ex // 2
    my_dp, my_core = lax.axis_index("dp"), lax.axis_index("expert") % 2
    at = np.arange(len(blocks) * n_z * rows, dtype=np.int32)
    block_dp = jnp.asarray(np.repeat(np.array(blocks, np.int32), n_z * rows)) ^ my_dp
    block = (block_dp * n_z + jnp.asarray(at // rows % n_z)) * 2 + my_core
    source = block * rows + jnp.asarray(at % rows)
    return (source[:, None] == jnp.arange(d, dtype=jnp.int32)[None, :]).astype(BF)


def dot_nn(a, b):
    return lax.dot_general(a, b, (((1,), (0,)), ((), ())), preferred_element_type=F32)


def dot_nt(a, b):
    return lax.dot_general(a, b, (((1,), (1,)), ((), ())), preferred_element_type=F32)


def dot_tn(a, b):
    return lax.dot_general(a, b, (((0,), (0,)), ((), ())), preferred_element_type=F32)


def picks(routes_t, expert, length, capacity):
    hit = jnp.where(routes_t.astype(F32) == expert.astype(F32), 1.0, 0.0)
    member = jnp.sum(hit, 0, keepdims=True)
    a = lax.broadcasted_iota(jnp.int32, (length, length), 0)
    b = lax.broadcasted_iota(jnp.int32, (length, length), 1)
    earlier = jnp.where(a < b, 1.0, 0.0).astype(BF)
    place = dot_nn(jnp.broadcast_to(member, (16, length)).astype(BF), earlier)[:1]
    row = lax.broadcasted_iota(jnp.int32, (capacity, length), 0).astype(F32)
    return jnp.where((place == row) & (member > 0.5), 1.0, 0.0).astype(BF)


def gates_of(x, router, expert, expert_count):
    logits = dot_nn(x, router)
    lane = lax.broadcasted_iota(jnp.int32, logits.shape, 1)
    logits = jnp.where(lane < expert_count, logits, -1e30)
    terms = jnp.exp(logits - jnp.max(logits, -1, keepdims=True))
    probs = terms / jnp.sum(terms, -1, keepdims=True)
    return jnp.sum(jnp.where(lane == expert, probs, 0.0), -1, keepdims=True)


def whole(shape):
    return pl.BlockSpec(shape, lambda *_: (0,) * len(shape))


def prepare_kernel(ids, early_ref, other_ref, down_ref, pick_ref, dh_ref, dy_ref):
    expert = ids[pl.program_id(0)]
    sources = early_ref.shape[0]
    capacity, length = pick_ref.shape[2:]
    for j, ref in enumerate((early_ref, other_ref)):
        for k in range(sources):
            n = j * sources + k
            pick = picks(ref[k, length : length + 16, :length], expert, length, capacity)
            pick_ref[0, n] = pick
            dy_ref[0, n * capacity : (n + 1) * capacity] = dot_nn(pick, ref[k, :length]).astype(BF)
    dh_ref[0] = dot_nt(dy_ref[0], down_ref[0])


def per_slot(*shape):
    return pl.BlockSpec((1,) + shape, lambda s, *_: (s,) + (0,) * len(shape))


def once(shape):
    return pl.BlockSpec(shape, lambda *_: (0,) * len(shape), pipeline_mode=pl.Buffered(1))


def prepare(ids, early, down, capacity):
    sources, length = early[0].shape[0], early[0].shape[1] - 16
    slots, ff, width = down.shape
    rows = 2 * sources * capacity
    return pl.pallas_call(
        prepare_kernel,
        grid_spec=pltpu.PrefetchScalarGridSpec(
            num_scalar_prefetch=1,
            grid=(slots,),
            in_specs=[once(v.shape) for v in early] + [per_slot(ff, width)],
            out_specs=[
                per_slot(2 * sources, capacity, length),
                per_slot(rows, ff),
                per_slot(rows, width),
            ],
        ),
        out_shape=[
            jax.ShapeDtypeStruct((slots, 2 * sources, capacity, length), BF),
            jax.ShapeDtypeStruct((slots, rows, ff), F32),
            jax.ShapeDtypeStruct((slots, rows, width), BF),
        ],
        compiler_params=pltpu.CompilerParams(vmem_limit_bytes=VMEM_LIMIT),
        cost_estimate=pl.CostEstimate(
            flops=int(COST * (4 * slots * rows * width * (ff + length))),
            bytes_accessed=int(COST * (slots * ff * (width * 2 + rows * 4))),
            transcendentals=0,
        ),
        name="prepare",
    )(ids, *early, down)


def experts_kernel(
    expert_count, ids, ns0_ref, ns1_ref, pick_ref, dh_ref, gate_ref, up_ref, router_ref,
    back0_ref, back1_ref, hid_ref, dg_ref, du_ref, rows_ref, row_gate_ref, d_rows_ref, probs_ref,
):
    s = pl.program_id(0)
    slots, total_sources, capacity, length = pick_ref.shape
    sources, _, width = ns0_ref.shape
    expert = ids[s]
    sides = [(ns0_ref, back0_ref), (ns1_ref, back1_ref)]
    for n in range(total_sources):
        ns = sides[n // sources][0][n % sources]
        rows_ref[0, n * capacity : (n + 1) * capacity] = dot_nn(pick_ref[s, n], ns).astype(BF)
    x = rows_ref[0]
    row_gate = gates_of(x, router_ref[...], expert, expert_count)
    row_gate_ref[0] = jnp.broadcast_to(row_gate, row_gate_ref.shape[1:])
    g = dot_nn(x, gate_ref[0])
    u = dot_nn(x, up_ref[0])
    sig = jax.nn.sigmoid(g)
    act = g * sig
    hid = (act * u).astype(BF)
    hid_ref[0] = hid
    raw = dh_ref[0]
    d_gate = jnp.sum(hid.astype(F32) * raw, -1, keepdims=True)
    dh = raw * row_gate
    dg = (dh * u * sig * (1.0 + g * (1.0 - sig))).astype(BF)
    du = (dh * act).astype(BF)
    dg_ref[0] = dg
    du_ref[0] = du
    d_rows_ref[s] = (dot_nt(dg, gate_ref[0]) + dot_nt(du, up_ref[0])).astype(BF)

    @pl.when(s == 0)
    def _():
        probs_ref[...] = jnp.zeros_like(probs_ref)

    parts = probs_ref.shape[2] // length
    row = lax.broadcasted_iota(jnp.int32, (16, length), 0)
    for n in range(total_sources):
        column = d_gate[n * capacity : (n + 1) * capacity]
        token = jnp.sum(pick_ref[s, n].astype(F32) * column, 0, keepdims=True)
        for b in range(parts):
            probs_ref[n, :, b * length : (b + 1) * length] += jnp.where(
                row == expert - 16 * b, token, 0.0
            )

    @pl.when(s == slots - 1)
    def _():
        wide = parts * length
        for n in range(total_sources):
            back, k = sides[n // sources][1], n % sources
            at = slice(n * capacity, (n + 1) * capacity)
            pick = jnp.concatenate([pick_ref[i, n] for i in range(slots)], 0)
            d_rows = jnp.concatenate([d_rows_ref[i, at] for i in range(slots)], 0)
            back[k, :length] = dot_tn(pick, d_rows).astype(BF)
            back[k, length:, :wide] = probs_ref[n].astype(BF)
            if wide < width:
                back[k, length:, wide:] = jnp.zeros((16, width - wide), BF)


def experts(ids, ns, pick, dh, gate, up, router, expert_count):
    sources, length, width = ns[0].shape
    slots, _, capacity, _ = pick.shape
    ff = gate.shape[2]
    rows = 2 * sources * capacity
    wide = -(-expert_count // 16) * length
    back = (sources, length + 16, width)
    return pl.pallas_call(
        functools.partial(experts_kernel, expert_count),
        grid_spec=pltpu.PrefetchScalarGridSpec(
            num_scalar_prefetch=1,
            grid=(slots,),
            in_specs=[
                once(ns[0].shape),
                once(ns[1].shape),
                once(pick.shape),
                per_slot(rows, ff),
                per_slot(width, ff),
                per_slot(width, ff),
                once(router.shape),
            ],
            out_specs=[
                once(back),
                once(back),
                per_slot(rows, ff),
                per_slot(rows, ff),
                per_slot(rows, ff),
                per_slot(rows, width),
                per_slot(rows, LANES),
            ],
            scratch_shapes=[
                pltpu.VMEM((slots, rows, width), BF),
                pltpu.VMEM((2 * sources, 16, wide), F32),
            ],
        ),
        out_shape=[jax.ShapeDtypeStruct(back, BF)] * 2
        + [jax.ShapeDtypeStruct((slots, rows, ff), BF)] * 3
        + [
            jax.ShapeDtypeStruct((slots, rows, width), BF),
            jax.ShapeDtypeStruct((slots, rows, LANES), F32),
        ],
        compiler_params=pltpu.CompilerParams(vmem_limit_bytes=VMEM_LIMIT),
        cost_estimate=pl.CostEstimate(
            flops=int(COST * (8 * slots * rows * width * ff)),
            bytes_accessed=int(COST * (slots * ff * (width * 4 + rows * 6))),
            transcendentals=slots * rows * ff,
        ),
        name="experts",
    )(ids, *ns, pick, dh, gate, up, router)


def combine_kernel(place, hid_ref, row_gate_ref, pick_ref, down_ref, out_ref, scaled_ref):
    s = pl.program_id(0)
    slots, sources, capacity, length = pick_ref.shape
    result = dot_nn(hid_ref[0], down_ref[0]).astype(BF)
    scaled_ref[s] = (result.astype(F32) * row_gate_ref[0, :, :1]).astype(BF)

    @pl.when(s == slots - 1)
    def _():
        for n in range(sources):
            at = slice(n * capacity, (n + 1) * capacity)
            pick = jnp.concatenate([pick_ref[i, n] for i in range(slots)], 0)
            scaled = jnp.concatenate([scaled_ref[i, at] for i in range(slots)], 0)
            out_ref[place[n]] = dot_tn(pick, scaled).astype(BF)


def combine(place, hid, row_gate, pick, down):
    slots, sources, capacity, length = pick.shape
    _, ff, width = down.shape
    rows = sources * capacity
    return pl.pallas_call(
        combine_kernel,
        grid_spec=pltpu.PrefetchScalarGridSpec(
            num_scalar_prefetch=1,
            grid=(slots,),
            in_specs=[per_slot(rows, ff), per_slot(rows, LANES), once(pick.shape), per_slot(ff, width)],
            out_specs=once((sources, length, width)),
            scratch_shapes=[pltpu.VMEM((slots, rows, width), BF)],
        ),
        out_shape=jax.ShapeDtypeStruct((sources, length, width), BF),
        compiler_params=pltpu.CompilerParams(vmem_limit_bytes=VMEM_LIMIT),
        cost_estimate=pl.CostEstimate(
            flops=int(COST * (4 * slots * rows * width * (ff + length))),
            bytes_accessed=int(COST * (slots * ff * (width * 2 + rows * 2))),
            transcendentals=0,
        ),
        name="combine",
    )(place, hid, row_gate, pick, down)


def routed_grads_kernel(first, mine, x_ref, dg_ref, du_ref, hid_ref, row_gate_ref, dy_ref, *outs):
    send_a, send_b, keep = outs
    d_result = (dy_ref[0].astype(F32) * row_gate_ref[0, :, :1]).astype(BF)
    x = x_ref[0]

    def place(value, size, send, start, kept):
        for q in range(4):
            rel = mine[0] ^ q
            second = jnp.where((rel & (3 ^ first)) == 0, 0, 1)
            for ref, at, there in ((send, start, (rel & first) != 0), (keep, kept, (rel & first) == 0)):

                @pl.when(there)
                def _():
                    for c in range(value.shape[1] // LANES):
                        ref[second, at + c * size : at + (c + 1) * size] = value[
                            q * size : (q + 1) * size, c * LANES : (c + 1) * LANES
                        ].astype(BF)

    width, ff = x.shape[1], dg_ref.shape[2]
    wide, part = width // 4, width // 4 * (ff // LANES)
    place(dot_tn(x, dg_ref[0]), wide, send_a, 0, 0)
    place(dot_tn(x, du_ref[0]), wide, send_a, part, part)
    place(dot_tn(hid_ref[0], d_result), ff // 4, send_b, 0, 2 * part)


def routed_grads(slot, first, mine, x, dg, du, hid, row_gate, dy):
    _, rows, width = dy.shape
    ff = dg.shape[2]
    at = lambda c: pl.BlockSpec((1, rows, c), lambda i, _: (slot, 0, 0))
    part = width * ff // 4 // LANES
    shapes = [(2, n * part, LANES) for n in (2, 1, 3)]
    return pl.pallas_call(
        functools.partial(routed_grads_kernel, first),
        grid_spec=pltpu.PrefetchScalarGridSpec(
            num_scalar_prefetch=1,
            grid=(1,),
            in_specs=[at(width), at(ff), at(ff), at(ff), at(LANES), at(width)],
            out_specs=[whole(shape) for shape in shapes],
        ),
        out_shape=[jax.ShapeDtypeStruct(shape, BF) for shape in shapes],
        compiler_params=pltpu.CompilerParams(vmem_limit_bytes=VMEM_LIMIT),
        cost_estimate=pl.CostEstimate(
            flops=int(COST * (12 * rows * width * ff)),
            bytes_accessed=int(COST * (6 * width * ff + 8 * rows * width)),
            transcendentals=0,
        ),
        name="routed_grads",
    )(mine, x, dg, du, hid, row_gate, dy)


def finish_kernel(slots, *refs):
    outs = refs[4 * slots :]
    for s in range(slots):
        keep, got_a, got_b, last = refs[4 * s : 4 * s + 4]

        @pl.when(pl.program_id(0) == s)
        def _():
            start = 0
            for i, out in enumerate(outs):
                size, columns = out.shape[1:]
                for c in range(columns // LANES):
                    at = slice(start, start + size)
                    skip = got_a.shape[1]
                    got = got_a[0, at] if i < 2 else got_b[0, start - skip : start - skip + size]
                    kept = (keep[0, at].astype(F32) + got.astype(F32)).astype(BF)
                    out[0, :, c * LANES : (c + 1) * LANES] = kept.astype(F32) + last[at].astype(F32)
                    start += size


def finish(pieces, shapes):
    slots = len(pieces)
    front = lambda v: pl.BlockSpec((1,) + v.shape[1:], lambda s: (0, 0, 0), pipeline_mode=pl.Buffered(1))
    return pl.pallas_call(
        functools.partial(finish_kernel, slots),
        grid=(slots,),
        in_specs=[front(v) if v.ndim == 3 else once(v.shape) for piece in pieces for v in piece],
        out_specs=[per_slot(*shape) for shape in shapes],
        out_shape=[jax.ShapeDtypeStruct((slots,) + shape, F32) for shape in shapes],
        compiler_params=pltpu.CompilerParams(vmem_limit_bytes=VMEM_LIMIT),
        name="finish",
    )(*(v for piece in pieces for v in piece))


def rotary(length):
    half = HEAD_DIM // 2
    frequencies = np.exp(np.arange(half, dtype=np.float32) * np.float32(-math.log(10000.0) / half))
    angles = np.arange(length, dtype=np.float32)[:, None] * frequencies.astype(np.float32)[None, :]
    cosine, sine = np.cos(angles), np.sin(angles)
    return (
        np.concatenate([cosine, cosine], 1).astype(np.float32),
        np.concatenate([-sine, sine], 1).astype(np.float32),
    )


def turn(x, cosine, sine):
    return x * cosine + pltpu.roll(x, HEAD_DIM // 2, 1) * sine


def causal_probs(q, k):
    scores = dot_nt(q, k) * (1.0 / math.sqrt(HEAD_DIM))
    row = lax.broadcasted_iota(jnp.int32, scores.shape, 0)
    lane = lax.broadcasted_iota(jnp.int32, scores.shape, 1)
    scores = jnp.where(row >= lane, scores, -1e30)
    terms = jnp.exp(scores - jnp.max(scores, -1, keepdims=True))
    return terms / jnp.sum(terms, -1, keepdims=True)


def unit_of(x):
    scale = lax.rsqrt(jnp.mean(x * x, -1, keepdims=True) + epsilon)
    return x * scale, scale


def attention_kernel(
    x_ref, gain1_ref, gain2_ref, cos_ref, sin_ref, wq_ref, wk_ref, wv_ref, wo_ref,
    q_ref, k_ref, v_ref, att_ref, nf_ref, residual_ref, ns_ref,
):
    i = pl.program_id(0)

    @pl.when(i == 0)
    def _():
        x = x_ref[...].astype(F32)
        nf_ref[...] = (unit_of(x)[0] * gain1_ref[...][None]).astype(BF)
        residual_ref[...] = x

    nf = nf_ref[...]
    q_all, k_all, v_all = dot_nn(nf, wq_ref[...]), dot_nn(nf, wk_ref[...]), dot_nn(nf, wv_ref[...])
    cosine, sine = cos_ref[...], sin_ref[...]
    v_ref[...] = v_all.astype(BF)
    for h in range(q_ref.shape[1] // HEAD_DIM):
        at = slice(h * HEAD_DIM, (h + 1) * HEAD_DIM)
        q = turn(q_all[:, at], cosine, sine).astype(BF)
        k = turn(k_all[:, at], cosine, sine).astype(BF)
        q_ref[:, at] = q
        k_ref[:, at] = k
        att_ref[:, at] = dot_nn(causal_probs(q, k).astype(BF), v_all[:, at].astype(BF)).astype(BF)
    residual_ref[...] += dot_nn(att_ref[...], wo_ref[...])

    @pl.when(i == pl.num_programs(0) - 1)
    def _():
        ns_ref[...] = (unit_of(residual_ref[...])[0] * gain2_ref[...][None]).astype(BF)


def attention(x, gain1, gain2, cosine, sine, wq, wk, wv, wo):
    length, width = x.shape
    step = 2 * HEAD_DIM
    columns = lambda rows: pl.BlockSpec((rows, step), lambda i: (0, i))
    low = jax.ShapeDtypeStruct((length, width), BF)
    return pl.pallas_call(
        attention_kernel,
        grid=(width // step,),
        in_specs=[
            whole((length, width)),
            whole((width,)),
            whole((width,)),
            whole(cosine.shape),
            whole(sine.shape),
            columns(width),
            columns(width),
            columns(width),
            pl.BlockSpec((step, width), lambda i: (i, 0)),
        ],
        out_specs=[columns(length)] * 4 + [whole((length, width))] * 3,
        out_shape=[low] * 5 + [jax.ShapeDtypeStruct((length, width), F32), low],
        compiler_params=pltpu.CompilerParams(vmem_limit_bytes=VMEM_LIMIT),
        cost_estimate=pl.CostEstimate(
            flops=int(COST * 8 * length * width * width), bytes_accessed=int(COST * 8 * width * width), transcendentals=0
        ),
        name="attention",
    )(x, gain1, gain2, cosine, sine, wq, wk, wv, wo)


def backward_kernel(
    expert_count,
    x_ref, dy_ref, residual_ref, ns_ref, shared_ref, router_t_ref, gain1_ref, gain2_ref,
    cos_ref, sin_ref, q_ref, k_ref, v_ref, wq_ref, wk_ref, wv_ref, wo_ref, *refs,
):
    parts = refs[0]
    cat_ref, grad_ref, branch_ref, d_res_ref, acc_ref = refs[1:]
    i = pl.program_id(0)
    length, width = x_ref.shape
    step = wq_ref.shape[1]
    here = pl.multiple_of(i * step, step)
    gains = slice(4 * length, 4 * length + 16)

    @pl.when(i == 0)
    def _():
        back = parts[0, :length].astype(F32)
        tail = parts[0, length:].astype(F32)
        for p in range(1, parts.shape[0]):
            back += parts[p, :length].astype(F32)
            tail += parts[p, length:].astype(F32)
        blocks = router_t_ref.shape[0] // 16
        d_probs = jnp.concatenate([tail[:, b * length : (b + 1) * length] for b in range(blocks)], 0)
        logits = dot_nt(router_t_ref[...], ns_ref[...])
        row = lax.broadcasted_iota(jnp.int32, logits.shape, 0)
        logits = jnp.where(row < expert_count, logits, -1e30)
        terms = jnp.exp(logits - jnp.max(logits, 0, keepdims=True))
        probs = terms / jnp.sum(terms, 0, keepdims=True)
        d_logits = probs * (d_probs - jnp.sum(probs * d_probs, 0, keepdims=True))
        d_logits = jnp.where(row < expert_count, d_logits, 0.0).astype(BF)
        cat_ref[4 * length + 16 :] = jnp.zeros((d_logits.shape[0], width), BF)
        cat_ref[4 * length + 16 :, :length] = d_logits
        d_normed = shared_ref[...] + back + dot_tn(d_logits, router_t_ref[...])
        unit, scale = unit_of(residual_ref[...])
        c = d_normed * gain2_ref[...][None]
        gain_row = jnp.sum(d_normed * unit, 0, keepdims=True)
        which = lax.broadcasted_iota(jnp.int32, (16, width), 0)
        cat_ref[gains] = jnp.where(which == 1, gain_row, 0.0).astype(BF)
        d_res = dy_ref[...].astype(F32) + scale * (c - unit * jnp.mean(c * unit, -1, keepdims=True))
        d_res_ref[...] = d_res
        branch_ref[...] = d_res.astype(BF)
        cat_ref[3 * length : 4 * length] = d_res.astype(BF)
        acc_ref[...] = jnp.zeros_like(acc_ref)

    cosine, sine = cos_ref[...], -sin_ref[...]
    att_scale = 1.0 / math.sqrt(HEAD_DIM)
    d_att_all = dot_nt(branch_ref[...], wo_ref[...]).astype(BF)
    d_q, d_k, d_v = [], [], []
    for h in range(step // HEAD_DIM):
        at = slice(h * HEAD_DIM, (h + 1) * HEAD_DIM)
        q, k, v, d_attended = q_ref[:, at], k_ref[:, at], v_ref[:, at], d_att_all[:, at]
        probs = causal_probs(q, k)
        d_att = dot_nt(d_attended, v)
        d_scores = (probs * (d_att - jnp.sum(probs * d_att, -1, keepdims=True))).astype(BF)
        d_q.append(turn(dot_nn(d_scores, k) * att_scale, cosine, sine).astype(BF))
        d_k.append(turn(dot_tn(d_scores, q) * att_scale, cosine, sine).astype(BF))
        d_v.append(dot_tn(probs.astype(BF), d_attended).astype(BF))
    d_q, d_k, d_v = (jnp.concatenate(v, 1) for v in (d_q, d_k, d_v))
    for n, v in enumerate((d_q, d_k, d_v)):
        cat_ref[n * length : (n + 1) * length, pl.ds(here, step)] = v
    acc_ref[...] += dot_nt(d_q, wq_ref[...]) + dot_nt(d_k, wk_ref[...]) + dot_nt(d_v, wv_ref[...])

    @pl.when(i == pl.num_programs(0) - 1)
    def _():
        unit, scale = unit_of(x_ref[...].astype(F32))
        d_normed = acc_ref[...]
        c = d_normed * gain1_ref[...][None]
        gain_row = jnp.sum(d_normed * unit, 0, keepdims=True)
        which = lax.broadcasted_iota(jnp.int32, (16, width), 0)
        cat_ref[gains] = jnp.where(which == 0, gain_row, cat_ref[gains].astype(F32)).astype(BF)
        grad_ref[...] = d_res_ref[...] + scale * (c - unit * jnp.mean(c * unit, -1, keepdims=True))


def backward(
    x, dy, residual, ns, shared, router_t, gain1, gain2, cosine, sine,
    q, k, v, wq, wk, wv, wo, parts, expert_count,
):
    length, width = x.shape
    step = 2 * HEAD_DIM
    columns = lambda rows: pl.BlockSpec((rows, step), lambda i: (0, i))
    tall = whole((length, width))
    return pl.pallas_call(
        functools.partial(backward_kernel, expert_count),
        grid=(width // step,),
        in_specs=[tall] * 5
        + [whole(router_t.shape), whole((width,)), whole((width,))]
        + [whole(cosine.shape)] * 2
        + [columns(length)] * 3
        + [columns(width)] * 3
        + [pl.BlockSpec((step, width), lambda i: (i, 0))]
        + [whole(parts.shape)],
        out_specs=[
            whole((4 * length + 16 + router_t.shape[0], width)),
            tall,
        ],
        scratch_shapes=[
            pltpu.VMEM((length, width), BF),
            pltpu.VMEM((length, width), F32),
            pltpu.VMEM((length, width), F32),
        ],
        out_shape=[
            jax.ShapeDtypeStruct((4 * length + 16 + router_t.shape[0], width), BF),
            jax.ShapeDtypeStruct((length, width), F32),
        ],
        compiler_params=pltpu.CompilerParams(vmem_limit_bytes=VMEM_LIMIT),
        cost_estimate=pl.CostEstimate(
            flops=int(COST * 8 * length * width * width), bytes_accessed=int(COST * 8 * width * width), transcendentals=0
        ),
        name="backward",
    )(
        x, dy, residual, ns, shared, router_t, gain1, gain2, cosine, sine,
        q, k, v, wq, wk, wv, wo, parts,
    )


def call(kernel, name, outs, *args, flops=1):
    return pl.pallas_call(
        kernel,
        in_specs=[pl.BlockSpec(memory_space=pltpu.VMEM)] * len(args),
        out_specs=[pl.BlockSpec(memory_space=pltpu.VMEM)] * len(outs),
        out_shape=[jax.ShapeDtypeStruct(*o) for o in outs],
        compiler_params=pltpu.CompilerParams(vmem_limit_bytes=VMEM_LIMIT),
        cost_estimate=pl.CostEstimate(flops=flops, bytes_accessed=flops, transcendentals=0),
        name=name,
    )(*args)


def shared_kernel(ns_ref, dy_ref, gate_ref, up_ref, down_ref, cat_ref, result_ref, back_ref):
    ns, dy = ns_ref[...], dy_ref[...]
    width, ff = gate_ref.shape
    g = dot_nn(ns, gate_ref[...])
    u = dot_nn(ns, up_ref[...])
    sig = jax.nn.sigmoid(g)
    act = g * sig
    hid = (act * u).astype(BF)
    dh = dot_nt(dy, down_ref[...])
    dg = (dh * u * sig * (1.0 + g * (1.0 - sig))).astype(BF)
    du = (dh * act).astype(BF)
    result_ref[...] = dot_nn(hid, down_ref[...])
    back_ref[...] = dot_nt(dg, gate_ref[...]) + dot_nt(du, up_ref[...])
    for i, v in enumerate((dg, du, hid)):
        cat_ref[:, i * ff : (i + 1) * ff] = v
    cat_ref[:, 3 * ff : 3 * ff + width] = ns
    cat_ref[:, 3 * ff + width :] = dy


def shared_grads_kernel(ff, width, cat_ref, other_ref, order_d_ref, order_f_ref, su_send, su_keep, sd_send, sd_keep):
    pair = jnp.concatenate([cat_ref[...], other_ref[...]], 0)
    ns_t = dot_nt(order_d_ref[...], pair[:, 3 * ff : 3 * ff + width]).astype(BF)
    hid_t = dot_nt(order_f_ref[...], pair[:, 2 * ff : 3 * ff]).astype(BF)
    su = dot_nn(ns_t, pair[:, : 2 * ff]).astype(BF)
    sd = dot_nn(hid_t, pair[:, 3 * ff + width :]).astype(BF)
    for value, send, keep in ((su, su_send, su_keep), (sd, sd_send, sd_keep)):
        n = send.shape[1]
        for i in range(2):
            send[i] = value[i * n : (i + 1) * n]
            keep[i] = value[(2 + i) * n : (3 + i) * n]


def lefts_kernel(at_ns, mine_ref, other_ref, ns_ref, cat_other_ref, order_a_ref, order_b_ref, a_ref, v_ref, o_ref, r_ref):
    width = ns_ref.shape[1]
    join = lambda *v: jnp.concatenate(v, 0)
    sets = lambda i, j: join(mine_ref[i], other_ref[i], mine_ref[j], other_ref[j])
    a_ref[...] = dot_nt(order_a_ref[...], sets(0, 2)).astype(BF)
    v_ref[...] = dot_nt(order_b_ref[...], sets(0, 3)).astype(BF)
    o_ref[...] = dot_nt(order_b_ref[...], sets(1, 4)).astype(BF)
    ns = join(ns_ref[...], cat_other_ref[:, at_ns : at_ns + width], mine_ref[5], other_ref[5])
    r_ref[...] = dot_nt(order_b_ref[...], ns).astype(BF)


def last_grads_kernel(
    length, mine_ref, other_ref, qx_ref, qxo_ref, by_ref, byo_ref, a_ref, v_ref, o_ref, r_ref, order_b_ref,
    a_send, a_keep, b_send, b_keep,
):
    width = mine_ref.shape[1]
    half = a_send.shape[0]
    join = lambda *v: jnp.concatenate(v, 0)

    def put(value, keep, send, columns):
        keep[:, columns] = value[:half].astype(BF)
        send[:, columns] = value[half:].astype(BF)

    for i in range(2):
        at = slice(i * length, (i + 1) * length)
        tokens = join(mine_ref[at], other_ref[at], qx_ref[at], qxo_ref[at])
        put(dot_nn(a_ref[...], tokens), a_keep, a_send, slice(i * width, (i + 1) * width))
        past = slice((2 + i) * length, (3 + i) * length)
        tokens = join(mine_ref[past], other_ref[past], by_ref[at], byo_ref[at])
        left = (v_ref, o_ref)[i]
        put(dot_nn(left[...], tokens), b_keep, b_send, slice(i * width, (i + 1) * width))
    start = 4 * length
    refs = ((mine_ref, start), (other_ref, start), (by_ref, start - 2 * length), (byo_ref, start - 2 * length))
    gains = sum(ref[i : i + 16].astype(F32) for ref, i in refs).astype(BF)
    logits = jnp.concatenate([ref[i + 16 :, :length] for ref, i in refs], 1)
    small = jnp.concatenate(
        [dot_nt(r_ref[...], logits), dot_nt(order_b_ref[...], gains)], 1
    )
    small = jnp.concatenate([small, jnp.zeros((2 * half, LANES - small.shape[1]), F32)], 1)
    put(small, b_keep, b_send, slice(2 * width, 2 * width + LANES))


def after(value, *earlier):
    return lax.optimization_barrier((value, earlier))[0]


def shards(
    tokens,
    cotangent,
    routes,
    expert_at,
    norm1_gain,
    w_query,
    w_key,
    w_value,
    w_out,
    norm2_gain,
    w_router,
    shared_gate,
    shared_up,
    shared_down,
    routed_gate,
    routed_up,
    routed_down,
):
    length, model_width = tokens.shape
    expert_count = w_router.shape[1]
    slot_dev = routed_gate.shape[0]
    n_ex = lax.axis_size("expert")
    n_dp = lax.axis_size("dp")
    capacity = (length * TOP * 5 // (4 * expert_count) + 7) // 8 * 8
    my_dp, my_ex = lax.axis_index("dp"), lax.axis_index("expert")
    n_z = n_ex // 2
    w = model_width
    rows = w // (n_dp * n_ex)
    over_core = lambda v: partner(v, "expert", 1)
    order_d = rows_for(w, (1, 3, 0, 2))
    order_a, order_b = rows_for(w, (0, 2)), rows_for(w, (0, 1))

    routes_t = jnp.pad(routes.T.astype(BF), ((0, 16 - TOP), (0, 0)), constant_values=-1)
    routes_t = jnp.pad(routes_t, ((0, 0), (0, w - length)))
    early = jnp.concatenate([cotangent, routes_t], 0)
    early = exchange_z(jnp.broadcast_to(early[None], (n_z,) + early.shape))
    early_other = over_core(early)
    cosine, sine = (jnp.asarray(t) for t in rotary(length))
    gain1, gain2 = norm1_gain, norm2_gain
    queries, key_rows, value_rows, attended, normed_first, residual, normed_second = attention(
        tokens, gain1, gain2, cosine, sine, w_query, w_key, w_value, w_out
    )
    ff = shared_gate.shape[1]
    from_shared, shared_result, shared_back = call(
        shared_kernel, "shared",
        [((length, 3 * ff + 2 * w), BF), ((length, w), F32), ((length, w), F32)],
        after(normed_second, early), cotangent, shared_gate, shared_up, shared_down,
    )
    my_z, my_core = my_ex // 2, my_ex % 2
    first_x = partner(normed_first, "dp", 1)
    first_y = partner(jnp.stack([normed_first, attended, normed_second]), "dp", 2)
    ns = gather_z(normed_second)
    ns = jnp.stack(ns)
    ns = jnp.concatenate([lax.dynamic_slice_in_dim(ns, (my_z - z) % n_z, 1) for z in range(n_z)])

    from_other = over_core(from_shared)
    part_d, part_f = w // (2 * n_dp), ff // (2 * n_dp)
    su_send, su_keep, sd_send, sd_keep = call(
        functools.partial(shared_grads_kernel, ff, w), "shared_grads",
        [((2, part_d, 2 * ff), BF)] * 2 + [((2, part_f, w), BF)] * 2,
        from_shared, from_other, order_d, rows_for(ff, (2, 3, 0, 1)),
    )
    su_got, sd_got = partner(su_send, "dp", 1), partner(sd_send, "dp", 2)

    my_expert = lax.dynamic_slice_in_dim(expert_at, my_ex * slot_dev, slot_dev)
    router_wide = jnp.pad(w_router, ((0, 0), (0, LANES - expert_count)))
    pick, dh_raw, dy_rows = prepare(my_expert, (early, early_other), routed_down, capacity)
    ns = after(ns, pick, dh_raw, su_send, first_x, first_y)
    ns_other = over_core(ns)
    back_mine, back_other, hid, dg, du, x_rows, row_gate = experts(
        my_expert, (ns, ns_other), pick, dh_raw, routed_gate, routed_up, router_wide, expert_count
    )
    back_sum = plus(back_mine, over_core(back_other))
    dg = after(dg, back_sum)
    back = exchange_z(back_sum)

    lefts = jnp.concatenate([normed_first[None], attended[None], first_x[None], first_y])
    lefts_other = over_core(lefts)
    left_shape = ((w // 4, 4 * length), BF)
    left_a, left_v, left_o, left_r = call(
        functools.partial(lefts_kernel, 3 * ff), "lefts", [left_shape] * 4,
        lefts, lefts_other, normed_second, from_other, order_a, order_b,
    )
    keeps, gots, waiting = [], [], []
    for slot in range(slot_dev):
        first = 1 if slot % 2 == 0 else 2
        send_a, send_b, keep = routed_grads(
            slot, first, my_dp[None], x_rows, dg, du, hid, row_gate, dy_rows
        )
        keeps.append(keep)
        waiting.append(send_b)
        gots.append([partner(send_a, "dp", first)])

    back = after(back, left_a, waiting)
    high = -(-expert_count // 16) * 16
    router_t = jnp.pad(w_router.T, ((0, high - expert_count), (0, 0)))
    d_cat, grad_inputs = backward(
        tokens, cotangent, residual, normed_second, shared_back, router_t, gain1, gain2, cosine, sine,
        queries, key_rows, value_rows, w_query, w_key, w_value, w_out, back, expert_count,
    )

    cat_other = over_core(d_cat)
    qk_x, b_y = partner(d_cat[: 2 * length], "dp", 1), partner(d_cat[2 * length :], "dp", 2)
    place = np.arange(n_z, dtype=np.int32) * 2
    place = jnp.concatenate([place + my_core, place + 1 - my_core])
    combined = combine(place, after(hid, d_cat), row_gate, pick, routed_down)
    combined = lax.psum_scatter(combined, "expert", scatter_dimension=0, tiled=False)
    qk_x_other, b_y_other = over_core(qk_x), over_core(b_y)
    waiting = after(waiting, gots, qk_x, b_y)
    for slot in range(slot_dev):
        gots[slot].append(partner(waiting[slot], "dp", 1 if slot % 2 == 0 else 2))
    a_send, a_keep, b_send, b_keep = call(
        functools.partial(last_grads_kernel, length), "last_grads",
        [((w // 8, 2 * w), BF)] * 2 + [((w // 8, 2 * w + LANES), BF)] * 2,
        d_cat, cat_other, qk_x, qk_x_other, b_y, b_y_other, left_a, left_v, left_o, left_r, order_b,
    )
    part_a, part_b = plus(a_keep, partner(a_send, "dp", 2)), plus(b_keep, partner(b_send, "dp", 1))
    last = jnp.concatenate([part_a, part_b], -1).reshape(n_z, rows, -1)

    gots, su_got, sd_got, combined = after((gots, su_got, sd_got, combined), last)
    output = (residual + shared_result + combined.astype(F32)).astype(BF)
    pieces = []
    for slot, (keep, (got_a, got_b)) in enumerate(zip(keeps, gots)):
        there = plus(keep[1], jnp.concatenate([got_a[1], got_b[1]]))
        pieces.append((keep, got_a, got_b, partner(there, "dp", 2 if slot % 2 == 0 else 1)))
    grad_rgate, grad_rup, grad_rdown = finish(pieces, [(w // n_dp, ff), (w // n_dp, ff), (ff // n_dp, w)])
    su, sd = plus(su_keep, su_got), plus(sd_keep, sd_got)
    su, sd = plus(su[0], partner(su[1], "dp", 2)), plus(sd[0], partner(sd[1], "dp", 1))
    sd = jnp.pad(sd.reshape(n_z, -1, w), ((0, 0), (0, (w - ff) // (n_dp * n_ex)), (0, 0)))
    grad_shared = reduce_here(jnp.concatenate([su.reshape(n_z, rows, -1), sd], -1))
    last = reduce_here(last)
    return (
        output,
        grad_inputs,
        last[:, 4 * w + high],
        last[:, :w],
        last[:, w : 2 * w],
        last[:, 2 * w : 3 * w],
        last[:, 3 * w : 4 * w],
        last[:, 4 * w + high + 1],
        last[:, 4 * w : 4 * w + expert_count],
        grad_shared[:, :ff],
        grad_shared[:, ff : 2 * ff],
        grad_shared[: ff // (n_dp * n_ex), 2 * ff :],
        grad_rgate,
        grad_rup,
        grad_rdown,
    )


def solution(mesh):
    placed = (
        P(("dp", "expert"), None),
        P(("dp", "expert"), None),
        P(("dp", "expert"), None),
        P(),
        P(),
        P(),
        P(),
        P(),
        P(),
        P(),
        P(),
        P(),
        P(),
        P(),
        P("expert", None, None),
        P("expert", None, None),
        P("expert", None, None),
    )
    return jax.shard_map(
        shards,
        mesh=mesh,
        in_specs=placed,
        out_specs=(
            P(("dp", "expert"), None),
            P(("dp", "expert"), None),
            P(("dp", "expert")),
            P(("dp", "expert"), None),
            P(("dp", "expert"), None),
            P(("dp", "expert"), None),
            P(("dp", "expert"), None),
            P(("dp", "expert")),
            P(("dp", "expert"), None),
            P(("dp", "expert"), None),
            P(("dp", "expert"), None),
            P(("dp", "expert"), None),
            P("expert", "dp", None),
            P("expert", "dp", None),
            P("expert", "dp", None),
        ),
        check_vma=False,
    )
```

```python
import functools
import math

import jax
import jax.numpy as jnp
import numpy as np
from jax import lax
from jax.experimental import pallas as pl
from jax.experimental.pallas import tpu as pltpu
from jax.sharding import PartitionSpec as P

HEADS = 10
HEAD_DIM = 128
TOP = 6
LANES = 128
epsilon = 1e-06
BF = jnp.bfloat16
F32 = jnp.float32
VMEM_LIMIT = 60 * 2**20
COST = 1


def partner(v, axis, mask):
    n = lax.axis_size(axis)
    return lax.ppermute(v, axis, [(i, i ^ mask) for i in range(n)])


def plus(a, b):
    return (a.astype(F32) + b.astype(F32)).astype(BF)


def exchange_z(s):
    n_z = lax.axis_size("expert") // 2
    groups = [[2 * z + c for z in range(n_z)] for c in (0, 1)]
    return lax.all_to_all(s, "expert", 0, 0, tiled=True, axis_index_groups=groups)


def total(blocks):
    out = blocks[0].astype(F32)
    for b in blocks[1:]:
        out = out + b.astype(F32)
    return out


def rows_for(d, blocks):
    n_dp, n_ex = lax.axis_size("dp"), lax.axis_size("expert")
    rows = d // (n_dp * n_ex)
    n_z = n_ex // 2
    my_dp, my_core = lax.axis_index("dp"), lax.axis_index("expert") % 2
    at = np.arange(len(blocks) * n_z * rows, dtype=np.int32)
    block_dp = jnp.asarray(np.repeat(np.array(blocks, np.int32), n_z * rows)) ^ my_dp
    block = (block_dp * n_z + jnp.asarray(at // rows % n_z)) * 2 + my_core
    source = block * rows + jnp.asarray(at % rows)
    return (source[:, None] == jnp.arange(d, dtype=jnp.int32)[None, :]).astype(BF)


def dot_nn(a, b):
    return lax.dot_general(a, b, (((1,), (0,)), ((), ())), preferred_element_type=F32)


def dot_nt(a, b):
    return lax.dot_general(a, b, (((1,), (1,)), ((), ())), preferred_element_type=F32)


def dot_tn(a, b):
    return lax.dot_general(a, b, (((0,), (0,)), ((), ())), preferred_element_type=F32)


def picks(routes_t, expert, length, capacity):
    hit = jnp.where(routes_t.astype(F32) == expert.astype(F32), 1.0, 0.0)
    member = jnp.sum(hit, 0, keepdims=True)
    a = lax.broadcasted_iota(jnp.int32, (length, length), 0)
    b = lax.broadcasted_iota(jnp.int32, (length, length), 1)
    earlier = jnp.where(a < b, 1.0, 0.0).astype(BF)
    place = dot_nn(jnp.broadcast_to(member, (16, length)).astype(BF), earlier)[:1]
    row = lax.broadcasted_iota(jnp.int32, (capacity, length), 0).astype(F32)
    return jnp.where((place == row) & (member > 0.5), 1.0, 0.0).astype(BF)


def gates_of(x, router, expert, expert_count):
    logits = dot_nn(x, router)
    lane = lax.broadcasted_iota(jnp.int32, logits.shape, 1)
    logits = jnp.where(lane < expert_count, logits, -1e30)
    terms = jnp.exp(logits - jnp.max(logits, -1, keepdims=True))
    probs = terms / jnp.sum(terms, -1, keepdims=True)
    return jnp.sum(jnp.where(lane == expert, probs, 0.0), -1, keepdims=True)


def whole(shape):
    return pl.BlockSpec(shape, lambda *_: (0,) * len(shape))


def prepare_kernel(ids, early_ref, other_ref, down_ref, pick_ref, dh_ref, dy_ref):
    expert = ids[pl.program_id(0)]
    sources = early_ref.shape[0]
    capacity, length = pick_ref.shape[2:]
    for j, ref in enumerate((early_ref, other_ref)):
        for k in range(sources):
            n = j * sources + k
            pick = picks(ref[k, length : length + 16, :length], expert, length, capacity)
            pick_ref[0, n] = pick
            dy_ref[0, n * capacity : (n + 1) * capacity] = dot_nn(pick, ref[k, :length]).astype(BF)
    dh_ref[0] = dot_nt(dy_ref[0], down_ref[0])


def per_slot(*shape):
    return pl.BlockSpec((1,) + shape, lambda s, *_: (s,) + (0,) * len(shape))


def once(shape):
    return pl.BlockSpec(shape, lambda *_: (0,) * len(shape), pipeline_mode=pl.Buffered(1))


def prepare(ids, early, down, capacity):
    sources, length = early[0].shape[0], early[0].shape[1] - 16
    slots, ff, width = down.shape
    rows = 2 * sources * capacity
    return pl.pallas_call(
        prepare_kernel,
        grid_spec=pltpu.PrefetchScalarGridSpec(
            num_scalar_prefetch=1,
            grid=(slots,),
            in_specs=[once(v.shape) for v in early] + [per_slot(ff, width)],
            out_specs=[
                per_slot(2 * sources, capacity, length),
                per_slot(rows, ff),
                per_slot(rows, width),
            ],
        ),
        out_shape=[
            jax.ShapeDtypeStruct((slots, 2 * sources, capacity, length), BF),
            jax.ShapeDtypeStruct((slots, rows, ff), F32),
            jax.ShapeDtypeStruct((slots, rows, width), BF),
        ],
        compiler_params=pltpu.CompilerParams(vmem_limit_bytes=VMEM_LIMIT),
        cost_estimate=pl.CostEstimate(
            flops=1,
            bytes_accessed=1,
            transcendentals=0,
        ),
        name="prepare",
    )(ids, *early, down)


def experts_kernel(
    expert_count, ids, ns0_ref, ns1_ref, pick_ref, dh_ref, gate_ref, up_ref, router_ref,
    back0_ref, back1_ref, hid_ref, dg_ref, du_ref, rows_ref, row_gate_ref, d_rows_ref, probs_ref,
):
    s = pl.program_id(0)
    slots, total_sources, capacity, length = pick_ref.shape
    sources, _, width = ns0_ref.shape
    expert = ids[s]
    sides = [(ns0_ref, back0_ref), (ns1_ref, back1_ref)]
    for n in range(total_sources):
        ns = sides[n // sources][0][n % sources]
        rows_ref[0, n * capacity : (n + 1) * capacity] = dot_nn(pick_ref[s, n], ns).astype(BF)
    x = rows_ref[0]
    row_gate = gates_of(x, router_ref[...], expert, expert_count)
    row_gate_ref[0] = jnp.broadcast_to(row_gate, row_gate_ref.shape[1:])
    g = dot_nn(x, gate_ref[0])
    u = dot_nn(x, up_ref[0])
    sig = jax.nn.sigmoid(g)
    act = g * sig
    hid = (act * u).astype(BF)
    hid_ref[0] = hid
    raw = dh_ref[0]
    d_gate = jnp.sum(hid.astype(F32) * raw, -1, keepdims=True)
    dh = raw * row_gate
    dg = (dh * u * sig * (1.0 + g * (1.0 - sig))).astype(BF)
    du = (dh * act).astype(BF)
    dg_ref[0] = dg
    du_ref[0] = du
    d_rows_ref[s] = (dot_nt(dg, gate_ref[0]) + dot_nt(du, up_ref[0])).astype(BF)

    @pl.when(s == 0)
    def _():
        probs_ref[...] = jnp.zeros_like(probs_ref)

    parts = probs_ref.shape[2] // length
    row = lax.broadcasted_iota(jnp.int32, (16, length), 0)
    for n in range(total_sources):
        column = d_gate[n * capacity : (n + 1) * capacity]
        token = jnp.sum(pick_ref[s, n].astype(F32) * column, 0, keepdims=True)
        for b in range(parts):
            probs_ref[n, :, b * length : (b + 1) * length] += jnp.where(
                row == expert - 16 * b, token, 0.0
            )

    @pl.when(s == slots - 1)
    def _():
        wide = parts * length
        for n in range(total_sources):
            back, k = sides[n // sources][1], n % sources
            at = slice(n * capacity, (n + 1) * capacity)
            pick = jnp.concatenate([pick_ref[i, n] for i in range(slots)], 0)
            d_rows = jnp.concatenate([d_rows_ref[i, at] for i in range(slots)], 0)
            back[k, :length] = dot_tn(pick, d_rows).astype(BF)
            back[k, length:, :wide] = probs_ref[n].astype(BF)
            if wide < width:
                back[k, length:, wide:] = jnp.zeros((16, width - wide), BF)


def experts(ids, ns, pick, dh, gate, up, router, expert_count):
    sources, length, width = ns[0].shape
    slots, _, capacity, _ = pick.shape
    ff = gate.shape[2]
    rows = 2 * sources * capacity
    wide = -(-expert_count // 16) * length
    back = (sources, length + 16, width)
    return pl.pallas_call(
        functools.partial(experts_kernel, expert_count),
        grid_spec=pltpu.PrefetchScalarGridSpec(
            num_scalar_prefetch=1,
            grid=(slots,),
            in_specs=[
                once(ns[0].shape),
                once(ns[1].shape),
                once(pick.shape),
                per_slot(rows, ff),
                per_slot(width, ff),
                per_slot(width, ff),
                once(router.shape),
            ],
            out_specs=[
                once(back),
                once(back),
                per_slot(rows, ff),
                per_slot(rows, ff),
                per_slot(rows, ff),
                per_slot(rows, width),
                per_slot(rows, LANES),
            ],
            scratch_shapes=[
                pltpu.VMEM((slots, rows, width), BF),
                pltpu.VMEM((2 * sources, 16, wide), F32),
            ],
        ),
        out_shape=[jax.ShapeDtypeStruct(back, BF)] * 2
        + [jax.ShapeDtypeStruct((slots, rows, ff), BF)] * 3
        + [
            jax.ShapeDtypeStruct((slots, rows, width), BF),
            jax.ShapeDtypeStruct((slots, rows, LANES), F32),
        ],
        compiler_params=pltpu.CompilerParams(vmem_limit_bytes=VMEM_LIMIT),
        cost_estimate=pl.CostEstimate(
            flops=int(COST * (8 * slots * rows * width * ff)),
            bytes_accessed=int(COST * (slots * ff * (width * 4 + rows * 6))),
            transcendentals=slots * rows * ff,
        ),
        name="experts",
    )(ids, *ns, pick, dh, gate, up, router)


def combine_kernel(place, hid_ref, row_gate_ref, pick_ref, down_ref, out_ref, scaled_ref):
    s = pl.program_id(0)
    slots, sources, capacity, length = pick_ref.shape
    result = dot_nn(hid_ref[0], down_ref[0]).astype(BF)
    scaled_ref[s] = (result.astype(F32) * row_gate_ref[0, :, :1]).astype(BF)

    @pl.when(s == slots - 1)
    def _():
        for n in range(sources):
            at = slice(n * capacity, (n + 1) * capacity)
            pick = jnp.concatenate([pick_ref[i, n] for i in range(slots)], 0)
            scaled = jnp.concatenate([scaled_ref[i, at] for i in range(slots)], 0)
            out_ref[place[n]] = dot_tn(pick, scaled).astype(BF)


def combine(place, hid, row_gate, pick, down):
    slots, sources, capacity, length = pick.shape
    _, ff, width = down.shape
    rows = sources * capacity
    return pl.pallas_call(
        combine_kernel,
        grid_spec=pltpu.PrefetchScalarGridSpec(
            num_scalar_prefetch=1,
            grid=(slots,),
            in_specs=[per_slot(rows, ff), per_slot(rows, LANES), once(pick.shape), per_slot(ff, width)],
            out_specs=once((sources, length, width)),
            scratch_shapes=[pltpu.VMEM((slots, rows, width), BF)],
        ),
        out_shape=jax.ShapeDtypeStruct((sources, length, width), BF),
        compiler_params=pltpu.CompilerParams(vmem_limit_bytes=VMEM_LIMIT),
        cost_estimate=pl.CostEstimate(
            flops=int(COST * (4 * slots * rows * width * (ff + length))),
            bytes_accessed=int(COST * (slots * ff * (width * 2 + rows * 2))),
            transcendentals=0,
        ),
        name="combine",
    )(place, hid, row_gate, pick, down)


def routed_grads_kernel(
    expert_count, slot, ids, x_ref, dg_ref, du_ref, hid_ref, row_gate_ref, dy_ref, ns0_ref, ns1_ref, early0_ref, early1_ref,
    gate_ref, up_ref, down_ref, router_ref, sel_d_ref, sel_f_ref, send_ref, keep_ref, far_x, far_dy,
):
    expert = ids[slot]
    sources, length, width = ns0_ref.shape
    rows = far_x.shape[0]
    capacity = rows // (2 * sources)
    for j, (ns, early) in enumerate(((ns0_ref, early0_ref), (ns1_ref, early1_ref))):
        for k in range(sources):
            pick = picks(early[k, length:, :length], expert, length, capacity)
            at = slice((j * sources + k) * capacity, (j * sources + k + 1) * capacity)
            far_x[at] = dot_nn(pick, ns[k]).astype(BF)
            far_dy[at] = dot_nn(pick, early[k, :length]).astype(BF)
    x = far_x[...]
    row_gate = gates_of(x, router_ref[...], expert, expert_count)
    d_far = (far_dy[...].astype(F32) * row_gate).astype(BF)
    g = dot_nn(x, gate_ref[0])
    u = dot_nn(x, up_ref[0])
    sig = jax.nn.sigmoid(g)
    act = g * sig
    hid = (act * u).astype(BF)
    dh = dot_nt(d_far, down_ref[0])
    dg = (dh * u * sig * (1.0 + g * (1.0 - sig))).astype(BF)
    du = (dh * act).astype(BF)
    x_t = dot_nt(sel_d_ref[...], x).astype(BF)
    x_own = dot_nt(sel_d_ref[...], x_ref[0]).astype(BF)
    hid_t = dot_nt(sel_f_ref[...], hid).astype(BF)
    hid_own = dot_nt(sel_f_ref[...], hid_ref[0]).astype(BF)
    d_own = (dy_ref[0].astype(F32) * row_gate_ref[0, :, :1]).astype(BF)
    start = 0
    for value in (
        dot_nn(x_own, dg_ref[0]) + dot_nn(x_t, dg),
        dot_nn(x_own, du_ref[0]) + dot_nn(x_t, du),
        dot_nn(hid_own, d_own) + dot_nn(hid_t, d_far),
    ):
        size = value.shape[0] // 2
        for c in range(value.shape[1] // LANES):
            columns = value[:, c * LANES : (c + 1) * LANES].astype(BF)
            send_ref[start : start + size] = columns[:size]
            keep_ref[start : start + size] = columns[size:]
            start += size


def routed_grads(slot, second, ids, own, far, weights, router, expert_count):
    gate, up, down = weights
    _, rows, width = own[0].shape
    ff = gate.shape[2]
    mine = lax.axis_index("dp")

    def selector(size):
        part = size // 4
        i = np.arange(part, dtype=np.int32)
        source = jnp.concatenate([(mine ^ second) * part + i, mine * part + i])
        return (source[:, None] == jnp.arange(size, dtype=jnp.int32)[None, :]).astype(BF)

    at = lambda v: pl.BlockSpec(
        (1,) + v.shape[1:], lambda i, _: (slot, 0, 0), pipeline_mode=pl.Buffered(1)
    )
    shape = (3 * width * ff // 4 // LANES, LANES)
    rest = far + [router, selector(width), selector(ff)]
    rest_specs = [once(v.shape) for v in rest]
    return pl.pallas_call(
        functools.partial(routed_grads_kernel, expert_count, slot),
        grid_spec=pltpu.PrefetchScalarGridSpec(
            num_scalar_prefetch=1,
            grid=(1,),
            in_specs=[at(v) for v in own]
            + rest_specs[: len(far)]
            + [at(v) for v in weights]
            + rest_specs[len(far) :],
            out_specs=[once(shape)] * 2,
            scratch_shapes=[pltpu.VMEM((rows, width), BF)] * 2,
        ),
        out_shape=[jax.ShapeDtypeStruct(shape, BF)] * 2,
        compiler_params=pltpu.CompilerParams(vmem_limit_bytes=VMEM_LIMIT),
        cost_estimate=pl.CostEstimate(
            flops=int(COST * (16 * rows * width * ff)),
            bytes_accessed=int(COST * (12 * width * ff + 16 * rows * width)),
            transcendentals=0,
        ),
        name="routed_grads",
    )(ids, *own, *far, *weights, *rest[len(far) :])


def finish_kernel(slots, *refs):
    outs = refs[2 * slots :]
    for s in range(slots):
        keep, got = refs[2 * s], refs[2 * s + 1]

        @pl.when(pl.program_id(0) == s)
        def _():
            start = 0
            for out in outs:
                size, columns = out.shape[1:]
                for c in range(columns // LANES):
                    at = slice(start, start + size)
                    out[0, :, c * LANES : (c + 1) * LANES] = keep[at].astype(F32) + got[at].astype(F32)
                    start += size


def finish(pieces, shapes):
    slots = len(pieces)
    return pl.pallas_call(
        functools.partial(finish_kernel, slots),
        grid=(slots,),
        in_specs=[once(v.shape) for piece in pieces for v in piece],
        out_specs=[per_slot(*shape) for shape in shapes],
        out_shape=[jax.ShapeDtypeStruct((slots,) + shape, F32) for shape in shapes],
        compiler_params=pltpu.CompilerParams(vmem_limit_bytes=VMEM_LIMIT),
        name="finish",
    )(*(v for piece in pieces for v in piece))


def rotary(length):
    half = HEAD_DIM // 2
    frequencies = np.exp(np.arange(half, dtype=np.float32) * np.float32(-math.log(10000.0) / half))
    angles = np.arange(length, dtype=np.float32)[:, None] * frequencies.astype(np.float32)[None, :]
    cosine, sine = np.cos(angles), np.sin(angles)
    return (
        np.concatenate([cosine, cosine], 1).astype(np.float32),
        np.concatenate([-sine, sine], 1).astype(np.float32),
    )


def turn(x, cosine, sine):
    return x * cosine + pltpu.roll(x, HEAD_DIM // 2, 1) * sine


def causal_probs(q, k):
    scores = dot_nt(q, k) * (1.0 / math.sqrt(HEAD_DIM))
    row = lax.broadcasted_iota(jnp.int32, scores.shape, 0)
    lane = lax.broadcasted_iota(jnp.int32, scores.shape, 1)
    scores = jnp.where(row >= lane, scores, -1e30)
    terms = jnp.exp(scores - jnp.max(scores, -1, keepdims=True))
    return terms / jnp.sum(terms, -1, keepdims=True)


def unit_of(x):
    scale = lax.rsqrt(jnp.mean(x * x, -1, keepdims=True) + epsilon)
    return x * scale, scale


def attention_kernel(
    x_ref, gain1_ref, gain2_ref, cos_ref, sin_ref, wq_ref, wk_ref, wv_ref, wo_ref,
    q_ref, k_ref, v_ref, att_ref, nf_ref, residual_ref, ns_ref,
):
    i = pl.program_id(0)

    @pl.when(i == 0)
    def _():
        x = x_ref[...].astype(F32)
        nf_ref[...] = (unit_of(x)[0] * gain1_ref[...][None]).astype(BF)
        residual_ref[...] = x

    nf = nf_ref[...]
    q_all, k_all, v_all = dot_nn(nf, wq_ref[...]), dot_nn(nf, wk_ref[...]), dot_nn(nf, wv_ref[...])
    cosine, sine = cos_ref[...], sin_ref[...]
    v_ref[...] = v_all.astype(BF)
    for h in range(q_ref.shape[1] // HEAD_DIM):
        at = slice(h * HEAD_DIM, (h + 1) * HEAD_DIM)
        q = turn(q_all[:, at], cosine, sine).astype(BF)
        k = turn(k_all[:, at], cosine, sine).astype(BF)
        q_ref[:, at] = q
        k_ref[:, at] = k
        att_ref[:, at] = dot_nn(causal_probs(q, k).astype(BF), v_all[:, at].astype(BF)).astype(BF)
    residual_ref[...] += dot_nn(att_ref[...], wo_ref[...])

    @pl.when(i == pl.num_programs(0) - 1)
    def _():
        ns_ref[...] = (unit_of(residual_ref[...])[0] * gain2_ref[...][None]).astype(BF)


def attention(x, gain1, gain2, cosine, sine, wq, wk, wv, wo):
    length, width = x.shape
    step = 2 * HEAD_DIM
    columns = lambda rows: pl.BlockSpec((rows, step), lambda i: (0, i))
    low = jax.ShapeDtypeStruct((length, width), BF)
    return pl.pallas_call(
        attention_kernel,
        grid=(width // step,),
        in_specs=[
            whole((length, width)),
            whole((width,)),
            whole((width,)),
            whole(cosine.shape),
            whole(sine.shape),
            columns(width),
            columns(width),
            columns(width),
            pl.BlockSpec((step, width), lambda i: (i, 0)),
        ],
        out_specs=[columns(length)] * 4 + [whole((length, width))] * 3,
        out_shape=[low] * 5 + [jax.ShapeDtypeStruct((length, width), F32), low],
        compiler_params=pltpu.CompilerParams(vmem_limit_bytes=VMEM_LIMIT),
        cost_estimate=pl.CostEstimate(
            flops=int(COST * 8 * length * width * width), bytes_accessed=int(COST * 8 * width * width), transcendentals=0
        ),
        name="attention",
    )(x, gain1, gain2, cosine, sine, wq, wk, wv, wo)


def backward_kernel(
    expert_count,
    x_ref, dy_ref, residual_ref, ns_ref, shared_ref, router_t_ref, gain1_ref, gain2_ref,
    cos_ref, sin_ref, q_ref, k_ref, v_ref, wq_ref, wk_ref, wv_ref, wo_ref, *refs,
):
    parts = refs[0]
    cat_ref, grad_ref, branch_ref, d_res_ref, acc_ref = refs[1:]
    i = pl.program_id(0)
    length, width = x_ref.shape
    step = wq_ref.shape[1]
    here = pl.multiple_of(i * step, step)
    gains = slice(4 * length, 4 * length + 16)

    @pl.when(i == 0)
    def _():
        back = parts[0, :length].astype(F32)
        tail = parts[0, length:].astype(F32)
        for p in range(1, parts.shape[0]):
            back += parts[p, :length].astype(F32)
            tail += parts[p, length:].astype(F32)
        blocks = router_t_ref.shape[0] // 16
        d_probs = jnp.concatenate([tail[:, b * length : (b + 1) * length] for b in range(blocks)], 0)
        logits = dot_nt(router_t_ref[...], ns_ref[...])
        row = lax.broadcasted_iota(jnp.int32, logits.shape, 0)
        logits = jnp.where(row < expert_count, logits, -1e30)
        terms = jnp.exp(logits - jnp.max(logits, 0, keepdims=True))
        probs = terms / jnp.sum(terms, 0, keepdims=True)
        d_logits = probs * (d_probs - jnp.sum(probs * d_probs, 0, keepdims=True))
        d_logits = jnp.where(row < expert_count, d_logits, 0.0).astype(BF)
        cat_ref[4 * length + 16 :] = jnp.zeros((d_logits.shape[0], width), BF)
        cat_ref[4 * length + 16 :, :length] = d_logits
        d_normed = shared_ref[...] + back + dot_tn(d_logits, router_t_ref[...])
        unit, scale = unit_of(residual_ref[...])
        c = d_normed * gain2_ref[...][None]
        gain_row = jnp.sum(d_normed * unit, 0, keepdims=True)
        which = lax.broadcasted_iota(jnp.int32, (16, width), 0)
        cat_ref[gains] = jnp.where(which == 1, gain_row, 0.0).astype(BF)
        d_res = dy_ref[...].astype(F32) + scale * (c - unit * jnp.mean(c * unit, -1, keepdims=True))
        d_res_ref[...] = d_res
        branch_ref[...] = d_res.astype(BF)
        cat_ref[3 * length : 4 * length] = d_res.astype(BF)
        acc_ref[...] = jnp.zeros_like(acc_ref)

    cosine, sine = cos_ref[...], -sin_ref[...]
    att_scale = 1.0 / math.sqrt(HEAD_DIM)
    d_att_all = dot_nt(branch_ref[...], wo_ref[...]).astype(BF)
    d_q, d_k, d_v = [], [], []
    for h in range(step // HEAD_DIM):
        at = slice(h * HEAD_DIM, (h + 1) * HEAD_DIM)
        q, k, v, d_attended = q_ref[:, at], k_ref[:, at], v_ref[:, at], d_att_all[:, at]
        probs = causal_probs(q, k)
        d_att = dot_nt(d_attended, v)
        d_scores = (probs * (d_att - jnp.sum(probs * d_att, -1, keepdims=True))).astype(BF)
        d_q.append(turn(dot_nn(d_scores, k) * att_scale, cosine, sine).astype(BF))
        d_k.append(turn(dot_tn(d_scores, q) * att_scale, cosine, sine).astype(BF))
        d_v.append(dot_tn(probs.astype(BF), d_attended).astype(BF))
    d_q, d_k, d_v = (jnp.concatenate(v, 1) for v in (d_q, d_k, d_v))
    for n, v in enumerate((d_q, d_k, d_v)):
        cat_ref[n * length : (n + 1) * length, pl.ds(here, step)] = v
    acc_ref[...] += dot_nt(d_q, wq_ref[...]) + dot_nt(d_k, wk_ref[...]) + dot_nt(d_v, wv_ref[...])

    @pl.when(i == pl.num_programs(0) - 1)
    def _():
        unit, scale = unit_of(x_ref[...].astype(F32))
        d_normed = acc_ref[...]
        c = d_normed * gain1_ref[...][None]
        gain_row = jnp.sum(d_normed * unit, 0, keepdims=True)
        which = lax.broadcasted_iota(jnp.int32, (16, width), 0)
        cat_ref[gains] = jnp.where(which == 0, gain_row, cat_ref[gains].astype(F32)).astype(BF)
        grad_ref[...] = d_res_ref[...] + scale * (c - unit * jnp.mean(c * unit, -1, keepdims=True))


def backward(
    x, dy, residual, ns, shared, router_t, gain1, gain2, cosine, sine,
    q, k, v, wq, wk, wv, wo, parts, expert_count,
):
    length, width = x.shape
    step = 2 * HEAD_DIM
    columns = lambda rows: pl.BlockSpec((rows, step), lambda i: (0, i))
    tall = whole((length, width))
    return pl.pallas_call(
        functools.partial(backward_kernel, expert_count),
        grid=(width // step,),
        in_specs=[tall] * 5
        + [whole(router_t.shape), whole((width,)), whole((width,))]
        + [whole(cosine.shape)] * 2
        + [columns(length)] * 3
        + [columns(width)] * 3
        + [pl.BlockSpec((step, width), lambda i: (i, 0))]
        + [whole(parts.shape)],
        out_specs=[
            whole((4 * length + 16 + router_t.shape[0], width)),
            tall,
        ],
        scratch_shapes=[
            pltpu.VMEM((length, width), BF),
            pltpu.VMEM((length, width), F32),
            pltpu.VMEM((length, width), F32),
        ],
        out_shape=[
            jax.ShapeDtypeStruct((4 * length + 16 + router_t.shape[0], width), BF),
            jax.ShapeDtypeStruct((length, width), F32),
        ],
        compiler_params=pltpu.CompilerParams(vmem_limit_bytes=VMEM_LIMIT),
        cost_estimate=pl.CostEstimate(
            flops=int(COST * 8 * length * width * width), bytes_accessed=int(COST * 8 * width * width), transcendentals=0
        ),
        name="backward",
    )(
        x, dy, residual, ns, shared, router_t, gain1, gain2, cosine, sine,
        q, k, v, wq, wk, wv, wo, parts,
    )


def call(kernel, name, outs, *args, flops=1):
    return pl.pallas_call(
        kernel,
        in_specs=[pl.BlockSpec(memory_space=pltpu.VMEM)] * len(args),
        out_specs=[pl.BlockSpec(memory_space=pltpu.VMEM)] * len(outs),
        out_shape=[jax.ShapeDtypeStruct(*o) for o in outs],
        compiler_params=pltpu.CompilerParams(vmem_limit_bytes=VMEM_LIMIT),
        cost_estimate=pl.CostEstimate(flops=flops, bytes_accessed=flops, transcendentals=0),
        name=name,
    )(*args)


def shared_kernel(ns_ref, dy_ref, gate_ref, up_ref, down_ref, cat_ref, result_ref, back_ref):
    ns, dy = ns_ref[...], dy_ref[...]
    width, ff = gate_ref.shape
    g = dot_nn(ns, gate_ref[...])
    u = dot_nn(ns, up_ref[...])
    sig = jax.nn.sigmoid(g)
    act = g * sig
    hid = (act * u).astype(BF)
    dh = dot_nt(dy, down_ref[...])
    dg = (dh * u * sig * (1.0 + g * (1.0 - sig))).astype(BF)
    du = (dh * act).astype(BF)
    result_ref[...] = dot_nn(hid, down_ref[...])
    back_ref[...] = dot_nt(dg, gate_ref[...]) + dot_nt(du, up_ref[...])
    for i, v in enumerate((dg, du, hid)):
        cat_ref[:, i * ff : (i + 1) * ff] = v
    cat_ref[:, 3 * ff : 3 * ff + width] = ns
    cat_ref[:, 3 * ff + width :] = dy


def shared_grads_kernel(ff, width, cat_ref, other_ref, order_d_ref, order_f_ref, su_send, su_keep, sd_send, sd_keep):
    pair = jnp.concatenate([cat_ref[...], other_ref[...]], 0)
    ns_t = dot_nt(order_d_ref[...], pair[:, 3 * ff : 3 * ff + width]).astype(BF)
    hid_t = dot_nt(order_f_ref[...], pair[:, 2 * ff : 3 * ff]).astype(BF)
    su = dot_nn(ns_t, pair[:, : 2 * ff]).astype(BF)
    sd = dot_nn(hid_t, pair[:, 3 * ff + width :]).astype(BF)
    for value, send, keep in ((su, su_send, su_keep), (sd, sd_send, sd_keep)):
        n = send.shape[1]
        for i in range(2):
            send[i] = value[i * n : (i + 1) * n]
            keep[i] = value[(2 + i) * n : (3 + i) * n]


def lefts_kernel(mine_ref, other_ref, order_a_ref, order_b_ref, a_ref, v_ref, o_ref):
    sets = lambda i, j: jnp.concatenate([mine_ref[i], other_ref[i], mine_ref[j], other_ref[j]], 0)
    a_ref[...] = dot_nt(order_a_ref[...], sets(0, 2)).astype(BF)
    v_ref[...] = dot_nt(order_b_ref[...], sets(0, 3)).astype(BF)
    o_ref[...] = dot_nt(order_b_ref[...], sets(1, 4)).astype(BF)


def last_grads_kernel(
    length, mine_ref, other_ref, qx_ref, qxo_ref, by_ref, byo_ref, a_ref, v_ref, o_ref, ns_ref, order_b_ref,
    a_send, a_keep, b_send, b_keep,
):
    width = mine_ref.shape[1]
    half = a_send.shape[0]
    join = lambda *v: jnp.concatenate(v, 0)

    def put(value, keep, send, columns):
        keep[:, columns] = value[:half].astype(BF)
        send[:, columns] = value[half:].astype(BF)

    for i in range(2):
        at = slice(i * length, (i + 1) * length)
        tokens = join(mine_ref[at], other_ref[at], qx_ref[at], qxo_ref[at])
        put(dot_nn(a_ref[...], tokens), a_keep, a_send, slice(i * width, (i + 1) * width))
        past = slice((2 + i) * length, (3 + i) * length)
        tokens = join(mine_ref[past], other_ref[past], by_ref[at], byo_ref[at])
        left = (v_ref, o_ref)[i]
        put(dot_nn(left[...], tokens), b_keep, b_send, slice(i * width, (i + 1) * width))
    start = 4 * length
    refs = ((mine_ref, start), (other_ref, start), (by_ref, start - 2 * length), (byo_ref, start - 2 * length))
    gains = sum(ref[i : i + 16].astype(F32) for ref, i in refs).astype(BF)
    logits = jnp.concatenate([ref[i + 16 :, :length] for ref, i in refs], 1)
    left_r = dot_nt(order_b_ref[...], ns_ref[...]).astype(BF)
    small = jnp.concatenate(
        [dot_nt(left_r, logits), dot_nt(order_b_ref[...], gains)], 1
    )
    small = jnp.concatenate([small, jnp.zeros((2 * half, LANES - small.shape[1]), F32)], 1)
    put(small, b_keep, b_send, slice(2 * width, 2 * width + LANES))


def after(value, *earlier):
    return lax.optimization_barrier((value, earlier))[0]


def shards(
    tokens,
    cotangent,
    routes,
    expert_at,
    norm1_gain,
    w_query,
    w_key,
    w_value,
    w_out,
    norm2_gain,
    w_router,
    shared_gate,
    shared_up,
    shared_down,
    routed_gate,
    routed_up,
    routed_down,
):
    length, model_width = tokens.shape
    expert_count = w_router.shape[1]
    slot_dev = routed_gate.shape[0]
    n_ex = lax.axis_size("expert")
    n_dp = lax.axis_size("dp")
    capacity = (length * TOP * 5 // (4 * expert_count) + 7) // 8 * 8
    my_dp, my_ex = lax.axis_index("dp"), lax.axis_index("expert")
    n_z = n_ex // 2
    w = model_width
    rows = w // (n_dp * n_ex)
    over_core = lambda v: partner(v, "expert", 1)
    order_d = rows_for(w, (1, 3, 0, 2))
    order_a, order_b = rows_for(w, (0, 2)), rows_for(w, (0, 1))

    routes_t = jnp.pad(routes.T.astype(BF), ((0, 16 - TOP), (0, 0)), constant_values=-1)
    routes_t = jnp.pad(routes_t, ((0, 0), (0, w - length)))
    spread = lambda v: exchange_z(jnp.broadcast_to(v[None], (n_z,) + v.shape))
    early = spread(jnp.concatenate([cotangent, routes_t], 0))
    cosine, sine = (jnp.asarray(t) for t in rotary(length))
    gain1, gain2 = norm1_gain, norm2_gain
    queries, key_rows, value_rows, attended, normed_first, residual, normed_second = attention(
        tokens, gain1, gain2, cosine, sine, w_query, w_key, w_value, w_out
    )
    ff = shared_gate.shape[1]
    from_shared, shared_result, shared_back = call(
        shared_kernel, "shared",
        [((length, 3 * ff + 2 * w), BF), ((length, w), F32), ((length, w), F32)],
        normed_second, cotangent, shared_gate, shared_up, shared_down,
    )
    my_z, my_core = my_ex // 2, my_ex % 2
    first_x = partner(normed_first, "dp", 1)
    first_y = partner(jnp.stack([normed_first, attended]), "dp", 2)
    ns = spread(after(normed_second, early, from_shared))
    from_other = over_core(from_shared)
    part_d, part_f = w // (2 * n_dp), ff // (2 * n_dp)
    su_send, su_keep, sd_send, sd_keep = call(
        functools.partial(shared_grads_kernel, ff, w), "shared_grads",
        [((2, part_d, 2 * ff), BF)] * 2 + [((2, part_f, w), BF)] * 2,
        from_shared, from_other, order_d, rows_for(ff, (2, 3, 0, 1)),
    )
    su_got, sd_got = partner(su_send, "dp", 1), partner(sd_send, "dp", 2)
    early_other = over_core(early)
    early_x, early_y = partner(early, "dp", 1), partner(early, "dp", 2)

    my_expert = lax.dynamic_slice_in_dim(expert_at, my_ex * slot_dev, slot_dev)
    router_wide = jnp.pad(w_router, ((0, 0), (0, LANES - expert_count)))
    pick, dh_raw, dy_rows = prepare(my_expert, (early, early_other), routed_down, capacity)
    ns = after(ns, pick, dh_raw, early_x, early_y, su_send)
    ns_other = over_core(ns)
    ns_x, ns_y = partner(ns, "dp", 1), partner(ns, "dp", 2)
    back_mine, back_other, hid, dg, du, x_rows, row_gate = experts(
        my_expert, (ns, ns_other), pick, dh_raw, routed_gate, routed_up, router_wide, expert_count
    )
    back_sum = plus(back_mine, over_core(back_other))
    back = exchange_z(back_sum)

    lefts = jnp.concatenate([normed_first[None], attended[None], first_x[None], first_y])
    lefts_other = over_core(lefts)
    left_shape = ((w // 4, 4 * length), BF)
    left_a, left_v, left_o = call(
        lefts_kernel, "lefts", [left_shape] * 3, lefts, lefts_other, order_a, order_b,
    )
    place = np.arange(n_z, dtype=np.int32) * 2
    place = jnp.concatenate([place + my_core, place + 1 - my_core])
    combined_rows = combine(place, after(hid, back_sum), row_gate, pick, routed_down)
    back = after(back, combined_rows, left_a, su_got, sd_got)
    combined = lax.psum_scatter(combined_rows, "expert", scatter_dimension=0, tiled=False)
    high = -(-expert_count // 16) * 16
    router_t = jnp.pad(w_router.T, ((0, high - expert_count), (0, 0)))
    d_cat, grad_inputs = backward(
        tokens, cotangent, residual, normed_second, shared_back, router_t, gain1, gain2, cosine, sine,
        queries, key_rows, value_rows, w_query, w_key, w_value, w_out, back, expert_count,
    )

    d_cat = after(d_cat, ns_x, ns_y)
    cat_other = over_core(d_cat)
    su, sd = plus(su_keep, su_got), plus(sd_keep, sd_got)
    su_last, sd_last = partner(after(su[1], d_cat), "dp", 2), partner(after(sd[1], d_cat), "dp", 1)
    su, sd = plus(su[0], su_last), plus(sd[0], sd_last)
    qk_x, b_y = partner(d_cat[: 2 * length], "dp", 1), partner(d_cat[2 * length :], "dp", 2)
    far_x = [ns_x, over_core(after(ns_x, d_cat)), early_x, over_core(early_x)]
    far_y = [ns_y, over_core(after(ns_y, d_cat)), early_y, over_core(early_y)]

    def slot_grads(slot, last_dg):
        return routed_grads(
            slot, 2 if slot % 2 == 0 else 1, my_expert, [x_rows, last_dg, du, hid, row_gate, dy_rows],
            far_x if slot % 2 == 0 else far_y, [routed_gate, routed_up, routed_down], router_wide, expert_count,
        )

    routed = [slot_grads(0, after(dg, d_cat))]
    qk_x, b_y = after((qk_x, b_y), routed[0])
    qk_x_other, b_y_other = over_core(qk_x), over_core(b_y)
    here = lambda v: lax.dynamic_index_in_dim(v, my_z, 0, keepdims=False)
    ns_sets = jnp.concatenate(
        [normed_second, from_other[:, 3 * ff : 3 * ff + w], here(far_y[0]), here(far_y[1])], 0
    )
    a_send, a_keep, b_send, b_keep = call(
        functools.partial(last_grads_kernel, length), "last_grads",
        [((w // 8, 2 * w), BF)] * 2 + [((w // 8, 2 * w + LANES), BF)] * 2,
        d_cat, cat_other, qk_x, qk_x_other, b_y, b_y_other, left_a, left_v, left_o, ns_sets, order_b,
    )
    a_got, b_got = partner(a_send, "dp", 2), partner(b_send, "dp", 1)

    routed += [slot_grads(slot, after(dg, a_send)) for slot in range(1, slot_dev)]
    pieces = [
        (keep, partner(after(send, a_send), "dp", 2 if slot % 2 == 0 else 1))
        for slot, (send, keep) in enumerate(routed)
    ]
    a_got = after(a_got, routed)
    last = jnp.concatenate([plus(a_keep, a_got), plus(b_keep, b_got)], -1).reshape(n_z, rows, -1)

    sd = jnp.pad(sd.reshape(n_z, -1, w), ((0, 0), (0, (w - ff) // (n_dp * n_ex)), (0, 0)))
    grad_shared = exchange_z(after(jnp.concatenate([su.reshape(n_z, rows, -1), sd], -1), d_cat))
    last = exchange_z(after(last, grad_shared))
    grad_shared, combined = after((grad_shared, combined), last)
    last, grad_shared = total(list(last)), total(list(grad_shared))
    output = (residual + shared_result + combined.astype(F32)).astype(BF)
    grad_rgate, grad_rup, grad_rdown = finish(pieces, [(w // n_dp, ff), (w // n_dp, ff), (ff // n_dp, w)])
    return (
        output,
        grad_inputs,
        last[:, 4 * w + high],
        last[:, :w],
        last[:, w : 2 * w],
        last[:, 2 * w : 3 * w],
        last[:, 3 * w : 4 * w],
        last[:, 4 * w + high + 1],
        last[:, 4 * w : 4 * w + expert_count],
        grad_shared[:, :ff],
        grad_shared[:, ff : 2 * ff],
        grad_shared[: ff // (n_dp * n_ex), 2 * ff :],
        grad_rgate,
        grad_rup,
        grad_rdown,
    )


def solution(mesh):
    placed = (
        P(("dp", "expert"), None),
        P(("dp", "expert"), None),
        P(("dp", "expert"), None),
        P(),
        P(),
        P(),
        P(),
        P(),
        P(),
        P(),
        P(),
        P(),
        P(),
        P(),
        P("expert", None, None),
        P("expert", None, None),
        P("expert", None, None),
    )
    return jax.shard_map(
        shards,
        mesh=mesh,
        in_specs=placed,
        out_specs=(
            P(("dp", "expert"), None),
            P(("dp", "expert"), None),
            P(("dp", "expert")),
            P(("dp", "expert"), None),
            P(("dp", "expert"), None),
            P(("dp", "expert"), None),
            P(("dp", "expert"), None),
            P(("dp", "expert")),
            P(("dp", "expert"), None),
            P(("dp", "expert"), None),
            P(("dp", "expert"), None),
            P(("dp", "expert"), None),
            P("expert", "dp", None),
            P("expert", "dp", None),
            P("expert", "dp", None),
        ),
        check_vma=False,
    )
```

```python
import functools
import math

import jax
import jax.numpy as jnp
import numpy as np
from jax import lax
from jax.experimental import pallas as pl
from jax.experimental.pallas import tpu as pltpu
from jax.sharding import PartitionSpec as P

HEADS = 10
HEAD_DIM = 128
TOP = 6
LANES = 128
epsilon = 1e-06
BF = jnp.bfloat16
F32 = jnp.float32
VMEM_LIMIT = 60 * 2**20
COST = 1


def partner(v, axis, mask):
    n = lax.axis_size(axis)
    return lax.ppermute(v, axis, [(i, i ^ mask) for i in range(n)])


def plus(a, b):
    return (a.astype(F32) + b.astype(F32)).astype(BF)


def exchange_z(s):
    n_z = lax.axis_size("expert") // 2
    groups = [[2 * z + c for z in range(n_z)] for c in (0, 1)]
    return lax.all_to_all(s, "expert", 0, 0, tiled=True, axis_index_groups=groups)


def total(blocks):
    out = blocks[0].astype(F32)
    for b in blocks[1:]:
        out = out + b.astype(F32)
    return out


def rows_for(d, blocks):
    n_dp, n_ex = lax.axis_size("dp"), lax.axis_size("expert")
    rows = d // (n_dp * n_ex)
    n_z = n_ex // 2
    my_dp, my_core = lax.axis_index("dp"), lax.axis_index("expert") % 2
    at = np.arange(len(blocks) * n_z * rows, dtype=np.int32)
    block_dp = jnp.asarray(np.repeat(np.array(blocks, np.int32), n_z * rows)) ^ my_dp
    block = (block_dp * n_z + jnp.asarray(at // rows % n_z)) * 2 + my_core
    source = block * rows + jnp.asarray(at % rows)
    return (source[:, None] == jnp.arange(d, dtype=jnp.int32)[None, :]).astype(BF)


def dot_nn(a, b):
    return lax.dot_general(a, b, (((1,), (0,)), ((), ())), preferred_element_type=F32)


def dot_nt(a, b):
    return lax.dot_general(a, b, (((1,), (1,)), ((), ())), preferred_element_type=F32)


def dot_tn(a, b):
    return lax.dot_general(a, b, (((0,), (0,)), ((), ())), preferred_element_type=F32)


def picks(routes_t, expert, length, capacity):
    hit = jnp.where(routes_t.astype(F32) == expert.astype(F32), 1.0, 0.0)
    member = jnp.sum(hit, 0, keepdims=True)
    a = lax.broadcasted_iota(jnp.int32, (length, length), 0)
    b = lax.broadcasted_iota(jnp.int32, (length, length), 1)
    earlier = jnp.where(a < b, 1.0, 0.0).astype(BF)
    place = dot_nn(jnp.broadcast_to(member, (16, length)).astype(BF), earlier)[:1]
    row = lax.broadcasted_iota(jnp.int32, (capacity, length), 0).astype(F32)
    return jnp.where((place == row) & (member > 0.5), 1.0, 0.0).astype(BF)


def gates_of(x, router, expert, expert_count):
    logits = dot_nn(x, router)
    lane = lax.broadcasted_iota(jnp.int32, logits.shape, 1)
    logits = jnp.where(lane < expert_count, logits, -1e30)
    terms = jnp.exp(logits - jnp.max(logits, -1, keepdims=True))
    probs = terms / jnp.sum(terms, -1, keepdims=True)
    return jnp.sum(jnp.where(lane == expert, probs, 0.0), -1, keepdims=True)


def whole(shape):
    return pl.BlockSpec(shape, lambda *_: (0,) * len(shape))


def prepare_kernel(ids, early_ref, other_ref, down_ref, pick_ref, dh_ref, dy_ref):
    expert = ids[pl.program_id(0)]
    sources = early_ref.shape[0]
    capacity, length = pick_ref.shape[2:]
    for j, ref in enumerate((early_ref, other_ref)):
        for k in range(sources):
            n = j * sources + k
            pick = picks(ref[k, length : length + 16, :length], expert, length, capacity)
            pick_ref[0, n] = pick
            dy_ref[0, n * capacity : (n + 1) * capacity] = dot_nn(pick, ref[k, :length]).astype(BF)
    dh_ref[0] = dot_nt(dy_ref[0], down_ref[0])


def per_slot(*shape):
    return pl.BlockSpec((1,) + shape, lambda s, *_: (s,) + (0,) * len(shape))


def once(shape):
    return pl.BlockSpec(shape, lambda *_: (0,) * len(shape), pipeline_mode=pl.Buffered(1))


def prepare(ids, early, down, capacity):
    sources, length = early[0].shape[0], early[0].shape[1] - 16
    slots, ff, width = down.shape
    rows = 2 * sources * capacity
    return pl.pallas_call(
        prepare_kernel,
        grid_spec=pltpu.PrefetchScalarGridSpec(
            num_scalar_prefetch=1,
            grid=(slots,),
            in_specs=[once(v.shape) for v in early] + [per_slot(ff, width)],
            out_specs=[
                per_slot(2 * sources, capacity, length),
                per_slot(rows, ff),
                per_slot(rows, width),
            ],
        ),
        out_shape=[
            jax.ShapeDtypeStruct((slots, 2 * sources, capacity, length), BF),
            jax.ShapeDtypeStruct((slots, rows, ff), F32),
            jax.ShapeDtypeStruct((slots, rows, width), BF),
        ],
        compiler_params=pltpu.CompilerParams(vmem_limit_bytes=VMEM_LIMIT),
        cost_estimate=pl.CostEstimate(
            flops=1,
            bytes_accessed=1,
            transcendentals=0,
        ),
        name="prepare",
    )(ids, *early, down)


def experts_kernel(
    expert_count, ids, ns0_ref, ns1_ref, pick_ref, dh_ref, gate_ref, up_ref, router_ref,
    back0_ref, back1_ref, hid_ref, dg_ref, du_ref, rows_ref, row_gate_ref, d_rows_ref, probs_ref,
):
    s = pl.program_id(0)
    slots, total_sources, capacity, length = pick_ref.shape
    sources, _, width = ns0_ref.shape
    expert = ids[s]
    sides = [(ns0_ref, back0_ref), (ns1_ref, back1_ref)]
    for n in range(total_sources):
        ns = sides[n // sources][0][n % sources]
        rows_ref[0, n * capacity : (n + 1) * capacity] = dot_nn(pick_ref[s, n], ns).astype(BF)
    x = rows_ref[0]
    row_gate = gates_of(x, router_ref[...], expert, expert_count)
    row_gate_ref[0] = jnp.broadcast_to(row_gate, row_gate_ref.shape[1:])
    g = dot_nn(x, gate_ref[0])
    u = dot_nn(x, up_ref[0])
    sig = jax.nn.sigmoid(g)
    act = g * sig
    hid = (act * u).astype(BF)
    hid_ref[0] = hid
    raw = dh_ref[0]
    d_gate = jnp.sum(hid.astype(F32) * raw, -1, keepdims=True)
    dh = raw * row_gate
    dg = (dh * u * sig * (1.0 + g * (1.0 - sig))).astype(BF)
    du = (dh * act).astype(BF)
    dg_ref[0] = dg
    du_ref[0] = du
    d_rows_ref[s] = (dot_nt(dg, gate_ref[0]) + dot_nt(du, up_ref[0])).astype(BF)

    @pl.when(s == 0)
    def _():
        probs_ref[...] = jnp.zeros_like(probs_ref)

    parts = probs_ref.shape[2] // length
    row = lax.broadcasted_iota(jnp.int32, (16, length), 0)
    for n in range(total_sources):
        column = d_gate[n * capacity : (n + 1) * capacity]
        token = jnp.sum(pick_ref[s, n].astype(F32) * column, 0, keepdims=True)
        for b in range(parts):
            probs_ref[n, :, b * length : (b + 1) * length] += jnp.where(
                row == expert - 16 * b, token, 0.0
            )

    @pl.when(s == slots - 1)
    def _():
        wide = parts * length
        for n in range(total_sources):
            back, k = sides[n // sources][1], n % sources
            at = slice(n * capacity, (n + 1) * capacity)
            pick = jnp.concatenate([pick_ref[i, n] for i in range(slots)], 0)
            d_rows = jnp.concatenate([d_rows_ref[i, at] for i in range(slots)], 0)
            back[k, :length] = dot_tn(pick, d_rows).astype(BF)
            back[k, length:, :wide] = probs_ref[n].astype(BF)
            if wide < width:
                back[k, length:, wide:] = jnp.zeros((16, width - wide), BF)


def experts(ids, ns, pick, dh, gate, up, router, expert_count):
    sources, length, width = ns[0].shape
    slots, _, capacity, _ = pick.shape
    ff = gate.shape[2]
    rows = 2 * sources * capacity
    wide = -(-expert_count // 16) * length
    back = (sources, length + 16, width)
    return pl.pallas_call(
        functools.partial(experts_kernel, expert_count),
        grid_spec=pltpu.PrefetchScalarGridSpec(
            num_scalar_prefetch=1,
            grid=(slots,),
            in_specs=[
                once(ns[0].shape),
                once(ns[1].shape),
                once(pick.shape),
                per_slot(rows, ff),
                per_slot(width, ff),
                per_slot(width, ff),
                once(router.shape),
            ],
            out_specs=[
                once(back),
                once(back),
                per_slot(rows, ff),
                per_slot(rows, ff),
                per_slot(rows, ff),
                per_slot(rows, width),
                per_slot(rows, LANES),
            ],
            scratch_shapes=[
                pltpu.VMEM((slots, rows, width), BF),
                pltpu.VMEM((2 * sources, 16, wide), F32),
            ],
        ),
        out_shape=[jax.ShapeDtypeStruct(back, BF)] * 2
        + [jax.ShapeDtypeStruct((slots, rows, ff), BF)] * 3
        + [
            jax.ShapeDtypeStruct((slots, rows, width), BF),
            jax.ShapeDtypeStruct((slots, rows, LANES), F32),
        ],
        compiler_params=pltpu.CompilerParams(vmem_limit_bytes=VMEM_LIMIT),
        cost_estimate=pl.CostEstimate(
            flops=int(COST * (8 * slots * rows * width * ff)),
            bytes_accessed=int(COST * (slots * ff * (width * 4 + rows * 6))),
            transcendentals=slots * rows * ff,
        ),
        name="experts",
    )(ids, *ns, pick, dh, gate, up, router)


def combine_kernel(hid_ref, row_gate_ref, pick_ref, down_ref, mine_ref, other_ref, scaled_ref):
    s = pl.program_id(0)
    slots, sources, capacity, length = pick_ref.shape
    result = dot_nn(hid_ref[0], down_ref[0]).astype(BF)
    scaled_ref[s] = (result.astype(F32) * row_gate_ref[0, :, :1]).astype(BF)

    @pl.when(s == slots - 1)
    def _():
        for n in range(sources):
            at = slice(n * capacity, (n + 1) * capacity)
            pick = jnp.concatenate([pick_ref[i, n] for i in range(slots)], 0)
            scaled = jnp.concatenate([scaled_ref[i, at] for i in range(slots)], 0)
            out = (mine_ref, other_ref)[n // (sources // 2)]
            out[n % (sources // 2)] = dot_tn(pick, scaled).astype(BF)


def combine(hid, row_gate, pick, down):
    slots, sources, capacity, length = pick.shape
    _, ff, width = down.shape
    rows = sources * capacity
    out = (sources // 2, length, width)
    return pl.pallas_call(
        combine_kernel,
        grid=(slots,),
        in_specs=[per_slot(rows, ff), per_slot(rows, LANES), once(pick.shape), per_slot(ff, width)],
        out_specs=[once(out)] * 2,
        scratch_shapes=[pltpu.VMEM((slots, rows, width), BF)],
        out_shape=[jax.ShapeDtypeStruct(out, BF)] * 2,
        compiler_params=pltpu.CompilerParams(vmem_limit_bytes=VMEM_LIMIT),
        cost_estimate=pl.CostEstimate(
            flops=int(COST * (4 * slots * rows * width * (ff + length))),
            bytes_accessed=int(COST * (slots * ff * (width * 2 + rows * 2))),
            transcendentals=0,
        ),
        name="combine",
    )(hid, row_gate, pick, down)


def keep_rows(size, second):
    mine = lax.axis_index("dp")
    i = np.arange(size // 4, dtype=np.int32)
    source = jnp.concatenate([(mine ^ second) * (size // 4) + i, mine * (size // 4) + i])
    return (source[:, None] == jnp.arange(size, dtype=jnp.int32)[None, :]).astype(BF)


def routed_grads_kernel(
    expert_count, slot, ids, x_ref, dg_ref, du_ref, hid_ref, row_gate_ref, dy_ref, ns0_ref, ns1_ref, early0_ref, early1_ref,
    gate_ref, up_ref, down_ref, router_ref, sel_d_ref, sel_f_ref, send_ref, keep_ref, far_x, far_dy,
):
    expert = ids[slot]
    sources, length, width = ns0_ref.shape
    rows = far_x.shape[0]
    capacity = rows // (2 * sources)
    for j, (ns, early) in enumerate(((ns0_ref, early0_ref), (ns1_ref, early1_ref))):
        for k in range(sources):
            pick = picks(early[k, length:, :length], expert, length, capacity)
            at = slice((j * sources + k) * capacity, (j * sources + k + 1) * capacity)
            far_x[at] = dot_nn(pick, ns[k]).astype(BF)
            far_dy[at] = dot_nn(pick, early[k, :length]).astype(BF)
    x = far_x[...]
    row_gate = gates_of(x, router_ref[...], expert, expert_count)
    d_far = (far_dy[...].astype(F32) * row_gate).astype(BF)
    g = dot_nn(x, gate_ref[0])
    u = dot_nn(x, up_ref[0])
    sig = jax.nn.sigmoid(g)
    act = g * sig
    hid = (act * u).astype(BF)
    dh = dot_nt(d_far, down_ref[0])
    dg = (dh * u * sig * (1.0 + g * (1.0 - sig))).astype(BF)
    du = (dh * act).astype(BF)
    x_t = dot_nt(sel_d_ref[...], x).astype(BF)
    x_own = dot_nt(sel_d_ref[...], x_ref[0]).astype(BF)
    hid_t = dot_nt(sel_f_ref[...], hid).astype(BF)
    hid_own = dot_nt(sel_f_ref[...], hid_ref[0]).astype(BF)
    d_own = (dy_ref[0].astype(F32) * row_gate_ref[0, :, :1]).astype(BF)
    start = 0
    for value in (
        dot_nn(x_own, dg_ref[0]) + dot_nn(x_t, dg),
        dot_nn(x_own, du_ref[0]) + dot_nn(x_t, du),
        dot_nn(hid_own, d_own) + dot_nn(hid_t, d_far),
    ):
        size = value.shape[0] // 2
        for c in range(value.shape[1] // LANES):
            columns = value[:, c * LANES : (c + 1) * LANES].astype(BF)
            send_ref[start : start + size] = columns[:size]
            keep_ref[start : start + size] = columns[size:]
            start += size


def routed_grads(slot, selectors, ids, own, far, weights, router, expert_count):
    gate, up, down = weights
    _, rows, width = own[0].shape
    ff = gate.shape[2]
    at = lambda v: pl.BlockSpec(
        (1,) + v.shape[1:], lambda i, _: (slot, 0, 0), pipeline_mode=pl.Buffered(1)
    )
    shape = (3 * width * ff // 4 // LANES, LANES)
    rest = far + [router, *selectors]
    rest_specs = [once(v.shape) for v in rest]
    return pl.pallas_call(
        functools.partial(routed_grads_kernel, expert_count, slot),
        grid_spec=pltpu.PrefetchScalarGridSpec(
            num_scalar_prefetch=1,
            grid=(1,),
            in_specs=[at(v) for v in own]
            + rest_specs[: len(far)]
            + [at(v) for v in weights]
            + rest_specs[len(far) :],
            out_specs=[once(shape)] * 2,
            scratch_shapes=[pltpu.VMEM((rows, width), BF)] * 2,
        ),
        out_shape=[jax.ShapeDtypeStruct(shape, BF)] * 2,
        compiler_params=pltpu.CompilerParams(vmem_limit_bytes=VMEM_LIMIT),
        cost_estimate=pl.CostEstimate(
            flops=int(COST * (16 * rows * width * ff)),
            bytes_accessed=int(COST * (12 * width * ff + 16 * rows * width)),
            transcendentals=0,
        ),
        name="routed_grads",
    )(ids, *own, *far, *weights, *rest[len(far) :])


def finish_kernel(slots, *refs):
    outs = refs[2 * slots :]
    for s in range(slots):
        keep, got = refs[2 * s], refs[2 * s + 1]

        @pl.when(pl.program_id(0) == s)
        def _():
            start = 0
            for out in outs:
                size, columns = out.shape[1:]
                for c in range(columns // LANES):
                    at = slice(start, start + size)
                    out[0, :, c * LANES : (c + 1) * LANES] = keep[at].astype(F32) + got[at].astype(F32)
                    start += size


def finish(pieces, shapes):
    slots = len(pieces)
    return pl.pallas_call(
        functools.partial(finish_kernel, slots),
        grid=(slots,),
        in_specs=[once(v.shape) for piece in pieces for v in piece],
        out_specs=[per_slot(*shape) for shape in shapes],
        out_shape=[jax.ShapeDtypeStruct((slots,) + shape, F32) for shape in shapes],
        compiler_params=pltpu.CompilerParams(vmem_limit_bytes=VMEM_LIMIT),
        name="finish",
    )(*(v for piece in pieces for v in piece))


def rotary(length):
    half = HEAD_DIM // 2
    frequencies = np.exp(np.arange(half, dtype=np.float32) * np.float32(-math.log(10000.0) / half))
    angles = np.arange(length, dtype=np.float32)[:, None] * frequencies.astype(np.float32)[None, :]
    cosine, sine = np.cos(angles), np.sin(angles)
    return (
        np.concatenate([cosine, cosine], 1).astype(np.float32),
        np.concatenate([-sine, sine], 1).astype(np.float32),
    )


def turn(x, cosine, sine):
    return x * cosine + pltpu.roll(x, HEAD_DIM // 2, 1) * sine


def causal_probs(q, k):
    scores = dot_nt(q, k) * (1.0 / math.sqrt(HEAD_DIM))
    row = lax.broadcasted_iota(jnp.int32, scores.shape, 0)
    lane = lax.broadcasted_iota(jnp.int32, scores.shape, 1)
    scores = jnp.where(row >= lane, scores, -1e30)
    terms = jnp.exp(scores - jnp.max(scores, -1, keepdims=True))
    return terms / jnp.sum(terms, -1, keepdims=True)


def unit_of(x):
    scale = lax.rsqrt(jnp.mean(x * x, -1, keepdims=True) + epsilon)
    return x * scale, scale


def attention_kernel(
    x_ref, gain1_ref, gain2_ref, cos_ref, sin_ref, wq_ref, wk_ref, wv_ref, wo_ref,
    q_ref, k_ref, v_ref, att_ref, nf_ref, residual_ref, ns_ref,
):
    i = pl.program_id(0)

    @pl.when(i == 0)
    def _():
        x = x_ref[...].astype(F32)
        nf_ref[...] = (unit_of(x)[0] * gain1_ref[...][None]).astype(BF)
        residual_ref[...] = x

    nf = nf_ref[...]
    q_all, k_all, v_all = dot_nn(nf, wq_ref[...]), dot_nn(nf, wk_ref[...]), dot_nn(nf, wv_ref[...])
    cosine, sine = cos_ref[...], sin_ref[...]
    v_ref[...] = v_all.astype(BF)
    for h in range(q_ref.shape[1] // HEAD_DIM):
        at = slice(h * HEAD_DIM, (h + 1) * HEAD_DIM)
        q = turn(q_all[:, at], cosine, sine).astype(BF)
        k = turn(k_all[:, at], cosine, sine).astype(BF)
        q_ref[:, at] = q
        k_ref[:, at] = k
        att_ref[:, at] = dot_nn(causal_probs(q, k).astype(BF), v_all[:, at].astype(BF)).astype(BF)
    residual_ref[...] += dot_nn(att_ref[...], wo_ref[...])

    @pl.when(i == pl.num_programs(0) - 1)
    def _():
        ns_ref[...] = (unit_of(residual_ref[...])[0] * gain2_ref[...][None]).astype(BF)


def attention(x, gain1, gain2, cosine, sine, wq, wk, wv, wo):
    length, width = x.shape
    step = 2 * HEAD_DIM
    columns = lambda rows: pl.BlockSpec((rows, step), lambda i: (0, i))
    low = jax.ShapeDtypeStruct((length, width), BF)
    return pl.pallas_call(
        attention_kernel,
        grid=(width // step,),
        in_specs=[
            whole((length, width)),
            whole((width,)),
            whole((width,)),
            whole(cosine.shape),
            whole(sine.shape),
            columns(width),
            columns(width),
            columns(width),
            pl.BlockSpec((step, width), lambda i: (i, 0)),
        ],
        out_specs=[columns(length)] * 4 + [whole((length, width))] * 3,
        out_shape=[low] * 5 + [jax.ShapeDtypeStruct((length, width), F32), low],
        compiler_params=pltpu.CompilerParams(vmem_limit_bytes=VMEM_LIMIT),
        cost_estimate=pl.CostEstimate(
            flops=int(COST * 8 * length * width * width), bytes_accessed=int(COST * 8 * width * width), transcendentals=0
        ),
        name="attention",
    )(x, gain1, gain2, cosine, sine, wq, wk, wv, wo)


def backward_kernel(
    expert_count,
    x_ref, dy_ref, residual_ref, ns_ref, shared_ref, router_t_ref, gain1_ref, gain2_ref,
    cos_ref, sin_ref, q_ref, k_ref, v_ref, wq_ref, wk_ref, wv_ref, wo_ref, *refs,
):
    parts = refs[0]
    cat_ref, grad_ref, branch_ref, d_res_ref, acc_ref = refs[1:]
    i = pl.program_id(0)
    length, width = x_ref.shape
    step = wq_ref.shape[1]
    here = pl.multiple_of(i * step, step)
    gains = slice(4 * length, 4 * length + 16)

    @pl.when(i == 0)
    def _():
        back = parts[0, :length].astype(F32)
        tail = parts[0, length:].astype(F32)
        for p in range(1, parts.shape[0]):
            back += parts[p, :length].astype(F32)
            tail += parts[p, length:].astype(F32)
        blocks = router_t_ref.shape[0] // 16
        d_probs = jnp.concatenate([tail[:, b * length : (b + 1) * length] for b in range(blocks)], 0)
        logits = dot_nt(router_t_ref[...], ns_ref[...])
        row = lax.broadcasted_iota(jnp.int32, logits.shape, 0)
        logits = jnp.where(row < expert_count, logits, -1e30)
        terms = jnp.exp(logits - jnp.max(logits, 0, keepdims=True))
        probs = terms / jnp.sum(terms, 0, keepdims=True)
        d_logits = probs * (d_probs - jnp.sum(probs * d_probs, 0, keepdims=True))
        d_logits = jnp.where(row < expert_count, d_logits, 0.0).astype(BF)
        cat_ref[4 * length + 16 :] = jnp.zeros((d_logits.shape[0], width), BF)
        cat_ref[4 * length + 16 :, :length] = d_logits
        d_normed = shared_ref[...] + back + dot_tn(d_logits, router_t_ref[...])
        unit, scale = unit_of(residual_ref[...])
        c = d_normed * gain2_ref[...][None]
        gain_row = jnp.sum(d_normed * unit, 0, keepdims=True)
        which = lax.broadcasted_iota(jnp.int32, (16, width), 0)
        cat_ref[gains] = jnp.where(which == 1, gain_row, 0.0).astype(BF)
        d_res = dy_ref[...].astype(F32) + scale * (c - unit * jnp.mean(c * unit, -1, keepdims=True))
        d_res_ref[...] = d_res
        branch_ref[...] = d_res.astype(BF)
        cat_ref[3 * length : 4 * length] = d_res.astype(BF)
        acc_ref[...] = jnp.zeros_like(acc_ref)

    cosine, sine = cos_ref[...], -sin_ref[...]
    att_scale = 1.0 / math.sqrt(HEAD_DIM)
    d_att_all = dot_nt(branch_ref[...], wo_ref[...]).astype(BF)
    d_q, d_k, d_v = [], [], []
    for h in range(step // HEAD_DIM):
        at = slice(h * HEAD_DIM, (h + 1) * HEAD_DIM)
        q, k, v, d_attended = q_ref[:, at], k_ref[:, at], v_ref[:, at], d_att_all[:, at]
        probs = causal_probs(q, k)
        d_att = dot_nt(d_attended, v)
        d_scores = (probs * (d_att - jnp.sum(probs * d_att, -1, keepdims=True))).astype(BF)
        d_q.append(turn(dot_nn(d_scores, k) * att_scale, cosine, sine).astype(BF))
        d_k.append(turn(dot_tn(d_scores, q) * att_scale, cosine, sine).astype(BF))
        d_v.append(dot_tn(probs.astype(BF), d_attended).astype(BF))
    d_q, d_k, d_v = (jnp.concatenate(v, 1) for v in (d_q, d_k, d_v))
    for n, v in enumerate((d_q, d_k, d_v)):
        cat_ref[n * length : (n + 1) * length, pl.ds(here, step)] = v
    acc_ref[...] += dot_nt(d_q, wq_ref[...]) + dot_nt(d_k, wk_ref[...]) + dot_nt(d_v, wv_ref[...])

    @pl.when(i == pl.num_programs(0) - 1)
    def _():
        unit, scale = unit_of(x_ref[...].astype(F32))
        d_normed = acc_ref[...]
        c = d_normed * gain1_ref[...][None]
        gain_row = jnp.sum(d_normed * unit, 0, keepdims=True)
        which = lax.broadcasted_iota(jnp.int32, (16, width), 0)
        cat_ref[gains] = jnp.where(which == 0, gain_row, cat_ref[gains].astype(F32)).astype(BF)
        grad_ref[...] = d_res_ref[...] + scale * (c - unit * jnp.mean(c * unit, -1, keepdims=True))


def backward(
    x, dy, residual, ns, shared, router_t, gain1, gain2, cosine, sine,
    q, k, v, wq, wk, wv, wo, parts, expert_count,
):
    length, width = x.shape
    step = 2 * HEAD_DIM
    columns = lambda rows: pl.BlockSpec((rows, step), lambda i: (0, i))
    tall = whole((length, width))
    return pl.pallas_call(
        functools.partial(backward_kernel, expert_count),
        grid=(width // step,),
        in_specs=[tall] * 5
        + [whole(router_t.shape), whole((width,)), whole((width,))]
        + [whole(cosine.shape)] * 2
        + [columns(length)] * 3
        + [columns(width)] * 3
        + [pl.BlockSpec((step, width), lambda i: (i, 0))]
        + [whole(parts.shape)],
        out_specs=[
            whole((4 * length + 16 + router_t.shape[0], width)),
            tall,
        ],
        scratch_shapes=[
            pltpu.VMEM((length, width), BF),
            pltpu.VMEM((length, width), F32),
            pltpu.VMEM((length, width), F32),
        ],
        out_shape=[
            jax.ShapeDtypeStruct((4 * length + 16 + router_t.shape[0], width), BF),
            jax.ShapeDtypeStruct((length, width), F32),
        ],
        compiler_params=pltpu.CompilerParams(vmem_limit_bytes=VMEM_LIMIT),
        cost_estimate=pl.CostEstimate(
            flops=int(COST * 8 * length * width * width), bytes_accessed=int(COST * 8 * width * width), transcendentals=0
        ),
        name="backward",
    )(
        x, dy, residual, ns, shared, router_t, gain1, gain2, cosine, sine,
        q, k, v, wq, wk, wv, wo, parts,
    )


def call(kernel, name, outs, *args, scalars=0):
    return pl.pallas_call(
        kernel,
        in_specs=[pl.BlockSpec(memory_space=pltpu.SMEM)] * scalars
        + [pl.BlockSpec(memory_space=pltpu.VMEM)] * (len(args) - scalars),
        out_specs=[pl.BlockSpec(memory_space=pltpu.VMEM)] * len(outs),
        out_shape=[jax.ShapeDtypeStruct(*o) for o in outs],
        compiler_params=pltpu.CompilerParams(vmem_limit_bytes=VMEM_LIMIT),
        cost_estimate=pl.CostEstimate(flops=1, bytes_accessed=1, transcendentals=0),
        name=name,
    )(*args)


def shared_kernel(ns_ref, dy_ref, gate_ref, up_ref, down_ref, cat_ref, result_ref, back_ref):
    ns, dy = ns_ref[...], dy_ref[...]
    width, ff = gate_ref.shape
    g = dot_nn(ns, gate_ref[...])
    u = dot_nn(ns, up_ref[...])
    sig = jax.nn.sigmoid(g)
    act = g * sig
    hid = (act * u).astype(BF)
    dh = dot_nt(dy, down_ref[...])
    dg = (dh * u * sig * (1.0 + g * (1.0 - sig))).astype(BF)
    du = (dh * act).astype(BF)
    result_ref[...] = dot_nn(hid, down_ref[...])
    back_ref[...] = dot_nt(dg, gate_ref[...]) + dot_nt(du, up_ref[...])
    for i, v in enumerate((dg, du, hid)):
        cat_ref[:, i * ff : (i + 1) * ff] = v
    cat_ref[:, 3 * ff : 3 * ff + width] = ns
    cat_ref[:, 3 * ff + width :] = dy


def shared_grads_kernel(ff, width, cat_ref, other_ref, order_d_ref, order_f_ref, su_send, su_keep, sd_send, sd_keep):
    pair = jnp.concatenate([cat_ref[...], other_ref[...]], 0)
    ns_t = dot_nt(order_d_ref[...], pair[:, 3 * ff : 3 * ff + width]).astype(BF)
    hid_t = dot_nt(order_f_ref[...], pair[:, 2 * ff : 3 * ff]).astype(BF)
    su = dot_nn(ns_t, pair[:, : 2 * ff]).astype(BF)
    sd = dot_nn(hid_t, pair[:, 3 * ff + width :]).astype(BF)
    for value, send, keep in ((su, su_send, su_keep), (sd, sd_send, sd_keep)):
        n = send.shape[1]
        for i in range(2):
            send[i] = value[i * n : (i + 1) * n]
            keep[i] = value[(2 + i) * n : (3 + i) * n]


def lefts_kernel(mine_ref, other_ref, order_a_ref, order_b_ref, a_ref, v_ref, o_ref):
    sets = lambda i, j: jnp.concatenate([mine_ref[i], other_ref[i], mine_ref[j], other_ref[j]], 0)
    a_ref[...] = dot_nt(order_a_ref[...], sets(0, 2)).astype(BF)
    v_ref[...] = dot_nt(order_b_ref[...], sets(0, 3)).astype(BF)
    o_ref[...] = dot_nt(order_b_ref[...], sets(1, 4)).astype(BF)


def last_grads_kernel(
    length, at_ns, z_ref, mine_ref, other_ref, qx_ref, qxo_ref, by_ref, byo_ref, a_ref, v_ref, o_ref,
    ns_ref, cat_other_ref, ns_y_ref, ns_yo_ref, order_b_ref,
    a_send, a_keep, b_send, b_keep,
):
    width = mine_ref.shape[1]
    half = a_send.shape[0]
    join = lambda *v: jnp.concatenate(v, 0)

    def put(value, keep, send, columns):
        keep[:, columns] = value[:half].astype(BF)
        send[:, columns] = value[half:].astype(BF)

    for i in range(2):
        at = slice(i * length, (i + 1) * length)
        tokens = join(mine_ref[at], other_ref[at], qx_ref[at], qxo_ref[at])
        put(dot_nn(a_ref[...], tokens), a_keep, a_send, slice(i * width, (i + 1) * width))
        past = slice((2 + i) * length, (3 + i) * length)
        tokens = join(mine_ref[past], other_ref[past], by_ref[at], byo_ref[at])
        left = (v_ref, o_ref)[i]
        put(dot_nn(left[...], tokens), b_keep, b_send, slice(i * width, (i + 1) * width))
    start = 4 * length
    refs = ((mine_ref, start), (other_ref, start), (by_ref, start - 2 * length), (byo_ref, start - 2 * length))
    gains = sum(ref[i : i + 16].astype(F32) for ref, i in refs).astype(BF)
    logits = jnp.concatenate([ref[i + 16 :, :length] for ref, i in refs], 1)
    ns = join(
        ns_ref[...], cat_other_ref[:, at_ns : at_ns + width], ns_y_ref[z_ref[0]], ns_yo_ref[z_ref[0]]
    )
    left_r = dot_nt(order_b_ref[...], ns).astype(BF)
    small = jnp.concatenate(
        [dot_nt(left_r, logits), dot_nt(order_b_ref[...], gains)], 1
    )
    small = jnp.concatenate([small, jnp.zeros((2 * half, LANES - small.shape[1]), F32)], 1)
    put(small, b_keep, b_send, slice(2 * width, 2 * width + LANES))


def after(value, *earlier):
    return lax.optimization_barrier((value, earlier))[0]


def shards(
    tokens,
    cotangent,
    routes,
    expert_at,
    norm1_gain,
    w_query,
    w_key,
    w_value,
    w_out,
    norm2_gain,
    w_router,
    shared_gate,
    shared_up,
    shared_down,
    routed_gate,
    routed_up,
    routed_down,
):
    length, model_width = tokens.shape
    expert_count = w_router.shape[1]
    slot_dev = routed_gate.shape[0]
    n_ex = lax.axis_size("expert")
    n_dp = lax.axis_size("dp")
    capacity = (length * TOP * 5 // (4 * expert_count) + 7) // 8 * 8
    my_dp, my_ex = lax.axis_index("dp"), lax.axis_index("expert")
    n_z = n_ex // 2
    w = model_width
    rows = w // (n_dp * n_ex)
    over_core = lambda v: partner(v, "expert", 1)
    order_d = rows_for(w, (2, 3, 0, 1))
    order_a, order_b = rows_for(w, (0, 2)), rows_for(w, (0, 1))

    routes_t = jnp.pad(routes.T.astype(BF), ((0, 16 - TOP), (0, 0)), constant_values=-1)
    routes_t = jnp.pad(routes_t, ((0, 0), (0, w - length)))
    spread = lambda v: exchange_z(jnp.broadcast_to(v[None], (n_z,) + v.shape))
    early = spread(jnp.concatenate([cotangent, routes_t], 0))
    cosine, sine = (jnp.asarray(t) for t in rotary(length))
    gain1, gain2 = norm1_gain, norm2_gain
    queries, key_rows, value_rows, attended, normed_first, residual, normed_second = attention(
        tokens, gain1, gain2, cosine, sine, w_query, w_key, w_value, w_out
    )
    ff = shared_gate.shape[1]
    from_shared, shared_result, shared_back = call(
        shared_kernel, "shared",
        [((length, 3 * ff + 2 * w), BF), ((length, w), F32), ((length, w), F32)],
        normed_second, cotangent, shared_gate, shared_up, shared_down,
    )
    my_z = my_ex // 2
    first_x = partner(normed_first, "dp", 1)
    first_y = partner(jnp.stack([normed_first, attended]), "dp", 2)
    ns = spread(after(normed_second, early, from_shared, first_x, first_y))
    from_other = over_core(from_shared)
    part_d, part_f = w // (2 * n_dp), ff // (2 * n_dp)
    su_send, su_keep, sd_send, sd_keep = call(
        functools.partial(shared_grads_kernel, ff, w), "shared_grads",
        [((2, part_d, 2 * ff), BF)] * 2 + [((2, part_f, w), BF)] * 2,
        from_shared, from_other, order_d, rows_for(ff, (1, 3, 0, 2)),
    )
    early_other = over_core(early)
    early_x, early_y = partner(early, "dp", 1), partner(early, "dp", 2)

    my_expert = lax.dynamic_slice_in_dim(expert_at, my_ex * slot_dev, slot_dev)
    router_wide = jnp.pad(w_router, ((0, 0), (0, LANES - expert_count)))
    pick, dh_raw, dy_rows = prepare(my_expert, (early, early_other), routed_down, capacity)
    ns = after(ns, pick, dh_raw, early_x, early_y, su_send)
    ns_other = over_core(ns)
    back_mine, back_other, hid, dg, du, x_rows, row_gate = experts(
        my_expert, (ns, ns_other), pick, dh_raw, routed_gate, routed_up, router_wide, expert_count
    )
    back_sum = plus(back_mine, over_core(back_other))
    back = exchange_z(back_sum)
    ns_far, su_send, sd_send, early_x, early_y = after((ns, su_send, sd_send, early_x, early_y), back_sum)
    early_x_other, early_y_other = over_core(early_x), over_core(early_y)
    su_got, sd_got = partner(su_send, "dp", 2), partner(sd_send, "dp", 1)
    ns_far = after(ns_far, su_got)
    ns_x, ns_y = partner(ns_far, "dp", 1), partner(ns_far, "dp", 2)
    su, sd = plus(su_keep, su_got), plus(sd_keep, sd_got)
    su_last, sd_last = partner(su[1], "dp", 1), partner(sd[1], "dp", 2)
    su, sd = plus(su[0], su_last), plus(sd[0], sd_last)

    lefts = jnp.concatenate([normed_first[None], attended[None], first_x[None], first_y])
    lefts = after(lefts, back_sum)
    lefts_other = over_core(lefts)
    left_shape = ((w // 4, 4 * length), BF)
    left_a, left_v, left_o = call(
        lefts_kernel, "lefts", [left_shape] * 3, lefts, lefts_other, order_a, order_b,
    )
    combined_mine, combined_other = combine(after(hid, early_x_other, early_y_other), row_gate, pick, routed_down)
    combined = plus(combined_mine, over_core(combined_other))
    selectors = [(keep_rows(w, q), keep_rows(ff, q)) for q in (2, 1)]
    back = after(back, combined, left_a, selectors)
    combined = exchange_z(after(combined, back))

    high = -(-expert_count // 16) * 16
    router_t = jnp.pad(w_router.T, ((0, high - expert_count), (0, 0)))
    d_cat, grad_inputs = backward(
        tokens, cotangent, residual, normed_second, shared_back, router_t, gain1, gain2, cosine, sine,
        queries, key_rows, value_rows, w_query, w_key, w_value, w_out, back, expert_count,
    )

    d_out = d_cat
    qk_x, b_y = partner(d_out[: 2 * length], "dp", 1), partner(d_out[2 * length :], "dp", 2)
    far_x = [ns_x, over_core(after(ns_x, d_cat)), early_x, early_x_other]

    far_y = [ns_y, over_core(after(ns_y, d_cat)), early_y, early_y_other]
    far = [far_x, far_y]

    def slot_grads(slot, last_dg):
        return routed_grads(
            slot, selectors[slot % 2], my_expert, [x_rows, last_dg, du, hid, row_gate, dy_rows],
            far[slot % 2], [routed_gate, routed_up, routed_down], router_wide, expert_count,
        )

    routed = [slot_grads(0, after(dg, d_cat, far_y[1]))]
    d_cat, qk_x, b_y = after((d_cat, qk_x, b_y), routed[0], su_last, sd_last)

    cat_other = over_core(d_cat)
    qk_x_other, b_y_other = over_core(qk_x), over_core(b_y)
    a_send, a_keep, b_send, b_keep = call(
        functools.partial(last_grads_kernel, length, 3 * ff), "last_grads",
        [((w // 8, 2 * w), BF)] * 2 + [((w // 8, 2 * w + LANES), BF)] * 2,
        my_z[None], d_cat, cat_other, qk_x, qk_x_other, b_y, b_y_other, left_a, left_v, left_o,
        normed_second, from_other, far_y[0], far_y[1], order_b, scalars=1,
    )
    a_got, b_got = partner(a_send, "dp", 2), partner(b_send, "dp", 1)

    routed += [slot_grads(slot, after(dg, a_send)) for slot in range(1, slot_dev)]
    pieces = [
        (keep, partner(after(send, a_send), "dp", 2 if slot % 2 == 0 else 1))
        for slot, (send, keep) in enumerate(routed)
    ]
    a_got = after(a_got, routed)
    last = jnp.concatenate([plus(a_keep, a_got), plus(b_keep, b_got)], -1).reshape(n_z, rows, -1)

    sd = jnp.pad(sd.reshape(n_z, -1, w), ((0, 0), (0, (w - ff) // (n_dp * n_ex)), (0, 0)))
    grad_shared = exchange_z(after(jnp.concatenate([su.reshape(n_z, rows, -1), sd], -1), combined))
    last = exchange_z(after(last, grad_shared))
    grad_shared, combined = after((grad_shared, combined), last)
    last, grad_shared = total(list(last)), total(list(grad_shared))
    output = (residual + shared_result + total(list(combined))).astype(BF)
    grad_rgate, grad_rup, grad_rdown = finish(pieces, [(w // n_dp, ff), (w // n_dp, ff), (ff // n_dp, w)])
    return (
        output,
        grad_inputs,
        last[:, 4 * w + high],
        last[:, :w],
        last[:, w : 2 * w],
        last[:, 2 * w : 3 * w],
        last[:, 3 * w : 4 * w],
        last[:, 4 * w + high + 1],
        last[:, 4 * w : 4 * w + expert_count],
        grad_shared[:, :ff],
        grad_shared[:, ff : 2 * ff],
        grad_shared[: ff // (n_dp * n_ex), 2 * ff :],
        grad_rgate,
        grad_rup,
        grad_rdown,
    )


def solution(mesh):
    placed = (
        P(("dp", "expert"), None),
        P(("dp", "expert"), None),
        P(("dp", "expert"), None),
        P(),
        P(),
        P(),
        P(),
        P(),
        P(),
        P(),
        P(),
        P(),
        P(),
        P(),
        P("expert", None, None),
        P("expert", None, None),
        P("expert", None, None),
    )
    return jax.shard_map(
        shards,
        mesh=mesh,
        in_specs=placed,
        out_specs=(
            P(("dp", "expert"), None),
            P(("dp", "expert"), None),
            P(("dp", "expert")),
            P(("dp", "expert"), None),
            P(("dp", "expert"), None),
            P(("dp", "expert"), None),
            P(("dp", "expert"), None),
            P(("dp", "expert")),
            P(("dp", "expert"), None),
            P(("dp", "expert"), None),
            P(("dp", "expert"), None),
            P(("dp", "expert"), None),
            P("expert", "dp", None),
            P("expert", "dp", None),
            P("expert", "dp", None),
        ),
        check_vma=False,
    )
```

```python
import functools
import math

import jax
import jax.numpy as jnp
import numpy as np
from jax import lax
from jax.experimental import pallas as pl
from jax.experimental.pallas import tpu as pltpu
from jax.sharding import PartitionSpec as P

HEADS = 10
HEAD_DIM = 128
TOP = 6
LANES = 128
epsilon = 1e-06
BF = jnp.bfloat16
F32 = jnp.float32
VMEM_LIMIT = 60 * 2**20
COST = 1


def partner(v, axis, mask):
    n = lax.axis_size(axis)
    return lax.ppermute(v, axis, [(i, i ^ mask) for i in range(n)])


def plus(a, b):
    return (a.astype(F32) + b.astype(F32)).astype(BF)


def exchange_z(s):
    n_z = lax.axis_size("expert") // 2
    groups = [[2 * z + c for z in range(n_z)] for c in (0, 1)]
    return lax.all_to_all(s, "expert", 0, 0, tiled=True, axis_index_groups=groups)


def total(blocks):
    out = blocks[0].astype(F32)
    for b in blocks[1:]:
        out = out + b.astype(F32)
    return out


def rows_for(d, blocks):
    n_dp, n_ex = lax.axis_size("dp"), lax.axis_size("expert")
    rows = d // (n_dp * n_ex)
    n_z = n_ex // 2
    my_dp, my_core = lax.axis_index("dp"), lax.axis_index("expert") % 2
    at = np.arange(len(blocks) * n_z * rows, dtype=np.int32)
    block_dp = jnp.asarray(np.repeat(np.array(blocks, np.int32), n_z * rows)) ^ my_dp
    block = (block_dp * n_z + jnp.asarray(at // rows % n_z)) * 2 + my_core
    source = block * rows + jnp.asarray(at % rows)
    return (source[:, None] == jnp.arange(d, dtype=jnp.int32)[None, :]).astype(BF)


def dot_nn(a, b):
    return lax.dot_general(a, b, (((1,), (0,)), ((), ())), preferred_element_type=F32)


def dot_nt(a, b):
    return lax.dot_general(a, b, (((1,), (1,)), ((), ())), preferred_element_type=F32)


def dot_tn(a, b):
    return lax.dot_general(a, b, (((0,), (0,)), ((), ())), preferred_element_type=F32)


def picks(routes_t, expert, length, capacity):
    hit = jnp.where(routes_t.astype(F32) == expert.astype(F32), 1.0, 0.0)
    member = jnp.sum(hit, 0, keepdims=True)
    a = lax.broadcasted_iota(jnp.int32, (length, length), 0)
    b = lax.broadcasted_iota(jnp.int32, (length, length), 1)
    earlier = jnp.where(a < b, 1.0, 0.0).astype(BF)
    place = dot_nn(jnp.broadcast_to(member, (16, length)).astype(BF), earlier)[:1]
    row = lax.broadcasted_iota(jnp.int32, (capacity, length), 0).astype(F32)
    return jnp.where((place == row) & (member > 0.5), 1.0, 0.0).astype(BF)


def gates_of(x, router, expert, expert_count):
    logits = dot_nn(x, router)
    lane = lax.broadcasted_iota(jnp.int32, logits.shape, 1)
    logits = jnp.where(lane < expert_count, logits, -1e30)
    terms = jnp.exp(logits - jnp.max(logits, -1, keepdims=True))
    probs = terms / jnp.sum(terms, -1, keepdims=True)
    return jnp.sum(jnp.where(lane == expert, probs, 0.0), -1, keepdims=True)


def whole(shape):
    return pl.BlockSpec(shape, lambda *_: (0,) * len(shape))


def prepare_kernel(ids, early_ref, other_ref, down_ref, pick_ref, dh_ref, dy_ref):
    expert = ids[pl.program_id(0)]
    sources = early_ref.shape[0]
    capacity, length = pick_ref.shape[2:]
    for j, ref in enumerate((early_ref, other_ref)):
        for k in range(sources):
            n = j * sources + k
            pick = picks(ref[k, length : length + 16, :length], expert, length, capacity)
            pick_ref[0, n] = pick
            dy_ref[0, n * capacity : (n + 1) * capacity] = dot_nn(pick, ref[k, :length]).astype(BF)
    dh_ref[0] = dot_nt(dy_ref[0], down_ref[0])


def per_slot(*shape):
    return pl.BlockSpec((1,) + shape, lambda s, *_: (s,) + (0,) * len(shape))


def once(shape):
    return pl.BlockSpec(shape, lambda *_: (0,) * len(shape), pipeline_mode=pl.Buffered(1))


def prepare(ids, early, down, capacity):
    sources, length = early[0].shape[0], early[0].shape[1] - 16
    slots, ff, width = down.shape
    rows = 2 * sources * capacity
    return pl.pallas_call(
        prepare_kernel,
        grid_spec=pltpu.PrefetchScalarGridSpec(
            num_scalar_prefetch=1,
            grid=(slots,),
            in_specs=[once(v.shape) for v in early] + [per_slot(ff, width)],
            out_specs=[
                per_slot(2 * sources, capacity, length),
                per_slot(rows, ff),
                per_slot(rows, width),
            ],
        ),
        out_shape=[
            jax.ShapeDtypeStruct((slots, 2 * sources, capacity, length), BF),
            jax.ShapeDtypeStruct((slots, rows, ff), F32),
            jax.ShapeDtypeStruct((slots, rows, width), BF),
        ],
        compiler_params=pltpu.CompilerParams(vmem_limit_bytes=VMEM_LIMIT),
        cost_estimate=pl.CostEstimate(
            flops=1,
            bytes_accessed=1,
            transcendentals=0,
        ),
        name="prepare",
    )(ids, *early, down)


def experts_kernel(
    expert_count, ids, ns0_ref, ns1_ref, pick_ref, dh_ref, gate_ref, up_ref, router_ref,
    back0_ref, back1_ref, hid_ref, dg_ref, du_ref, rows_ref, row_gate_ref, d_rows_ref, probs_ref,
):
    s = pl.program_id(0)
    slots, total_sources, capacity, length = pick_ref.shape
    sources, _, width = ns0_ref.shape
    expert = ids[s]
    sides = [(ns0_ref, back0_ref), (ns1_ref, back1_ref)]
    for n in range(total_sources):
        ns = sides[n // sources][0][n % sources]
        rows_ref[0, n * capacity : (n + 1) * capacity] = dot_nn(pick_ref[s, n], ns).astype(BF)
    x = rows_ref[0]
    row_gate = gates_of(x, router_ref[...], expert, expert_count)
    row_gate_ref[0] = jnp.broadcast_to(row_gate, row_gate_ref.shape[1:])
    g = dot_nn(x, gate_ref[0])
    u = dot_nn(x, up_ref[0])
    sig = jax.nn.sigmoid(g)
    act = g * sig
    hid = (act * u).astype(BF)
    hid_ref[0] = hid
    raw = dh_ref[0]
    d_gate = jnp.sum(hid.astype(F32) * raw, -1, keepdims=True)
    dh = raw * row_gate
    dg = (dh * u * sig * (1.0 + g * (1.0 - sig))).astype(BF)
    du = (dh * act).astype(BF)
    dg_ref[0] = dg
    du_ref[0] = du
    d_rows_ref[s] = (dot_nt(dg, gate_ref[0]) + dot_nt(du, up_ref[0])).astype(BF)

    @pl.when(s == 0)
    def _():
        probs_ref[...] = jnp.zeros_like(probs_ref)

    parts = probs_ref.shape[2] // length
    row = lax.broadcasted_iota(jnp.int32, (16, length), 0)
    for n in range(total_sources):
        column = d_gate[n * capacity : (n + 1) * capacity]
        token = jnp.sum(pick_ref[s, n].astype(F32) * column, 0, keepdims=True)
        for b in range(parts):
            probs_ref[n, :, b * length : (b + 1) * length] += jnp.where(
                row == expert - 16 * b, token, 0.0
            )

    @pl.when(s == slots - 1)
    def _():
        wide = parts * length
        for n in range(total_sources):
            back, k = sides[n // sources][1], n % sources
            at = slice(n * capacity, (n + 1) * capacity)
            pick = jnp.concatenate([pick_ref[i, n] for i in range(slots)], 0)
            d_rows = jnp.concatenate([d_rows_ref[i, at] for i in range(slots)], 0)
            back[k, :length] = dot_tn(pick, d_rows).astype(BF)
            back[k, length:, :wide] = probs_ref[n].astype(BF)
            if wide < width:
                back[k, length:, wide:] = jnp.zeros((16, width - wide), BF)


def experts(ids, ns, pick, dh, gate, up, router, expert_count):
    sources, length, width = ns[0].shape
    slots, _, capacity, _ = pick.shape
    ff = gate.shape[2]
    rows = 2 * sources * capacity
    wide = -(-expert_count // 16) * length
    back = (sources, length + 16, width)
    return pl.pallas_call(
        functools.partial(experts_kernel, expert_count),
        grid_spec=pltpu.PrefetchScalarGridSpec(
            num_scalar_prefetch=1,
            grid=(slots,),
            in_specs=[
                once(ns[0].shape),
                once(ns[1].shape),
                once(pick.shape),
                per_slot(rows, ff),
                per_slot(width, ff),
                per_slot(width, ff),
                once(router.shape),
            ],
            out_specs=[
                once(back),
                once(back),
                per_slot(rows, ff),
                per_slot(rows, ff),
                per_slot(rows, ff),
                per_slot(rows, width),
                per_slot(rows, LANES),
            ],
            scratch_shapes=[
                pltpu.VMEM((slots, rows, width), BF),
                pltpu.VMEM((2 * sources, 16, wide), F32),
            ],
        ),
        out_shape=[jax.ShapeDtypeStruct(back, BF)] * 2
        + [jax.ShapeDtypeStruct((slots, rows, ff), BF)] * 3
        + [
            jax.ShapeDtypeStruct((slots, rows, width), BF),
            jax.ShapeDtypeStruct((slots, rows, LANES), F32),
        ],
        compiler_params=pltpu.CompilerParams(vmem_limit_bytes=VMEM_LIMIT),
        cost_estimate=pl.CostEstimate(
            flops=int(COST * (8 * slots * rows * width * ff)),
            bytes_accessed=int(COST * (slots * ff * (width * 4 + rows * 6))),
            transcendentals=slots * rows * ff,
        ),
        name="experts",
    )(ids, *ns, pick, dh, gate, up, router)


def combine_kernel(hid_ref, row_gate_ref, pick_ref, down_ref, mine_ref, other_ref, scaled_ref):
    s = pl.program_id(0)
    slots, sources, capacity, length = pick_ref.shape
    result = dot_nn(hid_ref[0], down_ref[0]).astype(BF)
    scaled_ref[s] = (result.astype(F32) * row_gate_ref[0, :, :1]).astype(BF)

    @pl.when(s == slots - 1)
    def _():
        for n in range(sources):
            at = slice(n * capacity, (n + 1) * capacity)
            pick = jnp.concatenate([pick_ref[i, n] for i in range(slots)], 0)
            scaled = jnp.concatenate([scaled_ref[i, at] for i in range(slots)], 0)
            out = (mine_ref, other_ref)[n // (sources // 2)]
            out[n % (sources // 2)] = dot_tn(pick, scaled).astype(BF)


def combine(hid, row_gate, pick, down):
    slots, sources, capacity, length = pick.shape
    _, ff, width = down.shape
    rows = sources * capacity
    out = (sources // 2, length, width)
    return pl.pallas_call(
        combine_kernel,
        grid=(slots,),
        in_specs=[per_slot(rows, ff), per_slot(rows, LANES), once(pick.shape), per_slot(ff, width)],
        out_specs=[once(out)] * 2,
        scratch_shapes=[pltpu.VMEM((slots, rows, width), BF)],
        out_shape=[jax.ShapeDtypeStruct(out, BF)] * 2,
        compiler_params=pltpu.CompilerParams(vmem_limit_bytes=VMEM_LIMIT),
        cost_estimate=pl.CostEstimate(
            flops=int(COST * (4 * slots * rows * width * (ff + length))),
            bytes_accessed=int(COST * (slots * ff * (width * 2 + rows * 2))),
            transcendentals=0,
        ),
        name="combine",
    )(hid, row_gate, pick, down)


def keep_rows(size, second):
    mine = lax.axis_index("dp")
    i = np.arange(size // 4, dtype=np.int32)
    source = jnp.concatenate([(mine ^ second) * (size // 4) + i, mine * (size // 4) + i])
    return (source[:, None] == jnp.arange(size, dtype=jnp.int32)[None, :]).astype(BF)


def routed_grads_kernel(
    expert_count, slot, ids, row_gate_ref, ns0_ref, ns1_ref, early0_ref, early1_ref, router_ref, *refs,
):
    late, (send_ref, keep_ref, far_x, far_dy), bufs, sems = refs[:10], refs[10:14], refs[14:24], refs[24]
    copies = []
    for i, (ref, buf) in enumerate(zip(late, bufs)):
        source = ref.at[slot] if len(ref.shape) == 3 else ref
        copies.append(pltpu.make_async_copy(source, buf, sems.at[i]))
    for copy in copies:
        copy.start()
    gate_ref, up_ref, down_ref, sel_d_ref, x_ref, sel_f_ref, hid_ref, dg_ref, du_ref, dy_ref = bufs
    expert = ids[slot]
    sources, length, width = ns0_ref.shape
    rows = far_x.shape[0]
    capacity = rows // (2 * sources)
    for j, (ns, early) in enumerate(((ns0_ref, early0_ref), (ns1_ref, early1_ref))):
        for k in range(sources):
            pick = picks(early[k, length:, :length], expert, length, capacity)
            at = slice((j * sources + k) * capacity, (j * sources + k + 1) * capacity)
            far_x[at] = dot_nn(pick, ns[k]).astype(BF)
            far_dy[at] = dot_nn(pick, early[k, :length]).astype(BF)
    x = far_x[...]
    row_gate = gates_of(x, router_ref[...], expert, expert_count)
    d_far = (far_dy[...].astype(F32) * row_gate).astype(BF)
    copies[0].wait()
    g = dot_nn(x, gate_ref[...])
    copies[1].wait()
    u = dot_nn(x, up_ref[...])
    sig = jax.nn.sigmoid(g)
    act = g * sig
    hid = (act * u).astype(BF)
    copies[2].wait()
    dh = dot_nt(d_far, down_ref[...])
    dg = (dh * u * sig * (1.0 + g * (1.0 - sig))).astype(BF)
    du = (dh * act).astype(BF)
    for copy in copies[3:]:
        copy.wait()
    x_t = dot_nt(sel_d_ref[...], x).astype(BF)
    x_own = dot_nt(sel_d_ref[...], x_ref[...]).astype(BF)
    hid_t = dot_nt(sel_f_ref[...], hid).astype(BF)
    hid_own = dot_nt(sel_f_ref[...], hid_ref[...]).astype(BF)
    d_own = (dy_ref[...].astype(F32) * row_gate_ref[0, :, :1]).astype(BF)
    start = 0
    for value in (
        dot_nn(x_own, dg_ref[...]) + dot_nn(x_t, dg),
        dot_nn(x_own, du_ref[...]) + dot_nn(x_t, du),
        dot_nn(hid_own, d_own) + dot_nn(hid_t, d_far),
    ):
        size = value.shape[0] // 2
        for c in range(value.shape[1] // LANES):
            columns = value[:, c * LANES : (c + 1) * LANES].astype(BF)
            send_ref[start : start + size] = columns[:size]
            keep_ref[start : start + size] = columns[size:]
            start += size


def routed_grads(slot, selectors, ids, own, far, weights, router, expert_count):
    gate, up, down = weights
    x, dg, du, hid, row_gate, dy = own
    _, rows, width = x.shape
    ff = gate.shape[2]
    shape = (3 * width * ff // 4 // LANES, LANES)
    late = [gate, up, down, selectors[0], x, selectors[1], hid, dg, du, dy]
    return pl.pallas_call(
        functools.partial(routed_grads_kernel, expert_count, slot),
        grid_spec=pltpu.PrefetchScalarGridSpec(
            num_scalar_prefetch=1,
            grid=(1,),
            in_specs=[
                pl.BlockSpec((1, rows, LANES), lambda i, _: (slot, 0, 0), pipeline_mode=pl.Buffered(1))
            ]
            + [once(v.shape) for v in far]
            + [once(router.shape)]
            + [pl.BlockSpec(memory_space=pl.ANY)] * len(late),
            out_specs=[once(shape)] * 2,
            scratch_shapes=[pltpu.VMEM((rows, width), BF)] * 2
            + [pltpu.VMEM(v.shape[-2:], BF) for v in late]
            + [pltpu.SemaphoreType.DMA((len(late),))],
        ),
        out_shape=[jax.ShapeDtypeStruct(shape, BF)] * 2,
        compiler_params=pltpu.CompilerParams(vmem_limit_bytes=VMEM_LIMIT),
        cost_estimate=pl.CostEstimate(
            flops=int(COST * (16 * rows * width * ff)),
            bytes_accessed=int(COST * (12 * width * ff + 16 * rows * width)),
            transcendentals=0,
        ),
        name="routed_grads",
    )(ids, row_gate, *far, router, *late)


def finish_kernel(slots, *refs):
    outs = refs[2 * slots :]
    for s in range(slots):
        keep, got = refs[2 * s], refs[2 * s + 1]

        @pl.when(pl.program_id(0) == s)
        def _():
            start = 0
            for out in outs:
                size, columns = out.shape[1:]
                for c in range(columns // LANES):
                    at = slice(start, start + size)
                    out[0, :, c * LANES : (c + 1) * LANES] = keep[at].astype(F32) + got[at].astype(F32)
                    start += size


def finish(pieces, shapes):
    slots = len(pieces)
    return pl.pallas_call(
        functools.partial(finish_kernel, slots),
        grid=(slots,),
        in_specs=[once(v.shape) for piece in pieces for v in piece],
        out_specs=[per_slot(*shape) for shape in shapes],
        out_shape=[jax.ShapeDtypeStruct((slots,) + shape, F32) for shape in shapes],
        compiler_params=pltpu.CompilerParams(vmem_limit_bytes=VMEM_LIMIT),
        name="finish",
    )(*(v for piece in pieces for v in piece))


def rotary(length):
    half = HEAD_DIM // 2
    frequencies = np.exp(np.arange(half, dtype=np.float32) * np.float32(-math.log(10000.0) / half))
    angles = np.arange(length, dtype=np.float32)[:, None] * frequencies.astype(np.float32)[None, :]
    cosine, sine = np.cos(angles), np.sin(angles)
    return (
        np.concatenate([cosine, cosine], 1).astype(np.float32),
        np.concatenate([-sine, sine], 1).astype(np.float32),
    )


def turn(x, cosine, sine):
    return x * cosine + pltpu.roll(x, HEAD_DIM // 2, 1) * sine


def causal_probs(q, k):
    scores = dot_nt(q, k) * (1.0 / math.sqrt(HEAD_DIM))
    row = lax.broadcasted_iota(jnp.int32, scores.shape, 0)
    lane = lax.broadcasted_iota(jnp.int32, scores.shape, 1)
    scores = jnp.where(row >= lane, scores, -1e30)
    terms = jnp.exp(scores - jnp.max(scores, -1, keepdims=True))
    return terms / jnp.sum(terms, -1, keepdims=True)


def unit_of(x):
    scale = lax.rsqrt(jnp.mean(x * x, -1, keepdims=True) + epsilon)
    return x * scale, scale


def attention_kernel(
    x_ref, gain1_ref, gain2_ref, cos_ref, sin_ref, wq_ref, wk_ref, wv_ref, wo_ref,
    q_ref, k_ref, v_ref, att_ref, nf_ref, residual_ref, ns_ref,
):
    i = pl.program_id(0)

    @pl.when(i == 0)
    def _():
        x = x_ref[...].astype(F32)
        nf_ref[...] = (unit_of(x)[0] * gain1_ref[...][None]).astype(BF)
        residual_ref[...] = x

    nf = nf_ref[...]
    q_all, k_all, v_all = dot_nn(nf, wq_ref[...]), dot_nn(nf, wk_ref[...]), dot_nn(nf, wv_ref[...])
    cosine, sine = cos_ref[...], sin_ref[...]
    v_ref[...] = v_all.astype(BF)
    for h in range(q_ref.shape[1] // HEAD_DIM):
        at = slice(h * HEAD_DIM, (h + 1) * HEAD_DIM)
        q = turn(q_all[:, at], cosine, sine).astype(BF)
        k = turn(k_all[:, at], cosine, sine).astype(BF)
        q_ref[:, at] = q
        k_ref[:, at] = k
        att_ref[:, at] = dot_nn(causal_probs(q, k).astype(BF), v_all[:, at].astype(BF)).astype(BF)
    residual_ref[...] += dot_nn(att_ref[...], wo_ref[...])

    @pl.when(i == pl.num_programs(0) - 1)
    def _():
        ns_ref[...] = (unit_of(residual_ref[...])[0] * gain2_ref[...][None]).astype(BF)


def attention(x, gain1, gain2, cosine, sine, wq, wk, wv, wo):
    length, width = x.shape
    step = 2 * HEAD_DIM
    columns = lambda rows: pl.BlockSpec((rows, step), lambda i: (0, i))
    low = jax.ShapeDtypeStruct((length, width), BF)
    return pl.pallas_call(
        attention_kernel,
        grid=(width // step,),
        in_specs=[
            whole((length, width)),
            whole((width,)),
            whole((width,)),
            whole(cosine.shape),
            whole(sine.shape),
            columns(width),
            columns(width),
            columns(width),
            pl.BlockSpec((step, width), lambda i: (i, 0)),
        ],
        out_specs=[columns(length)] * 4 + [whole((length, width))] * 3,
        out_shape=[low] * 5 + [jax.ShapeDtypeStruct((length, width), F32), low],
        compiler_params=pltpu.CompilerParams(vmem_limit_bytes=VMEM_LIMIT),
        cost_estimate=pl.CostEstimate(
            flops=int(COST * 8 * length * width * width), bytes_accessed=int(COST * 8 * width * width), transcendentals=0
        ),
        name="attention",
    )(x, gain1, gain2, cosine, sine, wq, wk, wv, wo)


def backward_kernel(
    expert_count,
    x_ref, dy_ref, residual_ref, ns_ref, shared_ref, router_t_ref, gain1_ref, gain2_ref,
    cos_ref, sin_ref, q_ref, k_ref, v_ref, wq_ref, wk_ref, wv_ref, wo_ref, *refs,
):
    parts = refs[0]
    qk_ref, rest_ref, grad_ref, branch_ref, d_res_ref, acc_ref = refs[1:]
    i = pl.program_id(0)
    length, width = x_ref.shape
    step = wq_ref.shape[1]
    here = pl.multiple_of(i * step, step)
    gains = slice(2 * length, 2 * length + 16)

    @pl.when(i == 0)
    def _():
        back = parts[0, :length].astype(F32)
        tail = parts[0, length:].astype(F32)
        for p in range(1, parts.shape[0]):
            back += parts[p, :length].astype(F32)
            tail += parts[p, length:].astype(F32)
        blocks = router_t_ref.shape[0] // 16
        d_probs = jnp.concatenate([tail[:, b * length : (b + 1) * length] for b in range(blocks)], 0)
        logits = dot_nt(router_t_ref[...], ns_ref[...])
        row = lax.broadcasted_iota(jnp.int32, logits.shape, 0)
        logits = jnp.where(row < expert_count, logits, -1e30)
        terms = jnp.exp(logits - jnp.max(logits, 0, keepdims=True))
        probs = terms / jnp.sum(terms, 0, keepdims=True)
        d_logits = probs * (d_probs - jnp.sum(probs * d_probs, 0, keepdims=True))
        d_logits = jnp.where(row < expert_count, d_logits, 0.0).astype(BF)
        rest_ref[2 * length + 16 :] = jnp.zeros((d_logits.shape[0], width), BF)
        rest_ref[2 * length + 16 :, :length] = d_logits
        d_normed = shared_ref[...] + back + dot_tn(d_logits, router_t_ref[...])
        unit, scale = unit_of(residual_ref[...])
        c = d_normed * gain2_ref[...][None]
        gain_row = jnp.sum(d_normed * unit, 0, keepdims=True)
        which = lax.broadcasted_iota(jnp.int32, (16, width), 0)
        rest_ref[gains] = jnp.where(which == 1, gain_row, 0.0).astype(BF)
        d_res = dy_ref[...].astype(F32) + scale * (c - unit * jnp.mean(c * unit, -1, keepdims=True))
        d_res_ref[...] = d_res
        branch_ref[...] = d_res.astype(BF)
        rest_ref[length : 2 * length] = d_res.astype(BF)
        acc_ref[...] = jnp.zeros_like(acc_ref)

    cosine, sine = cos_ref[...], -sin_ref[...]
    att_scale = 1.0 / math.sqrt(HEAD_DIM)
    d_att_all = dot_nt(branch_ref[...], wo_ref[...]).astype(BF)
    d_q, d_k, d_v = [], [], []
    for h in range(step // HEAD_DIM):
        at = slice(h * HEAD_DIM, (h + 1) * HEAD_DIM)
        q, k, v, d_attended = q_ref[:, at], k_ref[:, at], v_ref[:, at], d_att_all[:, at]
        probs = causal_probs(q, k)
        d_att = dot_nt(d_attended, v)
        d_scores = (probs * (d_att - jnp.sum(probs * d_att, -1, keepdims=True))).astype(BF)
        d_q.append(turn(dot_nn(d_scores, k) * att_scale, cosine, sine).astype(BF))
        d_k.append(turn(dot_tn(d_scores, q) * att_scale, cosine, sine).astype(BF))
        d_v.append(dot_tn(probs.astype(BF), d_attended).astype(BF))
    d_q, d_k, d_v = (jnp.concatenate(v, 1) for v in (d_q, d_k, d_v))
    qk_ref[:length, pl.ds(here, step)] = d_q
    qk_ref[length:, pl.ds(here, step)] = d_k
    rest_ref[:length, pl.ds(here, step)] = d_v
    acc_ref[...] += dot_nt(d_q, wq_ref[...]) + dot_nt(d_k, wk_ref[...]) + dot_nt(d_v, wv_ref[...])

    @pl.when(i == pl.num_programs(0) - 1)
    def _():
        unit, scale = unit_of(x_ref[...].astype(F32))
        d_normed = acc_ref[...]
        c = d_normed * gain1_ref[...][None]
        gain_row = jnp.sum(d_normed * unit, 0, keepdims=True)
        which = lax.broadcasted_iota(jnp.int32, (16, width), 0)
        rest_ref[gains] = jnp.where(which == 0, gain_row, rest_ref[gains].astype(F32)).astype(BF)
        grad_ref[...] = d_res_ref[...] + scale * (c - unit * jnp.mean(c * unit, -1, keepdims=True))


def backward(
    x, dy, residual, ns, shared, router_t, gain1, gain2, cosine, sine,
    q, k, v, wq, wk, wv, wo, parts, expert_count,
):
    length, width = x.shape
    step = 2 * HEAD_DIM
    columns = lambda rows: pl.BlockSpec((rows, step), lambda i: (0, i))
    tall = whole((length, width))
    return pl.pallas_call(
        functools.partial(backward_kernel, expert_count),
        grid=(width // step,),
        in_specs=[tall] * 5
        + [whole(router_t.shape), whole((width,)), whole((width,))]
        + [whole(cosine.shape)] * 2
        + [columns(length)] * 3
        + [columns(width)] * 3
        + [pl.BlockSpec((step, width), lambda i: (i, 0))]
        + [whole(parts.shape)],
        out_specs=[
            whole((2 * length, width)),
            whole((2 * length + 16 + router_t.shape[0], width)),
            tall,
        ],
        scratch_shapes=[
            pltpu.VMEM((length, width), BF),
            pltpu.VMEM((length, width), F32),
            pltpu.VMEM((length, width), F32),
        ],
        out_shape=[
            jax.ShapeDtypeStruct((2 * length, width), BF),
            jax.ShapeDtypeStruct((2 * length + 16 + router_t.shape[0], width), BF),
            jax.ShapeDtypeStruct((length, width), F32),
        ],
        compiler_params=pltpu.CompilerParams(vmem_limit_bytes=VMEM_LIMIT),
        cost_estimate=pl.CostEstimate(
            flops=int(COST * 8 * length * width * width), bytes_accessed=int(COST * 8 * width * width), transcendentals=0
        ),
        name="backward",
    )(
        x, dy, residual, ns, shared, router_t, gain1, gain2, cosine, sine,
        q, k, v, wq, wk, wv, wo, parts,
    )


def call(kernel, name, outs, *args, scalars=0):
    return pl.pallas_call(
        kernel,
        in_specs=[pl.BlockSpec(memory_space=pltpu.SMEM)] * scalars
        + [pl.BlockSpec(memory_space=pltpu.VMEM)] * (len(args) - scalars),
        out_specs=[pl.BlockSpec(memory_space=pltpu.VMEM)] * len(outs),
        out_shape=[jax.ShapeDtypeStruct(*o) for o in outs],
        compiler_params=pltpu.CompilerParams(vmem_limit_bytes=VMEM_LIMIT),
        cost_estimate=pl.CostEstimate(flops=1, bytes_accessed=1, transcendentals=0),
        name=name,
    )(*args)


def shared_kernel(ns_ref, dy_ref, gate_ref, up_ref, down_ref, cat_ref, result_ref, back_ref):
    ns, dy = ns_ref[...], dy_ref[...]
    width, ff = gate_ref.shape
    g = dot_nn(ns, gate_ref[...])
    u = dot_nn(ns, up_ref[...])
    sig = jax.nn.sigmoid(g)
    act = g * sig
    hid = (act * u).astype(BF)
    dh = dot_nt(dy, down_ref[...])
    dg = (dh * u * sig * (1.0 + g * (1.0 - sig))).astype(BF)
    du = (dh * act).astype(BF)
    result_ref[...] = dot_nn(hid, down_ref[...])
    back_ref[...] = dot_nt(dg, gate_ref[...]) + dot_nt(du, up_ref[...])
    for i, v in enumerate((dg, du, hid)):
        cat_ref[:, i * ff : (i + 1) * ff] = v
    cat_ref[:, 3 * ff : 3 * ff + width] = ns
    cat_ref[:, 3 * ff + width :] = dy


def shared_grads_kernel(ff, width, cat_ref, other_ref, order_d_ref, order_f_ref, su_send, su_keep, sd_send, sd_keep):
    pair = jnp.concatenate([cat_ref[...], other_ref[...]], 0)
    ns_t = dot_nt(order_d_ref[...], pair[:, 3 * ff : 3 * ff + width]).astype(BF)
    hid_t = dot_nt(order_f_ref[...], pair[:, 2 * ff : 3 * ff]).astype(BF)
    su = dot_nn(ns_t, pair[:, : 2 * ff]).astype(BF)
    sd = dot_nn(hid_t, pair[:, 3 * ff + width :]).astype(BF)
    for value, send, keep in ((su, su_send, su_keep), (sd, sd_send, sd_keep)):
        n = send.shape[1]
        for i in range(2):
            send[i] = value[i * n : (i + 1) * n]
            keep[i] = value[(2 + i) * n : (3 + i) * n]


def lefts_kernel(mine_ref, other_ref, order_a_ref, order_b_ref, a_ref, v_ref, o_ref):
    sets = lambda i, j: jnp.concatenate([mine_ref[i], other_ref[i], mine_ref[j], other_ref[j]], 0)
    a_ref[...] = dot_nt(order_a_ref[...], sets(0, 2)).astype(BF)
    v_ref[...] = dot_nt(order_b_ref[...], sets(0, 3)).astype(BF)
    o_ref[...] = dot_nt(order_b_ref[...], sets(1, 4)).astype(BF)


def last_grads_kernel(
    length, at_ns, z_ref, mine_ref, other_ref, rest_ref, rest_other_ref, qx_ref, qxo_ref, by_ref, byo_ref, a_ref, v_ref, o_ref,
    ns_ref, cat_other_ref, ns_y_ref, ns_yo_ref, order_b_ref,
    a_send, a_keep, b_send, b_keep,
):
    width = mine_ref.shape[1]
    half = a_send.shape[0]
    join = lambda *v: jnp.concatenate(v, 0)

    def put(value, keep, send, columns):
        keep[:, columns] = value[:half].astype(BF)
        send[:, columns] = value[half:].astype(BF)

    for i in range(2):
        at = slice(i * length, (i + 1) * length)
        tokens = join(mine_ref[at], other_ref[at], qx_ref[at], qxo_ref[at])
        put(dot_nn(a_ref[...], tokens), a_keep, a_send, slice(i * width, (i + 1) * width))
        tokens = join(rest_ref[at], rest_other_ref[at], by_ref[at], byo_ref[at])
        left = (v_ref, o_ref)[i]
        put(dot_nn(left[...], tokens), b_keep, b_send, slice(i * width, (i + 1) * width))
    start = 2 * length
    refs = ((rest_ref, start), (rest_other_ref, start), (by_ref, start), (byo_ref, start))
    gains = sum(ref[i : i + 16].astype(F32) for ref, i in refs).astype(BF)
    logits = jnp.concatenate([ref[i + 16 :, :length] for ref, i in refs], 1)
    ns = join(
        ns_ref[...], cat_other_ref[:, at_ns : at_ns + width], ns_y_ref[z_ref[0]], ns_yo_ref[z_ref[0]]
    )
    left_r = dot_nt(order_b_ref[...], ns).astype(BF)
    small = jnp.concatenate(
        [dot_nt(left_r, logits), dot_nt(order_b_ref[...], gains)], 1
    )
    small = jnp.concatenate([small, jnp.zeros((2 * half, LANES - small.shape[1]), F32)], 1)
    put(small, b_keep, b_send, slice(2 * width, 2 * width + LANES))


def after(value, *earlier):
    return lax.optimization_barrier((value, earlier))[0]


def shards(
    tokens,
    cotangent,
    routes,
    expert_at,
    norm1_gain,
    w_query,
    w_key,
    w_value,
    w_out,
    norm2_gain,
    w_router,
    shared_gate,
    shared_up,
    shared_down,
    routed_gate,
    routed_up,
    routed_down,
):
    length, model_width = tokens.shape
    expert_count = w_router.shape[1]
    slot_dev = routed_gate.shape[0]
    n_ex = lax.axis_size("expert")
    n_dp = lax.axis_size("dp")
    capacity = (length * TOP * 5 // (4 * expert_count) + 7) // 8 * 8
    my_dp, my_ex = lax.axis_index("dp"), lax.axis_index("expert")
    n_z = n_ex // 2
    w = model_width
    rows = w // (n_dp * n_ex)
    over_core = lambda v: partner(v, "expert", 1)
    order_d = rows_for(w, (2, 3, 0, 1))
    order_a, order_b = rows_for(w, (0, 2)), rows_for(w, (0, 1))

    routes_t = jnp.pad(routes.T.astype(BF), ((0, 16 - TOP), (0, 0)), constant_values=-1)
    routes_t = jnp.pad(routes_t, ((0, 0), (0, w - length)))
    spread = lambda v: exchange_z(jnp.broadcast_to(v[None], (n_z,) + v.shape))
    early = spread(jnp.concatenate([cotangent, routes_t], 0))
    cosine, sine = (jnp.asarray(t) for t in rotary(length))
    gain1, gain2 = norm1_gain, norm2_gain
    queries, key_rows, value_rows, attended, normed_first, residual, normed_second = attention(
        tokens, gain1, gain2, cosine, sine, w_query, w_key, w_value, w_out
    )
    ff = shared_gate.shape[1]
    from_shared, shared_result, shared_back = call(
        shared_kernel, "shared",
        [((length, 3 * ff + 2 * w), BF), ((length, w), F32), ((length, w), F32)],
        normed_second, cotangent, shared_gate, shared_up, shared_down,
    )
    my_z = my_ex // 2
    first_x = partner(normed_first, "dp", 1)
    first_y = partner(jnp.stack([normed_first, attended]), "dp", 2)
    selectors = [(keep_rows(w, q), keep_rows(ff, q)) for q in (2, 1)]
    order_f = rows_for(ff, (1, 3, 0, 2))
    ns = spread(
        after(normed_second, early, from_shared, first_x, first_y, selectors, order_a, order_b, order_d, order_f)
    )
    from_other = over_core(from_shared)
    part_d, part_f = w // (2 * n_dp), ff // (2 * n_dp)
    su_send, su_keep, sd_send, sd_keep = call(
        functools.partial(shared_grads_kernel, ff, w), "shared_grads",
        [((2, part_d, 2 * ff), BF)] * 2 + [((2, part_f, w), BF)] * 2,
        from_shared, from_other, order_d, order_f,
    )
    early_other = over_core(early)
    early_x, early_y = partner(early, "dp", 1), partner(early, "dp", 2)

    my_expert = lax.dynamic_slice_in_dim(expert_at, my_ex * slot_dev, slot_dev)
    router_wide = jnp.pad(w_router, ((0, 0), (0, LANES - expert_count)))
    pick, dh_raw, dy_rows = prepare(my_expert, (early, early_other), routed_down, capacity)
    ns = after(ns, pick, dh_raw, early_x, early_y, su_send)
    ns_other = over_core(ns)
    back_mine, back_other, hid, dg, du, x_rows, row_gate = experts(
        my_expert, (ns, ns_other), pick, dh_raw, routed_gate, routed_up, router_wide, expert_count
    )
    back_sum = plus(back_mine, over_core(back_other))
    back = exchange_z(back_sum)
    ns_far, su_send, sd_send, early_x, early_y = after((ns, su_send, sd_send, early_x, early_y), back_sum)
    early_x_other, early_y_other = over_core(early_x), over_core(early_y)
    su_got, sd_got = partner(su_send, "dp", 2), partner(sd_send, "dp", 1)
    su, sd = plus(su_keep, su_got), plus(sd_keep, sd_got)
    su_sum, sd_sum = su, sd
    su_last, sd_last = partner(su[1], "dp", 1), partner(sd[1], "dp", 2)
    su, sd = plus(su[0], su_last), plus(sd[0], sd_last)

    lefts = jnp.concatenate([normed_first[None], attended[None], first_x[None], first_y])
    lefts = after(lefts, back_sum)
    lefts_other = over_core(lefts)
    left_shape = ((w // 4, 4 * length), BF)
    left_a, left_v, left_o = call(
        lefts_kernel, "lefts", [left_shape] * 3, lefts, lefts_other, order_a, order_b,
    )
    ns_y = partner(after(ns_far, su_got, left_a), "dp", 2)
    combined_mine, combined_other = combine(after(hid, early_x_other, early_y_other), row_gate, pick, routed_down)
    ns_x = partner(after(ns_far, combined_mine), "dp", 1)
    combined = plus(combined_mine, over_core(combined_other))
    back = after(back, combined, left_a, su_sum, sd_sum)
    combined = exchange_z(after(combined, back))

    high = -(-expert_count // 16) * 16
    router_t = jnp.pad(w_router.T, ((0, high - expert_count), (0, 0)))
    d_qk, d_rest, grad_inputs = backward(
        tokens, cotangent, residual, normed_second, shared_back, router_t, gain1, gain2, cosine, sine,
        queries, key_rows, value_rows, w_query, w_key, w_value, w_out, back, expert_count,
    )

    qk_x, b_y = partner(d_qk, "dp", 1), partner(d_rest, "dp", 2)
    far_x = [ns_x, over_core(after(ns_x, d_qk)), early_x, early_x_other]

    far = [far_x]

    def slot_grads(slot, last_dg):
        return routed_grads(
            slot, selectors[slot % 2], my_expert, [x_rows, last_dg, du, hid, row_gate, dy_rows],
            far[slot % 2], [routed_gate, routed_up, routed_down], router_wide, expert_count,
        )

    routed = [slot_grads(0, after(dg, d_qk, ns_y))]
    d_qk, d_rest, qk_x, b_y = after((d_qk, d_rest, qk_x, b_y), routed[0], su_last, sd_last)
    qk_other, rest_other = over_core(d_qk), over_core(d_rest)
    far_y = [ns_y, over_core(after(ns_y, routed[0])), early_y, early_y_other]
    far.append(far_y)
    qk_x_other, b_y_other = over_core(qk_x), over_core(b_y)
    a_send, a_keep, b_send, b_keep = call(
        functools.partial(last_grads_kernel, length, 3 * ff), "last_grads",
        [((w // 8, 2 * w), BF)] * 2 + [((w // 8, 2 * w + LANES), BF)] * 2,
        my_z[None], d_qk, qk_other, d_rest, rest_other, qk_x, qk_x_other, b_y, b_y_other, left_a, left_v, left_o,
        normed_second, from_other, far_y[0], far_y[1], order_b, scalars=1,
    )
    a_got, b_got = partner(a_send, "dp", 2), partner(b_send, "dp", 1)

    routed += [slot_grads(slot, after(dg, a_send)) for slot in range(1, slot_dev)]
    pieces = [
        (keep, partner(after(send, a_send), "dp", 2 if slot % 2 == 0 else 1))
        for slot, (send, keep) in enumerate(routed)
    ]
    a_got = after(a_got, routed)
    last = jnp.concatenate([plus(a_keep, a_got), plus(b_keep, b_got)], -1).reshape(n_z, rows, -1)

    sd = jnp.pad(sd.reshape(n_z, -1, w), ((0, 0), (0, (w - ff) // (n_dp * n_ex)), (0, 0)))
    grad_shared = exchange_z(after(jnp.concatenate([su.reshape(n_z, rows, -1), sd], -1), combined))
    last = exchange_z(after(last, grad_shared))
    grad_shared, combined = after((grad_shared, combined), last)
    last, grad_shared = total(list(last)), total(list(grad_shared))
    output = (residual + shared_result + total(list(combined))).astype(BF)
    grad_rgate, grad_rup, grad_rdown = finish(pieces, [(w // n_dp, ff), (w // n_dp, ff), (ff // n_dp, w)])
    return (
        output,
        grad_inputs,
        last[:, 4 * w + high],
        last[:, :w],
        last[:, w : 2 * w],
        last[:, 2 * w : 3 * w],
        last[:, 3 * w : 4 * w],
        last[:, 4 * w + high + 1],
        last[:, 4 * w : 4 * w + expert_count],
        grad_shared[:, :ff],
        grad_shared[:, ff : 2 * ff],
        grad_shared[: ff // (n_dp * n_ex), 2 * ff :],
        grad_rgate,
        grad_rup,
        grad_rdown,
    )


def solution(mesh):
    placed = (
        P(("dp", "expert"), None),
        P(("dp", "expert"), None),
        P(("dp", "expert"), None),
        P(),
        P(),
        P(),
        P(),
        P(),
        P(),
        P(),
        P(),
        P(),
        P(),
        P(),
        P("expert", None, None),
        P("expert", None, None),
        P("expert", None, None),
    )
    return jax.shard_map(
        shards,
        mesh=mesh,
        in_specs=placed,
        out_specs=(
            P(("dp", "expert"), None),
            P(("dp", "expert"), None),
            P(("dp", "expert")),
            P(("dp", "expert"), None),
            P(("dp", "expert"), None),
            P(("dp", "expert"), None),
            P(("dp", "expert"), None),
            P(("dp", "expert")),
            P(("dp", "expert"), None),
            P(("dp", "expert"), None),
            P(("dp", "expert"), None),
            P(("dp", "expert"), None),
            P("expert", "dp", None),
            P("expert", "dp", None),
            P("expert", "dp", None),
        ),
        check_vma=False,
    )
```

```python
import functools
import math

import jax
import jax.numpy as jnp
import numpy as np
from jax import lax
from jax.experimental import pallas as pl
from jax.experimental.pallas import tpu as pltpu
from jax.sharding import PartitionSpec as P

HEADS = 10
HEAD_DIM = 128
TOP = 6
LANES = 128
epsilon = 1e-06
BF = jnp.bfloat16
F32 = jnp.float32
VMEM_LIMIT = 60 * 2**20
COST = 4


def partner(v, axis, mask):
    n = lax.axis_size(axis)
    return lax.ppermute(v, axis, [(i, i ^ mask) for i in range(n)])


def plus(a, b):
    return (a.astype(F32) + b.astype(F32)).astype(BF)


def exchange_z(s):
    n_z = lax.axis_size("expert") // 2
    groups = [[2 * z + c for z in range(n_z)] for c in (0, 1)]
    return lax.all_to_all(s, "expert", 0, 0, tiled=True, axis_index_groups=groups)


def total(blocks):
    out = blocks[0].astype(F32)
    for b in blocks[1:]:
        out = out + b.astype(F32)
    return out


def rows_for(d, blocks):
    n_dp, n_ex = lax.axis_size("dp"), lax.axis_size("expert")
    rows = d // (n_dp * n_ex)
    n_z = n_ex // 2
    my_dp, my_core = lax.axis_index("dp"), lax.axis_index("expert") % 2
    at = np.arange(len(blocks) * n_z * rows, dtype=np.int32)
    block_dp = jnp.asarray(np.repeat(np.array(blocks, np.int32), n_z * rows)) ^ my_dp
    block = (block_dp * n_z + jnp.asarray(at // rows % n_z)) * 2 + my_core
    source = block * rows + jnp.asarray(at % rows)
    return (source[:, None] == jnp.arange(d, dtype=jnp.int32)[None, :]).astype(BF)


def dot_nn(a, b):
    return lax.dot_general(a, b, (((1,), (0,)), ((), ())), preferred_element_type=F32)


def dot_nt(a, b):
    return lax.dot_general(a, b, (((1,), (1,)), ((), ())), preferred_element_type=F32)


def dot_tn(a, b):
    return lax.dot_general(a, b, (((0,), (0,)), ((), ())), preferred_element_type=F32)


def picks(routes_t, expert, length, capacity):
    hit = jnp.where(routes_t.astype(F32) == expert.astype(F32), 1.0, 0.0)
    member = jnp.sum(hit, 0, keepdims=True)
    a = lax.broadcasted_iota(jnp.int32, (length, length), 0)
    b = lax.broadcasted_iota(jnp.int32, (length, length), 1)
    earlier = jnp.where(a < b, 1.0, 0.0).astype(BF)
    place = dot_nn(jnp.broadcast_to(member, (16, length)).astype(BF), earlier)[:1]
    row = lax.broadcasted_iota(jnp.int32, (capacity, length), 0).astype(F32)
    return jnp.where((place == row) & (member > 0.5), 1.0, 0.0).astype(BF)


def gates_of(x, router, expert, expert_count):
    logits = dot_nn(x, router)
    lane = lax.broadcasted_iota(jnp.int32, logits.shape, 1)
    logits = jnp.where(lane < expert_count, logits, -1e30)
    terms = jnp.exp(logits - jnp.max(logits, -1, keepdims=True))
    probs = terms / jnp.sum(terms, -1, keepdims=True)
    return jnp.sum(jnp.where(lane == expert, probs, 0.0), -1, keepdims=True)


def whole(shape):
    return pl.BlockSpec(shape, lambda *_: (0,) * len(shape))


def prepare_kernel(ids, early_ref, other_ref, down_ref, pick_ref, dh_ref, dy_ref):
    expert = ids[pl.program_id(0)]
    sources = early_ref.shape[0]
    capacity, length = pick_ref.shape[2:]
    for j, ref in enumerate((early_ref, other_ref)):
        for k in range(sources):
            n = j * sources + k
            pick = picks(ref[k, length : length + 16, :length], expert, length, capacity)
            pick_ref[0, n] = pick
            dy_ref[0, n * capacity : (n + 1) * capacity] = dot_nn(pick, ref[k, :length]).astype(BF)
    dh_ref[0] = dot_nt(dy_ref[0], down_ref[0])


def per_slot(*shape):
    return pl.BlockSpec((1,) + shape, lambda s, *_: (s,) + (0,) * len(shape))


def once(shape):
    return pl.BlockSpec(shape, lambda *_: (0,) * len(shape), pipeline_mode=pl.Buffered(1))


def prepare(ids, early, down, capacity):
    sources, length = early[0].shape[0], early[0].shape[1] - 16
    slots, ff, width = down.shape
    rows = 2 * sources * capacity
    return pl.pallas_call(
        prepare_kernel,
        grid_spec=pltpu.PrefetchScalarGridSpec(
            num_scalar_prefetch=1,
            grid=(slots,),
            in_specs=[once(v.shape) for v in early] + [per_slot(ff, width)],
            out_specs=[
                per_slot(2 * sources, capacity, length),
                per_slot(rows, ff),
                per_slot(rows, width),
            ],
        ),
        out_shape=[
            jax.ShapeDtypeStruct((slots, 2 * sources, capacity, length), BF),
            jax.ShapeDtypeStruct((slots, rows, ff), F32),
            jax.ShapeDtypeStruct((slots, rows, width), BF),
        ],
        compiler_params=pltpu.CompilerParams(vmem_limit_bytes=VMEM_LIMIT),
        cost_estimate=pl.CostEstimate(
            flops=1,
            bytes_accessed=1,
            transcendentals=0,
        ),
        name="prepare",
    )(ids, *early, down)


def experts_kernel(
    expert_count, ids, ns0_ref, ns1_ref, pick_ref, dh_ref, gate_ref, up_ref, router_ref,
    back0_ref, back1_ref, hid_ref, dg_ref, du_ref, rows_ref, row_gate_ref, d_rows_ref, probs_ref,
):
    s = pl.program_id(0)
    slots, total_sources, capacity, length = pick_ref.shape
    sources, _, width = ns0_ref.shape
    expert = ids[s]
    sides = [(ns0_ref, back0_ref), (ns1_ref, back1_ref)]
    for n in range(total_sources):
        ns = sides[n // sources][0][n % sources]
        rows_ref[0, n * capacity : (n + 1) * capacity] = dot_nn(pick_ref[s, n], ns).astype(BF)
    x = rows_ref[0]
    row_gate = gates_of(x, router_ref[...], expert, expert_count)
    row_gate_ref[0] = jnp.broadcast_to(row_gate, row_gate_ref.shape[1:])
    g = dot_nn(x, gate_ref[0])
    u = dot_nn(x, up_ref[0])
    sig = jax.nn.sigmoid(g)
    act = g * sig
    hid = (act * u).astype(BF)
    hid_ref[0] = hid
    raw = dh_ref[0]
    d_gate = jnp.sum(hid.astype(F32) * raw, -1, keepdims=True)
    dh = raw * row_gate
    dg = (dh * u * sig * (1.0 + g * (1.0 - sig))).astype(BF)
    du = (dh * act).astype(BF)
    dg_ref[0] = dg
    du_ref[0] = du
    d_rows_ref[s] = (dot_nt(dg, gate_ref[0]) + dot_nt(du, up_ref[0])).astype(BF)

    @pl.when(s == 0)
    def _():
        probs_ref[...] = jnp.zeros_like(probs_ref)

    parts = probs_ref.shape[2] // length
    row = lax.broadcasted_iota(jnp.int32, (16, length), 0)
    for n in range(total_sources):
        column = d_gate[n * capacity : (n + 1) * capacity]
        token = jnp.sum(pick_ref[s, n].astype(F32) * column, 0, keepdims=True)
        for b in range(parts):
            probs_ref[n, :, b * length : (b + 1) * length] += jnp.where(
                row == expert - 16 * b, token, 0.0
            )

    @pl.when(s == slots - 1)
    def _():
        wide = parts * length
        for n in range(total_sources):
            back, k = sides[n // sources][1], n % sources
            at = slice(n * capacity, (n + 1) * capacity)
            pick = jnp.concatenate([pick_ref[i, n] for i in range(slots)], 0)
            d_rows = jnp.concatenate([d_rows_ref[i, at] for i in range(slots)], 0)
            back[k, :length] = dot_tn(pick, d_rows).astype(BF)
            back[k, length:, :wide] = probs_ref[n].astype(BF)
            if wide < width:
                back[k, length:, wide:] = jnp.zeros((16, width - wide), BF)


def experts(ids, ns, pick, dh, gate, up, router, expert_count):
    sources, length, width = ns[0].shape
    slots, _, capacity, _ = pick.shape
    ff = gate.shape[2]
    rows = 2 * sources * capacity
    wide = -(-expert_count // 16) * length
    back = (sources, length + 16, width)
    return pl.pallas_call(
        functools.partial(experts_kernel, expert_count),
        grid_spec=pltpu.PrefetchScalarGridSpec(
            num_scalar_prefetch=1,
            grid=(slots,),
            in_specs=[
                once(ns[0].shape),
                once(ns[1].shape),
                once(pick.shape),
                per_slot(rows, ff),
                per_slot(width, ff),
                per_slot(width, ff),
                once(router.shape),
            ],
            out_specs=[
                once(back),
                once(back),
                per_slot(rows, ff),
                per_slot(rows, ff),
                per_slot(rows, ff),
                per_slot(rows, width),
                per_slot(rows, LANES),
            ],
            scratch_shapes=[
                pltpu.VMEM((slots, rows, width), BF),
                pltpu.VMEM((2 * sources, 16, wide), F32),
            ],
        ),
        out_shape=[jax.ShapeDtypeStruct(back, BF)] * 2
        + [jax.ShapeDtypeStruct((slots, rows, ff), BF)] * 3
        + [
            jax.ShapeDtypeStruct((slots, rows, width), BF),
            jax.ShapeDtypeStruct((slots, rows, LANES), F32),
        ],
        compiler_params=pltpu.CompilerParams(vmem_limit_bytes=VMEM_LIMIT),
        cost_estimate=pl.CostEstimate(
            flops=int(COST * (8 * slots * rows * width * ff)),
            bytes_accessed=int(COST * (slots * ff * (width * 4 + rows * 6))),
            transcendentals=slots * rows * ff,
        ),
        name="experts",
    )(ids, *ns, pick, dh, gate, up, router)


def combine_kernel(hid_ref, row_gate_ref, pick_ref, down_ref, mine_ref, other_ref, scaled_ref):
    s = pl.program_id(0)
    slots, sources, capacity, length = pick_ref.shape
    result = dot_nn(hid_ref[0], down_ref[0]).astype(BF)
    scaled_ref[s] = (result.astype(F32) * row_gate_ref[0, :, :1]).astype(BF)

    @pl.when(s == slots - 1)
    def _():
        for n in range(sources):
            at = slice(n * capacity, (n + 1) * capacity)
            pick = jnp.concatenate([pick_ref[i, n] for i in range(slots)], 0)
            scaled = jnp.concatenate([scaled_ref[i, at] for i in range(slots)], 0)
            out = (mine_ref, other_ref)[n // (sources // 2)]
            out[n % (sources // 2)] = dot_tn(pick, scaled).astype(BF)


def combine(hid, row_gate, pick, down):
    slots, sources, capacity, length = pick.shape
    _, ff, width = down.shape
    rows = sources * capacity
    out = (sources // 2, length, width)
    return pl.pallas_call(
        combine_kernel,
        grid=(slots,),
        in_specs=[per_slot(rows, ff), per_slot(rows, LANES), once(pick.shape), per_slot(ff, width)],
        out_specs=[once(out)] * 2,
        scratch_shapes=[pltpu.VMEM((slots, rows, width), BF)],
        out_shape=[jax.ShapeDtypeStruct(out, BF)] * 2,
        compiler_params=pltpu.CompilerParams(vmem_limit_bytes=VMEM_LIMIT),
        cost_estimate=pl.CostEstimate(
            flops=int(COST * (4 * slots * rows * width * (ff + length))),
            bytes_accessed=int(COST * (slots * ff * (width * 2 + rows * 2))),
            transcendentals=0,
        ),
        name="combine",
    )(hid, row_gate, pick, down)


def keep_rows(size, second):
    mine = lax.axis_index("dp")
    i = np.arange(size // 4, dtype=np.int32)
    source = jnp.concatenate([(mine ^ second) * (size // 4) + i, mine * (size // 4) + i])
    return (source[:, None] == jnp.arange(size, dtype=jnp.int32)[None, :]).astype(BF)


def routed_grads_kernel(
    expert_count, slot, ids, row_gate_ref, ns0_ref, ns1_ref, early0_ref, early1_ref, router_ref, *refs,
):
    late, (send_ref, keep_ref, far_x, far_dy), bufs, sems = refs[:10], refs[10:14], refs[14:24], refs[24]
    copies = []
    for i, (ref, buf) in enumerate(zip(late, bufs)):
        source = ref.at[slot] if len(ref.shape) == 3 else ref
        copies.append(pltpu.make_async_copy(source, buf, sems.at[i]))
    for copy in copies:
        copy.start()
    gate_ref, up_ref, down_ref, sel_d_ref, x_ref, sel_f_ref, hid_ref, dg_ref, du_ref, dy_ref = bufs
    expert = ids[slot]
    sources, length, width = ns0_ref.shape
    rows = far_x.shape[0]
    capacity = rows // (2 * sources)
    for j, (ns, early) in enumerate(((ns0_ref, early0_ref), (ns1_ref, early1_ref))):
        for k in range(sources):
            pick = picks(early[k, length:, :length], expert, length, capacity)
            at = slice((j * sources + k) * capacity, (j * sources + k + 1) * capacity)
            far_x[at] = dot_nn(pick, ns[k]).astype(BF)
            far_dy[at] = dot_nn(pick, early[k, :length]).astype(BF)
    x = far_x[...]
    row_gate = gates_of(x, router_ref[...], expert, expert_count)
    d_far = (far_dy[...].astype(F32) * row_gate).astype(BF)
    copies[0].wait()
    g = dot_nn(x, gate_ref[...])
    copies[1].wait()
    u = dot_nn(x, up_ref[...])
    sig = jax.nn.sigmoid(g)
    act = g * sig
    hid = (act * u).astype(BF)
    copies[2].wait()
    dh = dot_nt(d_far, down_ref[...])
    dg = (dh * u * sig * (1.0 + g * (1.0 - sig))).astype(BF)
    du = (dh * act).astype(BF)
    for copy in copies[3:]:
        copy.wait()
    x_t = dot_nt(sel_d_ref[...], x).astype(BF)
    x_own = dot_nt(sel_d_ref[...], x_ref[...]).astype(BF)
    hid_t = dot_nt(sel_f_ref[...], hid).astype(BF)
    hid_own = dot_nt(sel_f_ref[...], hid_ref[...]).astype(BF)
    d_own = (dy_ref[...].astype(F32) * row_gate_ref[0, :, :1]).astype(BF)
    start = 0
    for value in (
        dot_nn(x_own, dg_ref[...]) + dot_nn(x_t, dg),
        dot_nn(x_own, du_ref[...]) + dot_nn(x_t, du),
        dot_nn(hid_own, d_own) + dot_nn(hid_t, d_far),
    ):
        size = value.shape[0] // 2
        for c in range(value.shape[1] // LANES):
            columns = value[:, c * LANES : (c + 1) * LANES].astype(BF)
            send_ref[start : start + size] = columns[:size]
            keep_ref[start : start + size] = columns[size:]
            start += size


def routed_grads(slot, selectors, ids, own, far, weights, router, expert_count):
    gate, up, down = weights
    x, dg, du, hid, row_gate, dy = own
    _, rows, width = x.shape
    ff = gate.shape[2]
    shape = (3 * width * ff // 4 // LANES, LANES)
    late = [gate, up, down, selectors[0], x, selectors[1], hid, dg, du, dy]
    return pl.pallas_call(
        functools.partial(routed_grads_kernel, expert_count, slot),
        grid_spec=pltpu.PrefetchScalarGridSpec(
            num_scalar_prefetch=1,
            grid=(1,),
            in_specs=[
                pl.BlockSpec((1, rows, LANES), lambda i, _: (slot, 0, 0), pipeline_mode=pl.Buffered(1))
            ]
            + [once(v.shape) for v in far]
            + [once(router.shape)]
            + [pl.BlockSpec(memory_space=pl.ANY)] * len(late),
            out_specs=[once(shape)] * 2,
            scratch_shapes=[pltpu.VMEM((rows, width), BF)] * 2
            + [pltpu.VMEM(v.shape[-2:], BF) for v in late]
            + [pltpu.SemaphoreType.DMA((len(late),))],
        ),
        out_shape=[jax.ShapeDtypeStruct(shape, BF)] * 2,
        compiler_params=pltpu.CompilerParams(vmem_limit_bytes=VMEM_LIMIT),
        cost_estimate=pl.CostEstimate(
            flops=int(COST * (16 * rows * width * ff)),
            bytes_accessed=int(COST * (12 * width * ff + 16 * rows * width)),
            transcendentals=0,
        ),
        name="routed_grads",
    )(ids, row_gate, *far, router, *late)


def finish_kernel(slots, outs_count, *refs):
    sources, outs = refs[: 2 * slots], refs[2 * slots : 2 * slots + outs_count]
    bufs, sems = refs[2 * slots + outs_count : -1], refs[-1]
    copies = [
        pltpu.make_async_copy(ref, buf, sems.at[i]) for i, (ref, buf) in enumerate(zip(sources, bufs))
    ]

    @pl.when(pl.program_id(0) == 0)
    def _():
        for copy in copies:
            copy.start()

    for s in range(slots):
        keep, got = bufs[2 * s], bufs[2 * s + 1]

        @pl.when(pl.program_id(0) == s)
        def _():
            copies[2 * s].wait()
            copies[2 * s + 1].wait()
            start = 0
            for out in outs:
                size, columns = out.shape[1:]
                for c in range(columns // LANES):
                    at = slice(start, start + size)
                    out[0, :, c * LANES : (c + 1) * LANES] = keep[at].astype(F32) + got[at].astype(F32)
                    start += size


def finish(pieces, shapes):
    slots = len(pieces)
    flat = [v for piece in pieces for v in piece]
    return pl.pallas_call(
        functools.partial(finish_kernel, slots, len(shapes)),
        grid=(slots,),
        in_specs=[pl.BlockSpec(memory_space=pl.ANY)] * len(flat),
        out_specs=[per_slot(*shape) for shape in shapes],
        out_shape=[jax.ShapeDtypeStruct((slots,) + shape, F32) for shape in shapes],
        scratch_shapes=[pltpu.VMEM(v.shape, BF) for v in flat] + [pltpu.SemaphoreType.DMA((len(flat),))],
        compiler_params=pltpu.CompilerParams(vmem_limit_bytes=VMEM_LIMIT),
        name="finish",
    )(*flat)


def rotary(length):
    half = HEAD_DIM // 2
    frequencies = np.exp(np.arange(half, dtype=np.float32) * np.float32(-math.log(10000.0) / half))
    angles = np.arange(length, dtype=np.float32)[:, None] * frequencies.astype(np.float32)[None, :]
    cosine, sine = np.cos(angles), np.sin(angles)
    return (
        np.concatenate([cosine, cosine], 1).astype(np.float32),
        np.concatenate([-sine, sine], 1).astype(np.float32),
    )


def turn(x, cosine, sine):
    return x * cosine + pltpu.roll(x, HEAD_DIM // 2, 1) * sine


def causal_probs(q, k):
    scores = dot_nt(q, k) * (1.0 / math.sqrt(HEAD_DIM))
    row = lax.broadcasted_iota(jnp.int32, scores.shape, 0)
    lane = lax.broadcasted_iota(jnp.int32, scores.shape, 1)
    scores = jnp.where(row >= lane, scores, -1e30)
    terms = jnp.exp(scores - jnp.max(scores, -1, keepdims=True))
    return terms / jnp.sum(terms, -1, keepdims=True)


def unit_of(x):
    scale = lax.rsqrt(jnp.mean(x * x, -1, keepdims=True) + epsilon)
    return x * scale, scale


def attention_kernel(
    x_ref, gain1_ref, gain2_ref, cos_ref, sin_ref, wq_ref, wk_ref, wv_ref, wo_ref,
    q_ref, k_ref, v_ref, att_ref, nf_ref, residual_ref, ns_ref,
):
    i = pl.program_id(0)

    @pl.when(i == 0)
    def _():
        x = x_ref[...].astype(F32)
        nf_ref[...] = (unit_of(x)[0] * gain1_ref[...][None]).astype(BF)
        residual_ref[...] = x

    nf = nf_ref[...]
    q_all, k_all, v_all = dot_nn(nf, wq_ref[...]), dot_nn(nf, wk_ref[...]), dot_nn(nf, wv_ref[...])
    cosine, sine = cos_ref[...], sin_ref[...]
    v_ref[...] = v_all.astype(BF)
    for h in range(q_ref.shape[1] // HEAD_DIM):
        at = slice(h * HEAD_DIM, (h + 1) * HEAD_DIM)
        q = turn(q_all[:, at], cosine, sine).astype(BF)
        k = turn(k_all[:, at], cosine, sine).astype(BF)
        q_ref[:, at] = q
        k_ref[:, at] = k
        att_ref[:, at] = dot_nn(causal_probs(q, k).astype(BF), v_all[:, at].astype(BF)).astype(BF)
    residual_ref[...] += dot_nn(att_ref[...], wo_ref[...])

    @pl.when(i == pl.num_programs(0) - 1)
    def _():
        ns_ref[...] = (unit_of(residual_ref[...])[0] * gain2_ref[...][None]).astype(BF)


def attention(x, gain1, gain2, cosine, sine, wq, wk, wv, wo):
    length, width = x.shape
    step = 5 * HEAD_DIM
    columns = lambda rows: pl.BlockSpec((rows, step), lambda i: (0, i))
    low = jax.ShapeDtypeStruct((length, width), BF)
    return pl.pallas_call(
        attention_kernel,
        grid=(width // step,),
        in_specs=[
            whole((length, width)),
            whole((width,)),
            whole((width,)),
            whole(cosine.shape),
            whole(sine.shape),
            columns(width),
            columns(width),
            columns(width),
            pl.BlockSpec((step, width), lambda i: (i, 0)),
        ],
        out_specs=[columns(length)] * 4 + [whole((length, width))] * 3,
        out_shape=[low] * 5 + [jax.ShapeDtypeStruct((length, width), F32), low],
        compiler_params=pltpu.CompilerParams(vmem_limit_bytes=VMEM_LIMIT),
        cost_estimate=pl.CostEstimate(
            flops=int(COST * 8 * length * width * width), bytes_accessed=int(COST * 8 * width * width), transcendentals=0
        ),
        name="attention",
    )(x, gain1, gain2, cosine, sine, wq, wk, wv, wo)


def backward_kernel(
    expert_count,
    x_ref, dy_ref, residual_ref, ns_ref, shared_ref, router_t_ref, gain1_ref, gain2_ref,
    cos_ref, sin_ref, q_ref, k_ref, v_ref, wq_ref, wk_ref, wv_ref, wo_ref, *refs,
):
    parts = refs[0]
    qk_ref, rest_ref, grad_ref, branch_ref, d_res_ref, acc_ref = refs[1:]
    i = pl.program_id(0)
    length, width = x_ref.shape
    step = wq_ref.shape[1]
    here = pl.multiple_of(i * step, step)
    gains = slice(2 * length, 2 * length + 16)

    @pl.when(i == 0)
    def _():
        back = parts[0, :length].astype(F32)
        tail = parts[0, length:].astype(F32)
        for p in range(1, parts.shape[0]):
            back += parts[p, :length].astype(F32)
            tail += parts[p, length:].astype(F32)
        blocks = router_t_ref.shape[0] // 16
        d_probs = jnp.concatenate([tail[:, b * length : (b + 1) * length] for b in range(blocks)], 0)
        logits = dot_nt(router_t_ref[...], ns_ref[...])
        row = lax.broadcasted_iota(jnp.int32, logits.shape, 0)
        logits = jnp.where(row < expert_count, logits, -1e30)
        terms = jnp.exp(logits - jnp.max(logits, 0, keepdims=True))
        probs = terms / jnp.sum(terms, 0, keepdims=True)
        d_logits = probs * (d_probs - jnp.sum(probs * d_probs, 0, keepdims=True))
        d_logits = jnp.where(row < expert_count, d_logits, 0.0).astype(BF)
        rest_ref[2 * length + 16 :] = jnp.zeros((d_logits.shape[0], width), BF)
        rest_ref[2 * length + 16 :, :length] = d_logits
        d_normed = shared_ref[...] + back + dot_tn(d_logits, router_t_ref[...])
        unit, scale = unit_of(residual_ref[...])
        c = d_normed * gain2_ref[...][None]
        gain_row = jnp.sum(d_normed * unit, 0, keepdims=True)
        which = lax.broadcasted_iota(jnp.int32, (16, width), 0)
        rest_ref[gains] = jnp.where(which == 1, gain_row, 0.0).astype(BF)
        d_res = dy_ref[...].astype(F32) + scale * (c - unit * jnp.mean(c * unit, -1, keepdims=True))
        d_res_ref[...] = d_res
        branch_ref[...] = d_res.astype(BF)
        rest_ref[length : 2 * length] = d_res.astype(BF)
        acc_ref[...] = jnp.zeros_like(acc_ref)

    cosine, sine = cos_ref[...], -sin_ref[...]
    att_scale = 1.0 / math.sqrt(HEAD_DIM)
    d_att_all = dot_nt(branch_ref[...], wo_ref[...]).astype(BF)
    d_q, d_k, d_v = [], [], []
    for h in range(step // HEAD_DIM):
        at = slice(h * HEAD_DIM, (h + 1) * HEAD_DIM)
        q, k, v, d_attended = q_ref[:, at], k_ref[:, at], v_ref[:, at], d_att_all[:, at]
        probs = causal_probs(q, k)
        d_att = dot_nt(d_attended, v)
        d_scores = (probs * (d_att - jnp.sum(probs * d_att, -1, keepdims=True))).astype(BF)
        d_q.append(turn(dot_nn(d_scores, k) * att_scale, cosine, sine).astype(BF))
        d_k.append(turn(dot_tn(d_scores, q) * att_scale, cosine, sine).astype(BF))
        d_v.append(dot_tn(probs.astype(BF), d_attended).astype(BF))
    d_q, d_k, d_v = (jnp.concatenate(v, 1) for v in (d_q, d_k, d_v))
    qk_ref[:length, pl.ds(here, step)] = d_q
    qk_ref[length:, pl.ds(here, step)] = d_k
    rest_ref[:length, pl.ds(here, step)] = d_v
    acc_ref[...] += dot_nt(d_q, wq_ref[...]) + dot_nt(d_k, wk_ref[...]) + dot_nt(d_v, wv_ref[...])

    @pl.when(i == pl.num_programs(0) - 1)
    def _():
        unit, scale = unit_of(x_ref[...].astype(F32))
        d_normed = acc_ref[...]
        c = d_normed * gain1_ref[...][None]
        gain_row = jnp.sum(d_normed * unit, 0, keepdims=True)
        which = lax.broadcasted_iota(jnp.int32, (16, width), 0)
        rest_ref[gains] = jnp.where(which == 0, gain_row, rest_ref[gains].astype(F32)).astype(BF)
        grad_ref[...] = d_res_ref[...] + scale * (c - unit * jnp.mean(c * unit, -1, keepdims=True))


def backward(
    x, dy, residual, ns, shared, router_t, gain1, gain2, cosine, sine,
    q, k, v, wq, wk, wv, wo, parts, expert_count,
):
    length, width = x.shape
    step = 5 * HEAD_DIM
    columns = lambda rows: pl.BlockSpec((rows, step), lambda i: (0, i))
    tall = whole((length, width))
    return pl.pallas_call(
        functools.partial(backward_kernel, expert_count),
        grid=(width // step,),
        in_specs=[tall] * 5
        + [whole(router_t.shape), whole((width,)), whole((width,))]
        + [whole(cosine.shape)] * 2
        + [columns(length)] * 3
        + [columns(width)] * 3
        + [pl.BlockSpec((step, width), lambda i: (i, 0))]
        + [whole(parts.shape)],
        out_specs=[
            whole((2 * length, width)),
            whole((2 * length + 16 + router_t.shape[0], width)),
            tall,
        ],
        scratch_shapes=[
            pltpu.VMEM((length, width), BF),
            pltpu.VMEM((length, width), F32),
            pltpu.VMEM((length, width), F32),
        ],
        out_shape=[
            jax.ShapeDtypeStruct((2 * length, width), BF),
            jax.ShapeDtypeStruct((2 * length + 16 + router_t.shape[0], width), BF),
            jax.ShapeDtypeStruct((length, width), F32),
        ],
        compiler_params=pltpu.CompilerParams(vmem_limit_bytes=VMEM_LIMIT),
        cost_estimate=pl.CostEstimate(
            flops=int(COST * 8 * length * width * width), bytes_accessed=int(COST * 8 * width * width), transcendentals=0
        ),
        name="backward",
    )(
        x, dy, residual, ns, shared, router_t, gain1, gain2, cosine, sine,
        q, k, v, wq, wk, wv, wo, parts,
    )


def call(kernel, name, outs, *args, scalars=0):
    return pl.pallas_call(
        kernel,
        in_specs=[pl.BlockSpec(memory_space=pltpu.SMEM)] * scalars
        + [pl.BlockSpec(memory_space=pltpu.VMEM)] * (len(args) - scalars),
        out_specs=[pl.BlockSpec(memory_space=pltpu.VMEM)] * len(outs),
        out_shape=[jax.ShapeDtypeStruct(*o) for o in outs],
        compiler_params=pltpu.CompilerParams(vmem_limit_bytes=VMEM_LIMIT),
        cost_estimate=pl.CostEstimate(flops=1, bytes_accessed=1, transcendentals=0),
        name=name,
    )(*args)


def shared_kernel(ns_ref, dy_ref, gate_ref, up_ref, down_ref, cat_ref, result_ref, back_ref):
    ns, dy = ns_ref[...], dy_ref[...]
    width, ff = gate_ref.shape
    g = dot_nn(ns, gate_ref[...])
    u = dot_nn(ns, up_ref[...])
    sig = jax.nn.sigmoid(g)
    act = g * sig
    hid = (act * u).astype(BF)
    dh = dot_nt(dy, down_ref[...])
    dg = (dh * u * sig * (1.0 + g * (1.0 - sig))).astype(BF)
    du = (dh * act).astype(BF)
    result_ref[...] = dot_nn(hid, down_ref[...])
    back_ref[...] = dot_nt(dg, gate_ref[...]) + dot_nt(du, up_ref[...])
    for i, v in enumerate((dg, du, hid)):
        cat_ref[:, i * ff : (i + 1) * ff] = v
    cat_ref[:, 3 * ff : 3 * ff + width] = ns
    cat_ref[:, 3 * ff + width :] = dy


def shared_grads_kernel(ff, width, cat_ref, other_ref, order_d_ref, order_f_ref, su_send, su_keep, sd_send, sd_keep):
    pair = jnp.concatenate([cat_ref[...], other_ref[...]], 0)
    ns_t = dot_nt(order_d_ref[...], pair[:, 3 * ff : 3 * ff + width]).astype(BF)
    hid_t = dot_nt(order_f_ref[...], pair[:, 2 * ff : 3 * ff]).astype(BF)
    su = dot_nn(ns_t, pair[:, : 2 * ff]).astype(BF)
    sd = dot_nn(hid_t, pair[:, 3 * ff + width :]).astype(BF)
    for value, send, keep in ((su, su_send, su_keep), (sd, sd_send, sd_keep)):
        n = send.shape[1]
        for i in range(2):
            send[i] = value[i * n : (i + 1) * n]
            keep[i] = value[(2 + i) * n : (3 + i) * n]


def lefts_kernel(mine_ref, other_ref, order_a_ref, order_b_ref, a_ref, v_ref, o_ref):
    sets = lambda i, j: jnp.concatenate([mine_ref[i], other_ref[i], mine_ref[j], other_ref[j]], 0)
    a_ref[...] = dot_nt(order_a_ref[...], sets(0, 2)).astype(BF)
    v_ref[...] = dot_nt(order_b_ref[...], sets(0, 3)).astype(BF)
    o_ref[...] = dot_nt(order_b_ref[...], sets(1, 4)).astype(BF)


def last_grads_kernel(
    length, z_ref, mine_ref, other_ref, rest_ref, rest_other_ref, qx_ref, qxo_ref, by_ref, byo_ref, a_ref, v_ref, o_ref,
    ns_ref, ns_o_ref, ns_y_ref, ns_yo_ref, order_b_ref,
    a_send, a_keep, b_send, b_keep,
):
    width = mine_ref.shape[1]
    half = a_send.shape[0]
    join = lambda *v: jnp.concatenate(v, 0)

    def put(value, keep, send, columns):
        keep[:, columns] = value[:half].astype(BF)
        send[:, columns] = value[half:].astype(BF)

    for i in range(2):
        at = slice(i * length, (i + 1) * length)
        tokens = join(mine_ref[at], other_ref[at], qx_ref[at], qxo_ref[at])
        put(dot_nn(a_ref[...], tokens), a_keep, a_send, slice(i * width, (i + 1) * width))
        tokens = join(rest_ref[at], rest_other_ref[at], by_ref[at], byo_ref[at])
        left = (v_ref, o_ref)[i]
        put(dot_nn(left[...], tokens), b_keep, b_send, slice(i * width, (i + 1) * width))
    start = 2 * length
    refs = ((rest_ref, start), (rest_other_ref, start), (by_ref, start), (byo_ref, start))
    gains = sum(ref[i : i + 16].astype(F32) for ref, i in refs).astype(BF)
    logits = jnp.concatenate([ref[i + 16 :, :length] for ref, i in refs], 1)
    ns = join(
        ns_ref[...], ns_o_ref[0], ns_y_ref[0], ns_yo_ref[0]
    )
    left_r = dot_nt(order_b_ref[...], ns).astype(BF)
    small = jnp.concatenate(
        [dot_nt(left_r, logits), dot_nt(order_b_ref[...], gains)], 1
    )
    small = jnp.concatenate([small, jnp.zeros((2 * half, LANES - small.shape[1]), F32)], 1)
    put(small, b_keep, b_send, slice(2 * width, 2 * width + LANES))


def after(value, *earlier):
    return lax.optimization_barrier((value, earlier))[0]


def shards(
    tokens,
    cotangent,
    routes,
    expert_at,
    norm1_gain,
    w_query,
    w_key,
    w_value,
    w_out,
    norm2_gain,
    w_router,
    shared_gate,
    shared_up,
    shared_down,
    routed_gate,
    routed_up,
    routed_down,
):
    length, model_width = tokens.shape
    expert_count = w_router.shape[1]
    slot_dev = routed_gate.shape[0]
    n_ex = lax.axis_size("expert")
    n_dp = lax.axis_size("dp")
    capacity = (length * TOP * 5 // (4 * expert_count) + 7) // 8 * 8
    my_dp, my_ex = lax.axis_index("dp"), lax.axis_index("expert")
    n_z = n_ex // 2
    w = model_width
    rows = w // (n_dp * n_ex)
    over_core = lambda v: partner(v, "expert", 1)
    order_d = rows_for(w, (2, 3, 0, 1))
    order_a, order_b = rows_for(w, (0, 2)), rows_for(w, (0, 1))

    routes_t = jnp.pad(routes.T.astype(BF), ((0, 16 - TOP), (0, 0)), constant_values=-1)
    routes_t = jnp.pad(routes_t, ((0, 0), (0, w - length)))
    spread = lambda v: exchange_z(jnp.broadcast_to(v[None], (n_z,) + v.shape))
    early = spread(jnp.concatenate([cotangent, routes_t], 0))
    cosine, sine = (jnp.asarray(t) for t in rotary(length))
    gain1, gain2 = norm1_gain, norm2_gain
    queries, key_rows, value_rows, attended, normed_first, residual, normed_second = attention(
        tokens, gain1, gain2, cosine, sine, w_query, w_key, w_value, w_out
    )
    ff = shared_gate.shape[1]
    from_shared, shared_result, shared_back = call(
        shared_kernel, "shared",
        [((length, 3 * ff + 2 * w), BF), ((length, w), F32), ((length, w), F32)],
        normed_second, cotangent, shared_gate, shared_up, shared_down,
    )
    my_z = my_ex // 2
    first_x = partner(normed_first, "dp", 1)
    first_y = partner(jnp.stack([normed_first, attended]), "dp", 2)
    selectors = [(keep_rows(w, q), keep_rows(ff, q)) for q in (2, 1)]
    order_f = rows_for(ff, (1, 3, 0, 2))
    ns = spread(
        after(normed_second, early, from_shared, first_x, first_y, selectors, order_a, order_b, order_d, order_f)
    )
    from_other = over_core(from_shared)
    part_d, part_f = w // (2 * n_dp), ff // (2 * n_dp)
    su_send, su_keep, sd_send, sd_keep = call(
        functools.partial(shared_grads_kernel, ff, w), "shared_grads",
        [((2, part_d, 2 * ff), BF)] * 2 + [((2, part_f, w), BF)] * 2,
        from_shared, from_other, order_d, order_f,
    )
    early_other = over_core(early)
    early_x, early_y = partner(early, "dp", 1), partner(early, "dp", 2)

    my_expert = lax.dynamic_slice_in_dim(expert_at, my_ex * slot_dev, slot_dev)
    router_wide = jnp.pad(w_router, ((0, 0), (0, LANES - expert_count)))
    pick, dh_raw, dy_rows = prepare(my_expert, (early, early_other), routed_down, capacity)
    ns = after(ns, pick, dh_raw, early_x, early_y, su_send)
    ns_other = over_core(ns)
    back_mine, back_other, hid, dg, du, x_rows, row_gate = experts(
        my_expert, (ns, ns_other), pick, dh_raw, routed_gate, routed_up, router_wide, expert_count
    )
    back_sum = plus(back_mine, over_core(back_other))
    back = exchange_z(back_sum)
    ns_far, su_send, sd_send, early_x, early_y = after((ns, su_send, sd_send, early_x, early_y), back_sum)
    early_x_other, early_y_other = over_core(early_x), over_core(early_y)
    su_got, sd_got = partner(su_send, "dp", 2), partner(sd_send, "dp", 1)
    su, sd = plus(su_keep, su_got), plus(sd_keep, sd_got)
    su_sum, sd_sum = su, sd
    su_last, sd_last = partner(su[1], "dp", 1), partner(sd[1], "dp", 2)
    su, sd = plus(su[0], su_last), plus(sd[0], sd_last)

    lefts = jnp.concatenate([normed_first[None], attended[None], first_x[None], first_y])
    lefts = after(lefts, back_sum)
    lefts_other = over_core(lefts)
    left_shape = ((w // 4, 4 * length), BF)
    left_a, left_v, left_o = call(
        lefts_kernel, "lefts", [left_shape] * 3, lefts, lefts_other, order_a, order_b,
    )
    ns_y = partner(after(ns_far, su_got, left_a), "dp", 2)
    combined_mine, combined_other = combine(after(hid, early_x_other, early_y_other), row_gate, pick, routed_down)
    ns_x = partner(after(ns_far, combined_mine), "dp", 1)
    combined = plus(combined_mine, over_core(combined_other))
    back = after(back, combined, left_a, su_sum, sd_sum)
    combined = exchange_z(after(combined, back))

    high = -(-expert_count // 16) * 16
    router_t = jnp.pad(w_router.T, ((0, high - expert_count), (0, 0)))
    d_qk, d_rest, grad_inputs = backward(
        tokens, cotangent, residual, normed_second, shared_back, router_t, gain1, gain2, cosine, sine,
        queries, key_rows, value_rows, w_query, w_key, w_value, w_out, back, expert_count,
    )

    qk_x, b_y = partner(d_qk, "dp", 1), partner(d_rest, "dp", 2)
    far_x = [ns_x, over_core(after(ns_x, d_qk)), early_x, early_x_other]

    far = [far_x]

    def slot_grads(slot, last_dg):
        return routed_grads(
            slot, selectors[slot % 2], my_expert, [x_rows, last_dg, du, hid, row_gate, dy_rows],
            far[slot % 2], [routed_gate, routed_up, routed_down], router_wide, expert_count,
        )

    routed = [slot_grads(0, after(dg, d_qk, ns_y))]
    d_qk, d_rest, qk_x, b_y = after((d_qk, d_rest, qk_x, b_y), routed[0], su_last, sd_last)
    qk_other, rest_other = over_core(d_qk), over_core(d_rest)
    far_y = [ns_y, over_core(after(ns_y, routed[0])), early_y, early_y_other]
    far.append(far_y)
    qk_x_other, b_y_other = over_core(qk_x), over_core(b_y)
    blocks = [d_qk, qk_other, d_rest, rest_other, qk_x, qk_x_other, b_y, b_y_other, left_a, left_v, left_o, normed_second]
    out_a, out_b = (w // 8, 2 * w), (w // 8, 2 * w + LANES)
    a_send, a_keep, b_send, b_keep = pl.pallas_call(
        functools.partial(last_grads_kernel, length),
        grid_spec=pltpu.PrefetchScalarGridSpec(
            num_scalar_prefetch=1,
            grid=(1,),
            in_specs=[once(v.shape) for v in blocks]
            + [pl.BlockSpec((1, length, w), lambda i, z: (z[0], 0, 0), pipeline_mode=pl.Buffered(1))] * 3
            + [once(order_b.shape)],
            out_specs=[once(shape) for shape in (out_a, out_a, out_b, out_b)],
        ),
        out_shape=[jax.ShapeDtypeStruct(shape, BF) for shape in (out_a, out_a, out_b, out_b)],
        compiler_params=pltpu.CompilerParams(vmem_limit_bytes=VMEM_LIMIT),
        cost_estimate=pl.CostEstimate(flops=1, bytes_accessed=1, transcendentals=0),
        name="last_grads",
    )(my_z[None], *blocks, ns_other, far_y[0], far_y[1], order_b)
    a_got, b_got = partner(a_send, "dp", 2), partner(b_send, "dp", 1)

    routed += [slot_grads(slot, after(dg, a_send)) for slot in range(1, slot_dev)]
    pieces = [
        (keep, partner(after(send, a_send), "dp", 2 if slot % 2 == 0 else 1))
        for slot, (send, keep) in enumerate(routed)
    ]
    a_got = after(a_got, routed)
    last = jnp.concatenate([plus(a_keep, a_got), plus(b_keep, b_got)], -1).reshape(n_z, rows, -1)

    sd = jnp.pad(sd.reshape(n_z, -1, w), ((0, 0), (0, (w - ff) // (n_dp * n_ex)), (0, 0)))
    grad_shared = exchange_z(after(jnp.concatenate([su.reshape(n_z, rows, -1), sd], -1), combined))
    last = exchange_z(after(last, grad_shared))
    grad_shared, combined = after((grad_shared, combined), last)
    last, grad_shared = total(list(last)), total(list(grad_shared))
    output = (residual + shared_result + total(list(combined))).astype(BF)
    grad_rgate, grad_rup, grad_rdown = finish(pieces, [(w // n_dp, ff), (w // n_dp, ff), (ff // n_dp, w)])
    return (
        output,
        grad_inputs,
        last[:, 4 * w + high],
        last[:, :w],
        last[:, w : 2 * w],
        last[:, 2 * w : 3 * w],
        last[:, 3 * w : 4 * w],
        last[:, 4 * w + high + 1],
        last[:, 4 * w : 4 * w + expert_count],
        grad_shared[:, :ff],
        grad_shared[:, ff : 2 * ff],
        grad_shared[: ff // (n_dp * n_ex), 2 * ff :],
        grad_rgate,
        grad_rup,
        grad_rdown,
    )


def solution(mesh):
    placed = (
        P(("dp", "expert"), None),
        P(("dp", "expert"), None),
        P(("dp", "expert"), None),
        P(),
        P(),
        P(),
        P(),
        P(),
        P(),
        P(),
        P(),
        P(),
        P(),
        P(),
        P("expert", None, None),
        P("expert", None, None),
        P("expert", None, None),
    )
    return jax.shard_map(
        shards,
        mesh=mesh,
        in_specs=placed,
        out_specs=(
            P(("dp", "expert"), None),
            P(("dp", "expert"), None),
            P(("dp", "expert")),
            P(("dp", "expert"), None),
            P(("dp", "expert"), None),
            P(("dp", "expert"), None),
            P(("dp", "expert"), None),
            P(("dp", "expert")),
            P(("dp", "expert"), None),
            P(("dp", "expert"), None),
            P(("dp", "expert"), None),
            P(("dp", "expert"), None),
            P("expert", "dp", None),
            P("expert", "dp", None),
            P("expert", "dp", None),
        ),
        check_vma=False,
    )
```
